32 devices in a mesh: dp: 8 (over z, y), section: 4 (over x, core).
Axes of the slice: x: 2, y: 2, z: 4, core: 2. Of those that a mesh axis runs over, the one named last changes fastest.
Arguments:
- tokens: bfloat16 [16, 1024, 768], P('dp', 'section'), may hold values from -6 to 6
- seg_counts: int32 [16, 8], P('dp'), may hold values from 0 to 128, as said below
- w_in: bfloat16 [4, 768, 3072], P('section'), may hold values from -2 to 2
- w_down: bfloat16 [6144, 768], P('section'), may hold values from -0.109375 to 0.109375
- ln_gain: bfloat16 [4, 768], P('section'), may hold values from 0.5 to 1.5
- ln_bias: bfloat16 [4, 768], P('section'), may hold values from -1 to 1
- pos_table: bfloat16 [8, 768], P(None, 'section'), may hold values from -3 to 3
- cotangent: bfloat16 [16, 1024, 768], P('dp', 'section'), may hold values from -24 to 24
Outputs:
- mixed: bfloat16 [16, 1024, 768], P('dp', 'section')
- grad_tokens: float32 [16, 1024, 768], P('dp', 'section')
- grad_w_in: float32 [4, 768, 3072], P('section')
- grad_w_down: float32 [6144, 768], P('section')
- grad_gain: float32 [4, 768], P('section')
- grad_bias: float32 [4, 768], P('section')
- grad_pos: float32 [8, 768], P(None, 'section')
The draws below stay inside these ranges and needn't reach their ends.
Inputs may be any that keep to these rules, and one draw needn't show every extreme that they name: `seg_counts`: segment j of a document holds min(128, max(0, length - j * 128)) tokens for the document's length, which is 128 or more; of the 2 documents of one dp index, one has all 1024 tokens and another at most (7) * 128.
All inputs are finite; a program needn't handle non-finite values.
Results may differ from the reference program's by a relative error of at most 0.02.
Values may be sent and summed in bfloat16 or wider, within the bound.
A program may use at most 192 MiB of HBM per device.

```python
import math
import jax
import jax.numpy as jnp
from jax import lax

D = 768
H = 12
FF = 3072
SEG = 128
SEGS = 8
MB = 2
DOCS = 16
N_SECTION = 4


def draw_seg_counts(key, part):
    key = jax.random.fold_in(key, 5)
    groups = DOCS // MB
    full_key, other_key, length_key, short_key = jax.random.split(key, 4)
    chosen = jax.random.randint(full_key, (groups,), 0, MB)
    other_doc = (chosen + jax.random.randint(other_key, (groups,), 1, MB)) % MB
    lengths = jax.random.randint(length_key, (groups, MB), SEG, SEGS * SEG + 1)
    short_length = jax.random.randint(short_key, (groups,), SEG, (SEGS - 1) * SEG + 1)
    column = jnp.arange(MB, dtype=jnp.int32)[None, :]
    lengths = jnp.where(column == chosen[:, None], SEGS * SEG, lengths)
    lengths = jnp.where(column == other_doc[:, None], short_length[:, None], lengths)
    lengths = lengths.reshape(DOCS)
    segment_start = jnp.arange(SEGS, dtype=jnp.int32)[None, :] * SEG
    return jnp.clip(lengths[:, None] - segment_start, 0, SEG).astype(jnp.int32)


def draw_w_in(key, part):
    key = jax.random.fold_in(key, 9)
    base_draw = jnp.clip(jax.random.normal(key, (4, D, FF), jnp.float32), -5.0, 5.0)
    section_ids = jnp.arange(4, dtype=jnp.int32)[:, None, None]
    column_ids = jnp.arange(FF, dtype=jnp.int32)[None, None, :]
    widened = jnp.where(section_ids == 0, 0.6 * math.sqrt(SEG), 0.6 * math.sqrt(SEGS))
    factor_grid = jnp.where((column_ids >= 3 * D) & (section_ids % 2 == 0), widened, 1.0)
    return (base_draw * factor_grid / math.sqrt(D)).astype(jnp.bfloat16)


def draw_cotangent(key, part):
    key = jax.random.fold_in(key, 13)
    base_draw = jnp.clip(jax.random.normal(key, (DOCS, SEGS * SEG, D), jnp.float32), -6.0, 6.0)
    place = jnp.arange(SEGS * SEG, dtype=jnp.int32)[None, :, None]
    factor_grid = jnp.where(place % SEG == 0, 4.0, 1.0)
    return (base_draw * factor_grid).astype(jnp.bfloat16)


def block_levels(stream_key, shape, cuts, least, high):
    factor_of, own = 1.0, jax.random.fold_in(stream_key, 6)
    for dim, blocks in cuts:
        heights = jnp.exp(jax.random.uniform(jax.random.fold_in(own, dim), (blocks,), jnp.float32, least / len(cuts), high / len(cuts)))
        factor_of = factor_of * jnp.repeat(heights, shape[dim] // blocks).reshape([-1 if axis == dim else 1 for axis in range(len(shape))])
    return factor_of


def centred(stream_key, shape, scale, reach, cuts=(), held_as=jnp.bfloat16):
    result = jax.random.normal(stream_key, shape, jnp.float32) * scale
    if len(cuts) > 0:
        result = block_levels(stream_key, shape, cuts, -0.22, 0.18) * result
    return jnp.clip(result, min=-reach, max=reach).astype(held_as)


def setup_inputs(seed: int = 0) -> dict:
    key_of = jax.random.split(jax.random.key(seed), 9)
    tokens = centred(key_of[0], (DOCS, SEGS * SEG, D), 1.0, 6.0, ((0, 8), (1, 4)))
    seg_counts = draw_seg_counts(jax.random.fold_in(key_of[8], 71), 0)
    w_in = draw_w_in(jax.random.fold_in(key_of[8], 71), 0)
    w_down = centred(key_of[3], (2 * FF, D), FF ** -0.5, 0.109375, ((0, 4),))
    ln_gain = jnp.clip(1.0 + 0.1 * jax.random.normal(key_of[4], (N_SECTION, D), jnp.float32), 0.5, 1.5).astype(jnp.bfloat16)
    ln_bias = centred(key_of[5], (N_SECTION, D), 0.2, 1.0, ((0, 4),))
    pos_table = centred(key_of[6], (SEGS, D), 0.5, 3.0, ((1, 4),))
    cotangent = draw_cotangent(jax.random.fold_in(key_of[8], 71), 0)
    return dict(tokens=tokens, seg_counts=seg_counts, w_in=w_in, w_down=w_down, ln_gain=ln_gain, ln_bias=ln_bias, pos_table=pos_table, cotangent=cotangent)


@jax.custom_vjp
def low(v):
    return lax.optimization_barrier(v.astype(jnp.bfloat16)).astype(jnp.float32)

@jax.custom_vjp
def low_back(v):
    return v

def low_keep(v):
    return (low(v), None)

def low_pass(kept, grad):
    return (grad,)

def back_keep(v):
    return (v, None)

def back_low(kept, grad):
    return (low(grad),)
low.defvjp(low_keep, low_pass)
low_back.defvjp(back_keep, back_low)
epsilon = 1e-05
masked_score = -1e+30
highest = lax.Precision.HIGHEST

def round_both(value):
    return low(low_back(value))

def layer_norm(residual, gain_vector, bias_vector):
    mean_value = lax.optimization_barrier(jnp.mean(residual, axis=-1, keepdims=True))
    center = residual - mean_value
    variance = lax.optimization_barrier(jnp.mean(center * center, axis=-1, keepdims=True))
    return center * lax.rsqrt(variance + epsilon) * gain_vector + bias_vector

def attend(rows, weight, visible):
    block_count, row_count, model_width = rows.shape
    head_size = model_width // H
    qkv = round_both(jnp.einsum('nsd,de->nse', rows, weight[:, :3 * model_width], precision=highest))
    queries = qkv[..., :model_width].reshape(block_count, row_count, H, head_size)
    key_rows = qkv[..., model_width:2 * model_width].reshape(block_count, row_count, H, head_size)
    values = qkv[..., 2 * model_width:].reshape(block_count, row_count, H, head_size)
    scores = low_back(jnp.einsum('nqhd,nkhd->nhqk', queries, key_rows, precision=highest) * head_size ** (-0.5))
    scores = jnp.where(visible[:, None, None, :], scores, masked_score)
    probability = jax.nn.softmax(scores, axis=-1)
    context = jnp.einsum('nhqk,nkhd->nqhd', low(probability), values, precision=highest)
    context = round_both(context.reshape(block_count, row_count, model_width))
    return low_back(jnp.einsum('nsc,rc->nsr', context, weight[:, 3 * model_width:], precision=highest))

def feed_forward(rows, weight, down):
    pre_act = low_back(jnp.dot(rows, weight, precision=highest))
    hidden = low(jax.nn.gelu(pre_act, approximate=False))
    return low_back(jnp.dot(hidden, down, precision=highest))

def document(params, doc_rows, doc_counts):
    w_in, w_down, ln_gain, ln_bias, pos_table = params
    blocks = doc_rows.reshape(SEGS, SEG, D)
    position = jnp.arange(SEG, dtype=jnp.int32)[None, :]
    visible = position < jnp.maximum(doc_counts, 1)[:, None]
    first = round_both(layer_norm(blocks + attend(blocks, w_in[0], visible), ln_gain[0], ln_bias[0]))
    second = round_both(layer_norm(first + feed_forward(first, w_in[1], w_down[:FF]), ln_gain[1], ln_bias[1]))
    summary = round_both(second[:, 0, :] + pos_table)
    seg_live = (doc_counts > 0)[None]
    third = round_both(layer_norm(summary + attend(summary[None], w_in[2], seg_live)[0], ln_gain[2], ln_bias[2]))
    fourth = layer_norm(third + feed_forward(third, w_in[3], w_down[FF:]), ln_gain[3], ln_bias[3])
    joined = jnp.concatenate([fourth[:, None, :], second[:, 1:, :]], axis=1)
    live_rows = position < doc_counts[:, None]
    return jnp.where(live_rows[:, :, None], joined, 0.0).reshape(SEGS * SEG, D)

def reference(tokens, seg_counts, w_in, w_down, ln_gain, ln_bias, pos_table, cotangent):
    params = (w_in.astype(jnp.float32), w_down.astype(jnp.float32), ln_gain.astype(jnp.float32), ln_bias.astype(jnp.float32), pos_table.astype(jnp.float32))

    def doc_step(totals, doc_entry):
        doc_rows, doc_counts, doc_cotangent = doc_entry

        def forward(weights, rows):
            return document(weights, rows, doc_counts)
        doc_out, pull_back = jax.vjp(forward, params, doc_rows)
        weight_grads, row_grads = pull_back(doc_cotangent)
        totals = jax.tree.map(jnp.add, totals, weight_grads)
        return (totals, (doc_out.astype(jnp.bfloat16), row_grads))
    zero_totals = jax.tree.map(jnp.zeros_like, params)
    totals, outputs = lax.scan(doc_step, zero_totals, (tokens.astype(jnp.float32), seg_counts, cotangent.astype(jnp.float32)))
    return (outputs[0], outputs[1], totals[0], totals[1], totals[2], totals[3], totals[4])
```

```python
import functools

import jax
import jax.numpy as jnp
from jax import lax
from jax.experimental import pallas as pl
from jax.experimental.pallas import tpu as pltpu
from jax.sharding import PartitionSpec as P

bf16 = jnp.bfloat16
f32 = jnp.float32
D = 768
FF = 3072
ROWS = 1024
CH = 512
MESH = pl.DeviceIdType.MESH


class Refs:
    pass


def nn(a, b):
    return lax.dot_general(a, b, (((1,), (0,)), ((), ())), preferred_element_type=f32)


def nt(a, b):
    return lax.dot_general(a, b, (((1,), (1,)), ((), ())), preferred_element_type=f32)


def tn(a, b):
    return lax.dot_general(a, b, (((0,), (0,)), ((), ())), preferred_element_type=f32)


def cut(start, size):
    return pl.ds(pl.multiple_of(start, size), size)


def loop(n, body):
    def step(i, carry):
        body(i)
        return carry

    lax.fori_loop(0, n, step, 0)


def norm_stats(r):
    mean = jnp.mean(r, axis=-1, keepdims=True)
    cen = r - mean
    var = jnp.mean(cen * cen, axis=-1, keepdims=True)
    rstd = lax.rsqrt(var + 1e-5)
    return cen * rstd, rstd


def norm_back(dy, xhat, rstd, gain):
    dx = dy * gain
    m1 = jnp.mean(dx, axis=-1, keepdims=True)
    m2 = jnp.mean(dx * xhat, axis=-1, keepdims=True)
    return rstd * (dx - m1 - xhat * m2)


def gelu_parts(u):
    ax = jnp.abs(u)
    e = jnp.exp(u * u * -0.5)
    t = 1.0 / (1.0 + (0.3275911 * 0.7071067811865476) * ax)
    h = 0.7107068705 + t * (-0.7265760135 + t * 0.5307027145)
    h = t * (0.127414796 + t * (-0.142248368 + t * h)) * e
    phi = jnp.where(u >= 0, 1.0 - h, h)
    return u * phi, phi + u * (0.3989422804014327 * e)


def stacked(v):
    low = lax.broadcasted_iota(jnp.int32, v.shape, 1) < 64
    z = jnp.zeros_like(v)
    return jnp.concatenate([jnp.where(low, v, z), jnp.where(low, z, v)], axis=0)


def beside(v):
    low = lax.broadcasted_iota(jnp.int32, (128, 128), 1) < 64
    return jnp.where(low, v[:128], v[128:])


def attn_block(R, i, vis):
    rs = cut(i * 128, 128)
    for j in range(6):
        q2 = R.qkv[rs, 128 * j : 128 * j + 128]
        k2 = R.qkv[rs, 768 + 128 * j : 768 + 128 * j + 128]
        v2 = R.qkv[rs, 1536 + 128 * j : 1536 + 128 * j + 128]
        s = jnp.where(vis, nt(stacked(q2), k2) * 0.125, -1e30)
        s = jnp.exp(s - jnp.max(s, axis=-1, keepdims=True))
        pr = (s / jnp.sum(s, axis=-1, keepdims=True)).astype(bf16)
        R.p[cut(i * 1536 + 256 * j, 256), :] = pr
        R.ctx[rs, 128 * j : 128 * j + 128] = beside(nn(pr, v2)).astype(bf16)


def attn_block_back(R, i):
    rs = cut(i * 128, 128)
    for j in range(6):
        sq, sk, sv = [slice(b + 128 * j, b + 128 * j + 128) for b in (0, 768, 1536)]
        q2 = R.qkv[rs, sq]
        k2 = R.qkv[rs, sk]
        v2 = R.qkv[rs, sv]
        qs = stacked(q2)
        dos = stacked(R.xh1[rs, sq])
        pr = R.p[cut(i * 1536 + 256 * j, 256), :]
        pf = pr.astype(f32)
        dp = nt(dos, v2)
        ds = (pf * (dp - jnp.sum(dp * pf, axis=-1, keepdims=True))).astype(bf16)
        R.qkv[rs, sv] = tn(pr, dos).astype(bf16)
        R.qkv[rs, sq] = beside(nn(ds, k2) * 0.125).astype(bf16)
        R.qkv[rs, sk] = (tn(ds, qs) * 0.125).astype(bf16)


def qkv_half(R, r0):
    def body(n):
        cs = cut(n * 256, 256)
        R.qkv[pl.ds(r0, 512), cs] = nn(R.x[pl.ds(r0, 512), :], R.wall[0, :, cs]).astype(bf16)

    loop(9, body)


def attn_half(R, h):
    key = lax.broadcasted_iota(jnp.int32, (256, 128), 1)

    def seg(k):
        i = h * 4 + k
        attn_block(R, i, key < jnp.maximum(R.count_of(i), 1))

    loop(4, seg)


def attn_out(R, h):
    def body(k):
        rs = cut(h * 512 + k * 128, 128)
        att = nt(R.ctx[rs, :], R.wall[0, :, 2304:])
        xh, rstd = norm_stats(R.x[rs, :].astype(f32) + att)
        R.xh0[rs, :] = xh.astype(bf16)
        R.rs0[rs, :] = rstd
        R.a0[rs, :] = (xh * R.gains[0, 0:1, :] + R.gains[0, 1:2, :]).astype(bf16)

    loop(4, body)


def ffn_half(R, h):
    r0 = h * 512

    def up(n):
        cs = cut(n * 256, 256)
        mm, gg = gelu_parts(nn(R.a0[pl.ds(r0, 512), :], R.wall[1, :, cs]))
        R.m[pl.ds(r0, 512), cs] = mm.astype(bf16)
        R.gp[pl.ds(r0, 512), cs] = gg.astype(bf16)

    loop(12, up)

    def down(k):
        rs = cut(r0 + k * 256, 256)
        xh, rstd = norm_stats(R.a0[rs, :].astype(f32) + nn(R.m[rs, :], R.v0[...]))
        R.xh1[rs, :] = xh.astype(bf16)
        R.rs1[rs, :] = rstd
        R.a1[rs, :] = (xh * R.gains[1, 0:1, :] + R.gains[1, 1:2, :]).astype(bf16)

    loop(2, down)


def pad16(v):
    return jnp.concatenate([v, jnp.zeros_like(v)], axis=0).astype(bf16)


def first_ffn(R):
    rows = [R.a0[i * 128 : i * 128 + 16, :].astype(f32)[0:1, :] for i in range(8)]
    af = jnp.concatenate(rows, axis=0)
    a16 = pad16(af)

    def up(n):
        cs = cut(n * 256, 256)
        mm, gg = gelu_parts(nn(a16, R.wall[1, :, cs]))
        R.fm[:, cs] = mm.astype(bf16)
        R.fg[:, cs] = gg

    loop(12, up)
    xh, rstd = norm_stats(af + nn(R.fm[...], R.v0[...])[0:8])
    R.fxh[...] = xh
    R.frs[...] = rstd
    return (xh * R.gains[1, 0:1, :] + R.gains[1, 1:2, :]).astype(bf16).astype(f32)


def ln1_back(R):
    row = lax.broadcasted_iota(jnp.int32, (128, 1), 0)

    def body(i):
        rs = cut(i * 128, 128)
        live = (row < R.count_of(i)) & (row > 0)
        dy = jnp.where(live, R.cot[rs, :].astype(f32), 0.0)
        xh = R.xh1[rs, :].astype(f32)
        R.gsum[2:3, :] += jnp.sum(dy * xh, axis=0, keepdims=True)
        R.gsum[3:4, :] += jnp.sum(dy, axis=0, keepdims=True)
        dr = norm_back(dy, xh, R.rs1[rs, :], R.gains[1, 0:1, :])
        R.da0[rs, :] = dr
        R.cot[rs, :] = dr.astype(bf16)

    loop(8, body)


def row_pass(R):
    def hid(n):
        cs = cut(n * 256, 256)

        def part(k):
            rs = cut(k * 512, 512)
            dm = nt(R.cot[rs, :], R.v0[cs, :])
            R.gp[rs, cs] = (dm * R.gp[rs, cs].astype(f32)).astype(bf16)

        loop(2, part)

    loop(12, hid)

    def back(k):
        rs = cut(k * 256, 256)
        R.da0[rs, :] += nt(R.gp[rs, :], R.wall[1])

    loop(4, back)


def put_first(ref, i, rowval):
    rs = slice(i * 128, i * 128 + 16)
    blk = ref[rs, :]
    it = lax.broadcasted_iota(jnp.int32, blk.shape, 0)
    ref[rs, :] = jnp.where(it == 0, rowval.astype(f32), blk.astype(f32)).astype(blk.dtype)


def first_back(R, dc):
    xh = R.fxh[...]
    R.gsum[2:3, :] += jnp.sum(dc * xh, axis=0, keepdims=True)
    R.gsum[3:4, :] += jnp.sum(dc, axis=0, keepdims=True)
    dr = norm_back(dc, xh, R.frs[...], R.gains[1, 0:1, :])
    dz = pad16(dr)

    def hid(n):
        cs = cut(n * 256, 256)
        R.fdu[:, cs] = (nt(dz, R.v0[cs, :]) * R.fg[:, cs]).astype(bf16)

    loop(12, hid)
    da = dr + nt(R.fdu[...], R.wall[1])[0:8]
    for i in range(8):
        put_first(R.cot, i, dr[i : i + 1, :].astype(bf16))
        put_first(R.gp, i, R.fdu[...].astype(f32)[i : i + 1, :])
        put_first(R.da0, i, da[i : i + 1, :])


def transposes1(R):
    for b, ref in ((0, R.a0), (1536, R.cot)):

        def body(k, b=b, ref=ref):
            R.v0[b : b + 768, cut(k * 256, 256)] = ref[cut(k * 256, 256), :].T

        loop(3, body)
        R.v0[b + 768 : b + 1536, 0:256] = ref[768:1024, :].T


def tdot(R, b, rhs, cs):
    head = nn(R.v0[b : b + 768, :], rhs[0:768, cs])
    return head + nn(R.v0[b + 768 : b + 1536, 0:256], rhs[768:1024, cs])


def dvt_block(R, n):
    cs = cut(n * 256, 256)
    R.m[0:768, cs] = tdot(R, 1536, R.m, cs).astype(bf16)


def dw1_block(R, n):
    cs = cut(n * 256, 256)
    R.wall[1, :, cs] = tdot(R, 0, R.gp, cs).astype(bf16)


def ln0_back(R):
    def body(i):
        rs = cut(i * 128, 128)
        dy = R.da0[rs, :].astype(bf16).astype(f32)
        xh = R.xh0[rs, :].astype(f32)
        R.gsum[0:1, :] += jnp.sum(dy * xh, axis=0, keepdims=True)
        R.gsum[1:2, :] += jnp.sum(dy, axis=0, keepdims=True)
        dr = norm_back(dy, xh, R.rs0[rs, :], R.gains[0, 0:1, :])
        R.da0[rs, :] = dr
        R.a1[rs, :] = dr.astype(bf16)

    loop(8, body)


def dctx_pass(R):
    def body(k):
        rs = cut(k * 256, 256)
        R.xh1[rs, :] = nn(R.a1[rs, :], R.wall[0, :, 2304:]).astype(bf16)

    loop(4, body)


def transposes2(R):
    for c0, ref in ((0, R.x), (1024, R.a1)):

        def body(k, c0=c0, ref=ref):
            R.gp[0:768, cut(c0 + k * 256, 256)] = ref[cut(k * 256, 256), :].T

        loop(4, body)


def dx_pass(R):
    def body(k):
        rs = cut(k * 256, 256)
        R.cot[rs, :] = (R.da0[rs, :] + nt(R.qkv[rs, :], R.wall[0, :, :2304])).astype(bf16)

    loop(4, body)


def dw0_block(R, n):
    cs = pl.ds(n * 256, 256)
    if n < 9:
        R.wall[0, :, cs] = nn(R.gp[0:768, 0:1024], R.qkv[:, cs]).astype(bf16)
    else:
        c2 = pl.ds(n * 256 - 2304, 256)
        R.wall[0, :, cs] = nn(R.gp[0:768, 1024:2048], R.ctx[:, c2]).astype(bf16)


def cross_attn(R, pos_rows):
    g = R.gath[...].reshape(128, 896)
    cp = (g[:, :768] + jnp.concatenate([pos_rows] * 8, axis=0)).astype(bf16)
    R.x[0:128, :] = cp
    live = g[:, 768:896].T
    row = lax.broadcasted_iota(jnp.int32, (128, 128), 0)
    col = lax.broadcasted_iota(jnp.int32, (128, 128), 1)
    same = (row & 0x72) == (col & 0x72)
    vis = same & (live > 0.5)
    R.cmask[...] = jnp.where(vis, 1.0, 0.0)

    def qkv(n):
        cs = cut(n * 256, 256)
        R.qkv[0:128, cs] = nn(R.x[0:128, :], R.wall[1, :, cs]).astype(bf16)

    loop(9, qkv)
    mask = R.cmask[...] > 0.5
    attn_block(R, 0, jnp.concatenate([mask, mask], axis=0))
    att = nt(R.ctx[0:128, :], R.wall[1, :, 2304:])
    xh, rstd = norm_stats(R.x[0:128, :].astype(f32) + att)
    R.da0[0:128, :] = xh
    R.rs0[0:128, :] = rstd
    R.a0[0:128, :] = (xh * R.gains[0, 0:1, :] + R.gains[0, 1:2, :]).astype(bf16)


def cross_attn_back(R):
    dy = R.cot[0:128, :].astype(f32)
    xh = R.da0[0:128, :]
    R.gsum[0:1, :] = jnp.sum(dy * xh, axis=0, keepdims=True)
    R.gsum[1:2, :] = jnp.sum(dy, axis=0, keepdims=True)
    dr = norm_back(dy, xh, R.rs0[0:128, :], R.gains[0, 0:1, :])
    R.da0[0:128, :] = dr
    R.a1[0:128, :] = dr.astype(bf16)
    R.xh1[0:128, :] = nn(R.a1[0:128, :], R.wall[1, :, 2304:]).astype(bf16)
    attn_block_back(R, 0)
    dcp = R.da0[0:128, :] + nt(R.qkv[0:128, :], R.wall[1, :, :2304])
    R.da0[128:256, :] = dcp.astype(bf16).astype(f32)


def cross_attn_weights(R):
    R.gp[128:896, 0:128] = R.x[0:128, :].T
    R.gp[128:896, 128:256] = R.a1[0:128, :].T

    def one(n):
        cs = cut(n * 256, 256)
        R.wall[1, :, cs] = nn(R.gp[128:896, 0:128], R.qkv[0:128, cs]).astype(bf16)

    loop(9, one)

    def two(n):
        c2 = cut(n * 256, 256)
        cs = cut(2304 + n * 256, 256)
        R.wall[1, :, cs] = nn(R.gp[128:896, 128:256], R.ctx[0:128, c2]).astype(bf16)

    loop(3, two)


def cross_ffn(R):
    def up(n):
        cs = cut(n * 256, 256)
        mm, gg = gelu_parts(nn(R.a0[0:128, :], R.wall[0, :, cs]))
        R.gp[896:1024, cs] = mm.astype(bf16)
        R.gp[0:128, cs] = gg.astype(bf16)

    loop(12, up)
    xh, rstd = norm_stats(R.a0[0:128, :].astype(f32) + nn(R.gp[896:1024, :], R.v0[...]))
    R.da0[0:128, :] = xh
    R.rs0[0:128, :] = rstd
    R.da0[128:256, :] = xh * R.gains[0, 0:1, :] + R.gains[0, 1:2, :]


def cross_ffn_back(R):
    dy = R.gath[...].reshape(128, 896)[:, :768]
    xh = R.da0[0:128, :]
    R.gsum[0:1, :] = jnp.sum(dy * xh, axis=0, keepdims=True)
    R.gsum[1:2, :] = jnp.sum(dy, axis=0, keepdims=True)
    dr = norm_back(dy, xh, R.rs0[0:128, :], R.gains[0, 0:1, :])
    R.da0[0:128, :] = dr
    R.cot[0:128, :] = dr.astype(bf16)

    def hid(n):
        cs = cut(n * 256, 256)
        dm = nt(R.cot[0:128, :], R.v0[cs, :])
        R.gp[0:128, cs] = (dm * R.gp[0:128, cs].astype(f32)).astype(bf16)

    loop(12, hid)
    R.a1[0:128, :] = (R.da0[0:128, :] + nt(R.gp[0:128, :], R.wall[0])).astype(bf16)


def cross_ffn_weights(R):
    R.qkv[0:768, 0:128] = R.a0[0:128, :].T
    R.qkv[0:768, 128:256] = R.cot[0:128, :].T

    def body(n):
        cs = cut(n * 256, 256)
        R.wall[0, :, cs] = nn(R.qkv[0:768, 0:128], R.gp[0:128, cs]).astype(bf16)
        R.gp[128:896, cs] = nn(R.qkv[0:768, 128:256], R.gp[896:1024, cs]).astype(bf16)

    loop(12, body)


SCRATCH = dict(
    wall=((2, D, FF), bf16),
    v0=((FF, D), bf16),
    x=((ROWS, D), bf16),
    qkv=((ROWS, 2304), bf16),
    p=((12288, 128), bf16),
    ctx=((ROWS, D), bf16),
    xh0=((ROWS, D), bf16),
    rs0=((ROWS, 1), f32),
    a0=((ROWS, D), bf16),
    m=((ROWS, FF), bf16),
    gp=((ROWS, FF), bf16),
    xh1=((ROWS, D), bf16),
    rs1=((ROWS, 1), f32),
    a1=((ROWS, D), bf16),
    cot=((ROWS, D), bf16),
    da0=((ROWS, D), f32),
    gains=((2, 8, D), f32),
    gsum=((8, D), f32),
    gtot=((8, D), f32),
    gsr=((8, 8, D), f32),
    fm=((16, FF), bf16),
    fg=((16, FF), f32),
    fdu=((16, FF), bf16),
    fxh=((8, D), f32),
    frs=((8, 1), f32),
    cmask=((128, 128), f32),
    gath=((8, 16, 896), f32),
    cx=((8, 896), f32),
    cxr=((2, 8, 896), f32),
    ctmp=((4, 16, D), bf16),
    cfs=((8, D), f32),
    cfr=((4, 8, D), f32),
    dcs=((2, 8, D), f32),
    dcr=((8, D), f32),
    a3s=((16, D), f32),
    posf=((8, 192), f32),
    posr=((4, 8, 192), f32),
    gps=((4, 8, 192), f32),
    rx=((D, 4608), bf16),
    yb=((5, 384, CH), bf16),
    zb=((5, 3, 96, CH), bf16),
)
SEMS = dict(
    load=16, ctmp=4, ws=2, wr=2, vs=1, vr=1, gns=1, gnr=1, tks=2, tkr=2, pos_s=1, pos_r=4, cfs_s=1, cfr_r=4,
    cx_s=1, cx_r=2, gat_s=8, gat_r=8, a2_s=1, a2_r=1, a3_s=4, a3_r=1, da2_s=1, da2_r=1, dc_s=2, dc_r=1,
    gp_s=4, gp_r=1, dv_s=1, dv_r=1, a1_s=1, a1_r=1, a1_l=1, gt_s=1, gt_r=1, gt_l=1, gs_s=8, gs_r=8, og=1, ow=2,
    s1_s=9, s1_r=9, xf_s=9, xf_r=9, y_s=9, y_r=9, z_s=27, z_r=27, g_s=27, g_r=27, h_s=9, h_r=9, b_s=9, b_r=9, out=9,
)


def kernel(
    counts, tokens, cotan, w_in, w_down, gain, bias, pos,
    o_a1, o_a3, o_gt, o_g, o_gg, o_pos, *scratch,
):
    R, S = Refs(), Refs()
    for name, ref in zip(SCRATCH, scratch):
        setattr(R, name, ref)
    for name, ref in zip(SEMS, scratch[len(SCRATCH) :]):
        setattr(S, name, ref)

    dp = lax.axis_index("dp")
    sec = lax.axis_index("section")
    z, y = lax.div(dp, 2), lax.rem(dp, 2)
    xx, c = lax.div(sec, 2), lax.rem(sec, 2)

    def at(px, pc):
        return {"section": px * 2 + pc}

    def at_dp(pz, py):
        return {"dp": pz * 2 + py}

    core_peer, x_peer, diag = at(xx, 1 - c), at(1 - xx, c), at(1 - xx, 1 - c)
    y_peer = at_dp(z, 1 - y)
    z_peers = [at_dp(z ^ d, y) for d in (1, 2, 3)]
    dp_peers = [{"dp": dp ^ d} for d in range(1, 8)]

    def rcopy(src, dst, ss, rs, dev):
        return pltpu.make_async_remote_copy(
            src_ref=src, dst_ref=dst, send_sem=ss, recv_sem=rs, device_id=dev, device_id_type=MESH
        )

    def lcopy(src, dst, sem):
        return pltpu.make_async_copy(src, dst, sem)

    def count_of(i):
        return counts[lax.rem(lax.div(i, 2), 2), 2 * (c + 2 * lax.div(i, 4)) + lax.rem(i, 2)]

    R.count_of = count_of
    is0, is1 = xx == 0, xx == 1
    c0, c1 = c == 0, c == 1

    barrier = pltpu.get_barrier_semaphore()
    partners = [core_peer, x_peer, diag] + dp_peers
    for dev in partners:
        pl.semaphore_signal(barrier, inc=1, device_id=dev, device_id_type=MESH)

    own_w = lcopy(w_in, R.wall.at[jnp.where(is0, c, 1 - c)], S.load.at[0])
    own_v = lcopy(w_down, R.v0.at[cut(c * 1536, 1536)], S.load.at[1])
    own_x = lcopy(tokens, R.x.at[0:512], S.load.at[2])
    own_ct = lcopy(cotan, R.cot.at[0:512], S.load.at[3])
    heads = [lcopy(cotan.at[pl.ds(k * 128, 16)], R.ctmp.at[k], S.ctmp.at[k]) for k in range(4)]

    @pl.when(is0)
    def _():
        own_x.start()

    own_w.start()

    @pl.when(is0 | c1)
    def _():
        own_v.start()

    for cp in heads:
        cp.start()
    R.gsum[...] = jnp.zeros_like(R.gsum)
    gslot = jnp.where(is0, c, 0)
    R.gains[gslot, 0:1, :] = gain[...].astype(f32)
    R.gains[gslot, 1:2, :] = bias[...].astype(f32)
    R.posf[...] = pos[...].astype(f32)
    for cp in heads:
        cp.wait()
    first_rows = []
    for k in range(4):
        n = counts[k // 2, 2 * sec + k % 2]
        r = R.ctmp[k].astype(f32)[0:1, :]
        first_rows.append(jnp.where(n > 0, r, 0.0))
    R.cfs[...] = jnp.concatenate(first_rows + first_rows, axis=0)

    pl.semaphore_wait(barrier, len(partners))

    send_w = rcopy(w_in, R.wall.at[c], S.ws.at[0], S.wr.at[0], core_peer)
    send_v = rcopy(w_down, R.v0.at[cut(c * 1536, 1536)], S.vs.at[0], S.vr.at[0], core_peer)
    send_g = rcopy(R.gains.at[c], R.gains.at[c], S.gns.at[0], S.gnr.at[0], core_peer)
    send_x = rcopy(tokens, R.x.at[512:1024], S.tks.at[0], S.tkr.at[0], x_peer)
    send_ct = rcopy(cotan, R.cot.at[512:1024], S.tks.at[1], S.tkr.at[1], x_peer)
    other_w = rcopy(w_in, R.wall.at[1 - c], S.ws.at[0], S.wr.at[0], core_peer)
    other_v = rcopy(w_down, R.v0.at[cut((1 - c) * 1536, 1536)], S.vs.at[0], S.vr.at[0], core_peer)
    other_g = rcopy(R.gains.at[1 - c], R.gains.at[1 - c], S.gns.at[0], S.gnr.at[0], core_peer)

    def pos_copy(dev):
        return rcopy(R.posf, R.posr.at[sec], S.pos_s.at[0], S.pos_r.at[sec], dev)

    def cf_copy(dev):
        return rcopy(R.cfs, R.cfr.at[sec], S.cfs_s.at[0], S.cfr_r.at[sec], dev)

    def each_to(make, target):
        by = {2: (x_peer, diag, core_peer), 3: (diag, x_peer, core_peer)}[target]
        for s, dev in zip((0, 1, 5 - target), by):

            @pl.when(sec == s)
            def _(dev=dev):
                make(dev).start()

    def each_sent(make, target):
        @pl.when(sec != target)
        def _():
            make(core_peer).wait_send()

    @pl.when(is0)
    def _():
        send_w.start()
        send_g.start()
        send_v.start()

    @pl.when(is1)
    def _():
        send_x.start()

    each_to(pos_copy, 2)
    each_to(cf_copy, 3)

    def part_of(own, q):
        if q < 3:
            return R.m.at[0:768, pl.ds(pl.multiple_of(own * 1536 + q * CH, CH), CH)]
        return R.wall.at[own, :, pl.ds((q - 3) * CH, CH)]

    def add_rows(dst, r0, terms, n, step):
        def body(k):
            rs = pl.ds(pl.multiple_of(r0 + k * step, 32), step)
            total = dst[rs, :].astype(f32)
            for ref in terms:
                total = total + ref[pl.ds(pl.multiple_of(k * step, 32), step), :].astype(f32)
            dst[rs, :] = total.astype(bf16)

        loop(n // step, body)

    def s1_copy(q):
        return rcopy(
            part_of(1 - c, q), R.rx.at[:, pl.ds(q * CH, CH)], S.s1_s.at[q], S.s1_r.at[q], core_peer
        )

    def xf_copy(q):
        return rcopy(part_of(c, q), part_of(c, q), S.xf_s.at[q], S.xf_r.at[q], x_peer)

    def y_copy(q):
        half = part_of(c, q).at[pl.ds(pl.multiple_of((1 - y) * 384, 384), 384), :]
        return rcopy(half, R.yb.at[q // 2], S.y_s.at[q], S.y_r.at[q], y_peer)

    def z_copies(q):
        made = []
        for d in (1, 2, 3):
            piece = part_of(c, q).at[pl.ds(pl.multiple_of(y * 384 + (z ^ d) * 96, 96), 96), :]
            k = q * 3 + d - 1
            made.append(
                rcopy(piece, R.zb.at[q // 2, d - 1], S.z_s.at[k], S.z_r.at[k], z_peers[d - 1])
            )
        return made

    def g_copies(q):
        made = []
        piece = R.rx.at[pl.ds(pl.multiple_of(y * 384 + z * 96, 96), 96), pl.ds(q * CH, CH)]
        for d in (1, 2, 3):
            k = q * 3 + d - 1
            made.append(rcopy(piece, piece, S.g_s.at[k], S.g_r.at[k], z_peers[d - 1]))
        return made

    def h_copy(q):
        half = R.rx.at[pl.ds(pl.multiple_of(y * 384, 384), 384), pl.ds(q * CH, CH)]
        return rcopy(half, half, S.h_s.at[q], S.h_r.at[q], y_peer)

    def b_copy(q):
        cs = pl.ds(q * CH, CH)
        return rcopy(R.rx.at[:, cs], o_g.at[:, cs], S.b_s.at[q], S.b_r.at[q], x_peer)

    def out_copy(q):
        cs = pl.ds(q * CH, CH)
        return lcopy(R.rx.at[:, cs], o_g.at[:, cs], S.out.at[q])

    def chip_sum(q):
        s1_copy(q).wait_recv()
        add_rows(part_of(c, q), 0, [R.rx.at[:, pl.ds(q * CH, CH)]], 768, 64)
        if q % 2 == 0:
            y_copy(q).start()
        else:
            xf_copy(q).start()

    def step_a(q):
        xf_copy(q).wait_recv()
        y_copy(q).start()

    def step_b(q):
        y_copy(q).wait()
        mine = part_of(c, q)
        add_rows(mine, y * 384, [R.yb.at[q // 2]], 384, 64)
        for cp in z_copies(q):
            cp.start()

    def step_c(q):
        for cp in z_copies(q):
            cp.wait()
        r0 = pl.multiple_of(y * 384 + z * 96, 96)
        total = part_of(c, q)[pl.ds(r0, 96), :].astype(f32)
        for d in range(3):
            total = total + R.zb[q // 2, d].astype(f32)
        R.rx[pl.ds(r0, 96), pl.ds(q * CH, CH)] = total.astype(bf16)
        for cp in g_copies(q):
            cp.start()

    def step_d(q):
        for cp in g_copies(q):
            cp.wait()
        h_copy(q).start()

    def step_e0(q):
        h_copy(q).wait()
        out_copy(q).start()

    def step_e1(q):
        h_copy(q).wait()
        b_copy(q).start()

    def staged(qs, steps):
        for t in range(len(qs) + len(steps) - 1):
            for k, step in enumerate(steps):
                if 0 <= t - k < len(qs):
                    step(qs[t - k])

    def cx_copy(dev):
        return rcopy(R.cx, R.cxr.at[c], S.cx_s.at[0], S.cx_r.at[c], dev)

    def dc_copy(k, dev):
        return rcopy(R.dcs.at[k], R.dcr, S.dc_s.at[k], S.dc_r.at[0], dev)

    def a3_copy(k, dev):
        return rcopy(R.a3s, o_a3, S.a3_s.at[k], S.a3_r.at[0], dev)

    def gp_copy(s, dev):
        return rcopy(R.gps.at[s], o_pos, S.gp_s.at[s], S.gp_r.at[0], dev)

    a1_copy = rcopy(R.a1.at[512:1024], o_a1, S.a1_s.at[0], S.a1_r.at[0], x_peer)
    gt_copy = rcopy(R.cot.at[512:1024], o_gt, S.gt_s.at[0], S.gt_r.at[0], x_peer)
    a1_own = lcopy(R.a1.at[0:512], o_a1, S.a1_l.at[0])
    gt_own = lcopy(R.cot.at[0:512], o_gt, S.gt_l.at[0])
    gg_own = lcopy(R.gtot, o_gg, S.og.at[0])

    @pl.when(is0)
    def _():
        own_x.wait()
        own_ct.start()

        @pl.when(c0)
        def _():
            own_w.wait()

        @pl.when(c1)
        def _():
            other_w.wait_recv()

        other_g.wait_recv()
        qkv_half(R, 0)
        attn_half(R, 0)
        attn_out(R, 0)

        @pl.when(c1)
        def _():
            own_w.wait()

        @pl.when(c0)
        def _():
            other_w.wait_recv()

        own_v.wait()
        other_v.wait_recv()
        ffn_half(R, 0)
        send_x.wait_recv()
        qkv_half(R, 512)
        attn_half(R, 1)
        attn_out(R, 1)
        R.cx[:, 0:768] = first_ffn(R)
        it = lax.broadcasted_iota(jnp.int32, (8, 128), 0)
        flags = jnp.zeros((8, 128), f32)
        for i in range(8):
            flags = jnp.where((it == i) & (count_of(jnp.int32(i)) > 0), 1.0, flags)
        R.cx[:, 768:896] = flags

        @pl.when(c0)
        def _():
            cx_copy(x_peer).start()

        @pl.when(c1)
        def _():
            cx_copy(diag).start()

        ffn_half(R, 1)
        a1_copy.start()
        a1_own.start()
        own_ct.wait()
        send_ct.wait_recv()
        ln1_back(R)
        row_pass(R)
        dc_copy(0, core_peer).wait_recv()
        first_back(R, R.dcr[...])
        transposes1(R)
        for q in range(3):
            for n in (2 * q, 2 * q + 1, 6 + 2 * q, 7 + 2 * q):
                dvt_block(R, n)
            s1_copy(q).start()
            if q > 0:
                chip_sum(q - 1)
        for q in range(3, 9):
            dw1_block(R, 2 * (q - 3))
            dw1_block(R, 2 * (q - 3) + 1)

            @pl.when(c0)
            def _(q=q):
                s1_copy(q).start()

            if q == 3:
                chip_sum(2)
            else:

                @pl.when(c1)
                def _(q=q):
                    chip_sum(q - 1)

        a1_copy.wait_send()
        a1_own.wait()
        ln0_back(R)

        @pl.when(c1)
        def _():
            chip_sum(8)

        step_b(0)
        chip_g = rcopy(R.gsum, R.gsr.at[0], S.gs_s.at[0], S.gs_r.at[0], core_peer)
        chip_g.start()
        dctx_pass(R)
        chip_g.wait_recv()
        R.gtot[...] = R.gsum[...] + R.gsr[0]
        gsends = [
            rcopy(R.gtot, R.gsr.at[d], S.gs_s.at[d], S.gs_r.at[d], dp_peers[d - 1])
            for d in range(1, 8)
        ]
        for cp in gsends:
            cp.start()
        transposes2(R)
        step_c(0)

        def seg(i):
            attn_block_back(R, i)

            @pl.when(i == 1)
            def _():
                step_d(0)
                step_b(2)

            @pl.when(i == 3)
            def _():
                step_c(2)

                @pl.when(c1)
                def _():
                    step_b(4)

            @pl.when(i == 5)
            def _():
                step_e0(0)
                step_d(2)

                @pl.when(c1)
                def _():
                    step_c(4)
                    step_b(6)

            @pl.when(i == 7)
            def _():
                @pl.when(c1)
                def _():
                    step_d(4)
                    step_c(6)
                    step_b(8)

        loop(8, seg)
        dx_pass(R)
        gt_copy.start()
        gt_own.start()
        step_e0(2)

        @pl.when(c1)
        def _():
            step_e0(4)
            step_d(6)
            step_c(8)

        for k, q in enumerate(range(3, 9)):
            dw0_block(R, 2 * (q - 3))
            dw0_block(R, 2 * (q - 3) + 1)

            @pl.when(c1)
            def _(q=q):
                s1_copy(q).start()

            if q > 3:

                @pl.when(c0)
                def _(q=q):
                    chip_sum(q - 1)

        @pl.when(c0)
        def _():
            chip_sum(8)
            staged([4, 6, 8], [step_b, step_c, step_d, step_e0])

        @pl.when(c1)
        def _():
            step_e0(6)
            step_d(8)
            step_e0(8)

        for cp in gsends:
            cp.wait()
        total = R.gsum[...] + R.gsr[0]
        for d in range(1, 8):
            total = total + R.gsr[d]
        pair = jnp.where(c0, total[0:2], total[2:4])
        R.gtot[...] = jnp.concatenate([pair] * 4, axis=0)
        gg_own.start()
        send_w.wait_send()
        send_g.wait_send()
        send_v.wait_send()
        each_sent(pos_copy, 2)
        each_sent(cf_copy, 3)
        cx_copy(diag).wait_send()
        chip_g.wait_send()
        gt_copy.wait_send()
        gt_own.wait()
        for q in range(9):
            if q < 3:
                s1_copy(q).wait_send()
            else:

                @pl.when(c0)
                def _(q=q):
                    s1_copy(q).wait_send()

                @pl.when(c1)
                def _(q=q):
                    s1_copy(q).wait_send()

            if q % 2 == 1:
                xf_copy(q).wait_send()
                b_copy(q).wait_recv()
            else:
                out_copy(q).wait()
        a3_copy(0, diag).wait_recv()
        gp_copy(0, diag).wait_recv()
        gg_own.wait()

    def share(block):
        R.gath[dp] = block
        made = [
            rcopy(R.gath.at[dp], R.gath.at[dp], S.gat_s.at[d], S.gat_r.at[d], dp_peers[d - 1])
            for d in range(1, 8)
        ]
        for cp in made:
            cp.start()
        for d in range(1, 8):
            there = R.gath.at[dp ^ d]
            rcopy(there, there, S.gat_s.at[d], S.gat_r.at[d], dp_peers[d - 1]).wait_recv()
        return made

    @pl.when(is1)
    def _():
        send_x.wait_send()
        send_ct.start()

    @pl.when(is1 & c0)
    def _():
        rcopy(w_down, R.v0.at[0:1536], S.vs.at[0], S.vr.at[0], core_peer).start()
        for s in (0, 1, 3):
            rcopy(R.posf, R.posr.at[s], S.pos_s.at[0], S.pos_r.at[s], core_peer).wait_recv()
        R.posr[2] = R.posf[...]
        table = jnp.concatenate([R.posr[s] for s in range(4)], axis=1)
        picks = []
        for r in range(16):
            j = 2 * (r // 8 + 2 * ((r // 4) % 2)) + r % 2
            picks.append(table[j : j + 1, :])
        pos_rows = jnp.concatenate(picks, axis=0)
        for k in range(2):
            rcopy(R.cx, R.cxr.at[k], S.cx_s.at[0], S.cx_r.at[k], x_peer).wait_recv()
        own_w.wait()
        made = share(jnp.concatenate([R.cxr[0], R.cxr[1]], axis=0))
        cross_attn(R, pos_rows)
        a2 = rcopy(R.a0.at[0:128], R.a0.at[0:128], S.a2_s.at[0], S.a2_r.at[0], core_peer)
        a2.start()
        da2 = rcopy(R.a1.at[0:128], R.cot.at[0:128], S.da2_s.at[0], S.da2_r.at[0], core_peer)
        da2.wait_recv()
        cross_attn_back(R)
        for k in range(2):
            R.dcs[k] = R.da0[cut(128 + dp * 16 + k * 8, 8), :]
        dc_copy(0, x_peer).start()
        dc_copy(1, diag).start()
        rr = lax.broadcasted_iota(jnp.int32, (8, 128), 1)
        jj = lax.broadcasted_iota(jnp.int32, (8, 128), 0)
        seg_of = 2 * (((rr >> 3) & 1) + 2 * ((rr >> 2) & 1)) + (rr & 1)
        pick = jnp.where(seg_of == jj, 1.0, 0.0).astype(bf16)
        dpos = nn(pick, R.da0[128:256, :].astype(bf16))
        for s in range(4):
            R.gps[s] = dpos[:, 192 * s : 192 * s + 192]
        gp_copy(0, x_peer).start()
        gp_copy(1, diag).start()
        gp_copy(3, core_peer).start()
        gp_own = lcopy(R.gps.at[2], o_pos, S.gp_s.at[2])
        gp_own.start()
        R.gtot[...] = R.gsum[...]
        gg_own.start()
        cross_attn_weights(R)
        w_out = lcopy(R.wall.at[1], o_g.at[:, 1536:4608], S.ow.at[0])
        w_out.start()
        rcopy(w_down, R.v0.at[0:1536], S.vs.at[0], S.vr.at[0], core_peer).wait_send()
        each_sent(cf_copy, 3)
        for cp in made:
            cp.wait_send()
        a2.wait_send()
        dc_copy(0, x_peer).wait_send()
        dc_copy(1, diag).wait_send()
        gp_copy(0, x_peer).wait_send()
        gp_copy(1, diag).wait_send()
        gp_copy(3, core_peer).wait_send()
        gp_own.wait()
        gg_own.wait()
        w_out.wait()
        rcopy(R.a3s, o_a3, S.a3_s.at[0], S.a3_r.at[0], core_peer).wait_recv()

    @pl.when(is1 & c1)
    def _():
        for s in (0, 1, 2):
            rcopy(R.cfs, R.cfr.at[s], S.cfs_s.at[0], S.cfr_r.at[s], core_peer).wait_recv()
        R.cfr[3] = R.cfs[...]
        block = jnp.concatenate([R.cfr[k, 0:4] for k in (0, 2, 1, 3)], axis=0)
        made = share(jnp.concatenate([block, jnp.zeros((16, 128), f32)], axis=1))
        own_w.wait()
        own_v.wait()
        rcopy(w_down, R.v0.at[0:1536], S.vs.at[0], S.vr.at[0], core_peer).wait_recv()
        rcopy(R.a0.at[0:128], R.a0.at[0:128], S.a2_s.at[0], S.a2_r.at[0], core_peer).wait_recv()
        cross_ffn(R)
        R.a3s[...] = R.da0[cut(128 + dp * 16, 16), :]
        a3_copy(0, diag).start()
        a3_copy(1, x_peer).start()
        a3_copy(2, core_peer).start()
        a3_own = lcopy(R.a3s, o_a3, S.a3_s.at[3])
        a3_own.start()
        cross_ffn_back(R)
        da2 = rcopy(R.a1.at[0:128], R.cot.at[0:128], S.da2_s.at[0], S.da2_r.at[0], core_peer)
        da2.start()
        R.gtot[...] = R.gsum[...]
        gg_own.start()
        cross_ffn_weights(R)
        dv = rcopy(
            R.gp.at[128:896, 0:1536], o_g.at[:, 0:1536], S.dv_s.at[0], S.dv_r.at[0], core_peer
        )
        dv.start()
        w_out = lcopy(R.wall.at[0], o_g.at[:, 1536:4608], S.ow.at[0])
        v_out = lcopy(R.gp.at[128:896, 1536:3072], o_g.at[:, 0:1536], S.ow.at[1])
        w_out.start()
        v_out.start()
        each_sent(pos_copy, 2)
        for cp in made:
            cp.wait_send()
        a3_copy(0, diag).wait_send()
        a3_copy(1, x_peer).wait_send()
        a3_copy(2, core_peer).wait_send()
        a3_own.wait()
        da2.wait_send()
        gg_own.wait()
        dv.wait_send()
        w_out.wait()
        v_out.wait()
        gp_copy(0, core_peer).wait_recv()

    @pl.when(is1)
    def _():
        send_ct.wait_send()
        staged([1], [step_a, step_b, step_c, step_d, step_e1])
        staged([3, 5, 7], [step_a, step_b, step_c, step_d, step_e1])
        a1_copy.wait_recv()
        gt_copy.wait_recv()
        for q in (1, 3, 5, 7):
            b_copy(q).wait_send()

        @pl.when(c0)
        def _():
            dv = rcopy(
                R.gp.at[128:896, 0:1536], o_g.at[:, 0:1536], S.dv_s.at[0], S.dv_r.at[0], core_peer
            )
            dv.wait_recv()


def fused(counts, tokens, cotan, w_in, w_down, gain, bias, pos):
    hbm = pl.BlockSpec(memory_space=pl.ANY)
    vmem = pl.BlockSpec(memory_space=pltpu.VMEM)
    out = jax.ShapeDtypeStruct
    return pl.pallas_call(
        kernel,
        in_specs=[pl.BlockSpec(memory_space=pltpu.SMEM), hbm, hbm, hbm, hbm, vmem, vmem, vmem],
        out_specs=[hbm] * 6,
        out_shape=[
            out((512, D), bf16),
            out((16, D), f32),
            out((512, D), bf16),
            out((D, 4608), bf16),
            out((8, D), f32),
            out((8, 192), f32),
        ],
        scratch_shapes=[pltpu.VMEM(s, d) for s, d in SCRATCH.values()]
        + [pltpu.SemaphoreType.DMA((n,)) for n in SEMS.values()],
        compiler_params=pltpu.CompilerParams(
            collective_id=0, has_side_effects=True, vmem_limit_bytes=64 * 2**20 - 2**17
        ),
        name="layers",
    )(counts, tokens, cotan, w_in, w_down, gain, bias, pos)


def shards(tokens, seg_counts, w_in, w_down, ln_gain, ln_bias, pos_table, cotangent):
    sec = lax.axis_index("section")
    a1, a3, gt, g, gg, gpos = fused(
        seg_counts,
        tokens.reshape(512, D),
        cotangent.reshape(512, D),
        w_in[0],
        w_down,
        ln_gain,
        ln_bias,
        pos_table,
    )
    own = lax.dynamic_slice(seg_counts, (0, 2 * sec), (2, 2))
    top = lax.dynamic_slice(a3, (lax.rem(sec, 2) * 8 + lax.div(sec, 2) * 4, 0), (4, D))
    place = lax.broadcasted_iota(jnp.int32, (2, 2, 128, 1), 2)
    mixed = jnp.where(place == 0, top.reshape(2, 2, 1, D).astype(bf16), a1.reshape(2, 2, 128, D))
    mixed = jnp.where(place < own[:, :, None, None], mixed, jnp.zeros((), bf16))
    return (
        mixed.reshape(2, 256, D),
        gt.astype(f32).reshape(2, 256, D),
        g[:, 1536:].astype(f32)[None],
        g[:, :1536].astype(f32).T,
        gg[0:1],
        gg[1:2],
        gpos,
    )


def solution(mesh):
    return jax.shard_map(
        shards,
        mesh=mesh,
        in_specs=(
            P("dp", "section", None),
            P("dp", None),
            P("section", None, None),
            P("section", None),
            P("section", None),
            P("section", None),
            P(None, "section"),
            P("dp", "section", None),
        ),
        out_specs=(
            P("dp", "section", None),
            P("dp", "section", None),
            P("section", None, None),
            P("section", None),
            P("section", None),
            P("section", None),
            P(None, "section"),
        ),
        check_vma=False,
    )
```

```python
import functools

import jax
import jax.numpy as jnp
from jax import lax
from jax.experimental import pallas as pl
from jax.experimental.pallas import tpu as pltpu
from jax.sharding import PartitionSpec as P

bf16 = jnp.bfloat16
f32 = jnp.float32
D = 768
FF = 3072
ROWS = 1024
CH = 512
PLANE = ((0, 1, 1, 1, 1, 0, 0, 0, 0), (1, 0, 1, 0, 1, 0, 1, 0, 0))
MESH = pl.DeviceIdType.MESH


class Refs:
    pass


def nn(a, b):
    return lax.dot_general(a, b, (((1,), (0,)), ((), ())), preferred_element_type=f32)


def nt(a, b):
    return lax.dot_general(a, b, (((1,), (1,)), ((), ())), preferred_element_type=f32)


def tn(a, b):
    return lax.dot_general(a, b, (((0,), (0,)), ((), ())), preferred_element_type=f32)


def cut(start, size):
    return pl.ds(pl.multiple_of(start, size), size)


def loop(n, body):
    def step(i, carry):
        body(i)
        return carry

    lax.fori_loop(0, n, step, 0)


def norm_stats(r):
    mean = jnp.mean(r, axis=-1, keepdims=True)
    cen = r - mean
    var = jnp.mean(cen * cen, axis=-1, keepdims=True)
    rstd = lax.rsqrt(var + 1e-5)
    return cen * rstd, rstd


def norm_back(dy, xhat, rstd, gain):
    dx = dy * gain
    m1 = jnp.mean(dx, axis=-1, keepdims=True)
    m2 = jnp.mean(dx * xhat, axis=-1, keepdims=True)
    return rstd * (dx - m1 - xhat * m2)


def gelu_parts(u):
    phi = 0.5 * lax.erf(u * 0.7071067811865476) + 0.5
    density = jnp.exp2(u * u * -0.7213475204444817 - 1.3257480647361595)
    return u * phi, phi + u * density


def stacked(v):
    low = lax.broadcasted_iota(jnp.int32, v.shape, 1) < 64
    z = jnp.zeros_like(v)
    return jnp.concatenate([jnp.where(low, v, z), jnp.where(low, z, v)], axis=0)


def beside(v):
    low = lax.broadcasted_iota(jnp.int32, (128, 128), 1) < 64
    return jnp.where(low, v[:128], v[128:])


def attn_block(R, i, vis):
    rs = cut(i * 128, 128)
    for j in range(6):
        q2 = R.qkv[rs, 128 * j : 128 * j + 128]
        k2 = R.qkv[rs, 768 + 128 * j : 768 + 128 * j + 128]
        v2 = R.qkv[rs, 1536 + 128 * j : 1536 + 128 * j + 128]
        s = jnp.where(vis, nt(stacked(q2), k2) * 0.125, -1e30)
        s = jnp.exp(s - jnp.max(s, axis=-1, keepdims=True))
        pr = (s / jnp.sum(s, axis=-1, keepdims=True)).astype(bf16)
        R.p[cut(i * 1536 + 256 * j, 256), :] = pr
        R.ctx[rs, 128 * j : 128 * j + 128] = beside(nn(pr, v2)).astype(bf16)


def attn_block_back(R, i):
    rs = cut(i * 128, 128)
    for j in range(6):
        sq, sk, sv = [slice(b + 128 * j, b + 128 * j + 128) for b in (0, 768, 1536)]
        q2 = R.qkv[rs, sq]
        k2 = R.qkv[rs, sk]
        v2 = R.qkv[rs, sv]
        qs = stacked(q2)
        dos = stacked(R.xh1[rs, sq])
        pr = R.p[cut(i * 1536 + 256 * j, 256), :]
        pf = pr.astype(f32)
        dp = nt(dos, v2)
        ds = (pf * (dp - jnp.sum(dp * pf, axis=-1, keepdims=True))).astype(bf16)
        R.qkv[rs, sv] = tn(pr, dos).astype(bf16)
        R.qkv[rs, sq] = beside(nn(ds, k2) * 0.125).astype(bf16)
        R.qkv[rs, sk] = (tn(ds, qs) * 0.125).astype(bf16)


def qkv_half(R, r0):
    def body(n):
        cs = cut(n * 768, 768)
        R.qkv[pl.ds(r0, 512), cs] = nn(R.x[pl.ds(r0, 512), :], R.wall[0, :, cs]).astype(bf16)

    loop(3, body)


def attn_half(R, h):
    key = lax.broadcasted_iota(jnp.int32, (256, 128), 1)

    def seg(k):
        i = h * 4 + k
        attn_block(R, i, key < jnp.maximum(R.count_of(i), 1))

    loop(4, seg)


def attn_out(R, h):
    rs = pl.ds(h * 512, 512)
    R.da0[rs, :] = nt(R.ctx[rs, :], R.wall[0, :, 2304:])

    def norm(k):
        rs = cut(h * 512 + k * 128, 128)
        xh, rstd = norm_stats(R.x[rs, :].astype(f32) + R.da0[rs, :])
        R.xh0[rs, :] = xh.astype(bf16)
        R.rs[rs, 0:1] = rstd
        R.a0[rs, :] = (xh * R.gains[0, 0:1, :] + R.gains[0, 1:2, :]).astype(bf16)

    loop(4, norm)


def ffn_half(R, h):
    rs = pl.ds(h * 512, 512)

    def up(n):
        cs = cut(n * CH, CH)
        mm, gg = gelu_parts(nn(R.a0[rs, :], R.wall[1, :, cs]))
        R.m[rs, cs] = mm.astype(bf16)
        R.gp[rs, cs] = gg.astype(bf16)

    loop(6, up)
    R.da0[rs, :] = nn(R.m[rs, :], R.v0[...])

    def norm(k):
        rs = cut(h * 512 + k * 128, 128)
        xh, rstd = norm_stats(R.a0[rs, :].astype(f32) + R.da0[rs, :])
        R.xh1[rs, :] = xh.astype(bf16)
        R.rs[rs, 1:2] = rstd
        R.a1[rs, :] = (xh * R.gains[1, 0:1, :] + R.gains[1, 1:2, :]).astype(bf16)

    loop(4, norm)


def pad16(v):
    return jnp.concatenate([v, jnp.zeros_like(v)], axis=0).astype(bf16)


def first_ffn(R):
    rows = [R.a0[i * 128 : i * 128 + 16, :].astype(f32)[0:1, :] for i in range(8)]
    af = jnp.concatenate(rows, axis=0)
    a16 = pad16(af)

    def up(n):
        cs = cut(n * 1536, 1536)
        mm, gg = gelu_parts(nn(a16, R.wall[1, :, cs]))
        R.fm[:, cs] = mm.astype(bf16)
        R.fg[:, cs] = gg.astype(bf16)

    loop(2, up)
    xh, rstd = norm_stats(af + nn(R.fm[...], R.v0[...])[0:8])
    R.fxh[...] = xh
    R.frs[...] = rstd
    return (xh * R.gains[1, 0:1, :] + R.gains[1, 1:2, :]).astype(bf16).astype(f32)


def ln1_back(R):
    row = lax.broadcasted_iota(jnp.int32, (128, 1), 0)

    def body(i):
        rs = cut(i * 128, 128)
        live = (row < R.count_of(i)) & (row > 0)
        dy = jnp.where(live, R.cot[rs, :].astype(f32), 0.0)
        xh = R.xh1[rs, :].astype(f32)
        R.gsum[2:3, :] += jnp.sum(dy * xh, axis=0, keepdims=True)
        R.gsum[3:4, :] += jnp.sum(dy, axis=0, keepdims=True)
        dr = norm_back(dy, xh, R.rs[rs, 1:2], R.gains[1, 0:1, :])
        R.da0[rs, :] = dr
        R.cot[rs, :] = dr.astype(bf16)

    loop(8, body)


def row_pass(R):
    def hid(n):
        cs = cut(n * CH, CH)
        dm = nt(R.cot[...], R.v0[cs, :])
        R.gp[:, cs] = (dm * R.gp[:, cs].astype(f32)).astype(bf16)

    loop(6, hid)

    def back(k):
        rs = cut(k * 512, 512)
        R.da0[rs, :] += nt(R.gp[rs, :], R.wall[1])

    loop(2, back)


def put_first(ref, i, rowval):
    rs = slice(i * 128, i * 128 + 16)
    blk = ref[rs, :]
    it = lax.broadcasted_iota(jnp.int32, blk.shape, 0)
    ref[rs, :] = jnp.where(it == 0, rowval.astype(f32), blk.astype(f32)).astype(blk.dtype)


def first_back(R, dc):
    xh = R.fxh[...]
    R.gsum[2:3, :] += jnp.sum(dc * xh, axis=0, keepdims=True)
    R.gsum[3:4, :] += jnp.sum(dc, axis=0, keepdims=True)
    dr = norm_back(dc, xh, R.frs[...], R.gains[1, 0:1, :])
    dz = pad16(dr)

    def hid(n):
        cs = cut(n * 1536, 1536)
        R.fdu[:, cs] = (nt(dz, R.v0[cs, :]) * R.fg[:, cs].astype(f32)).astype(bf16)

    loop(2, hid)
    da = dr + nt(R.fdu[...], R.wall[1])[0:8]
    for i in range(8):
        put_first(R.cot, i, dr[i : i + 1, :].astype(bf16))
        put_first(R.gp, i, R.fdu[...].astype(f32)[i : i + 1, :])
        put_first(R.da0, i, da[i : i + 1, :])


def transposes1(R):
    for b, ref in ((0, R.a0), (1536, R.cot)):

        def body(k, b=b, ref=ref):
            R.v0[b : b + 768, cut(k * 256, 256)] = ref[cut(k * 256, 256), :].T

        loop(3, body)
        R.v0[b + 768 : b + 1536, 0:256] = ref[768:1024, :].T


def tdot(R, b, rhs, cs):
    head = nn(R.v0[b : b + 768, :], rhs[0:768, cs])
    return head + nn(R.v0[b + 768 : b + 1536, 0:256], rhs[768:1024, cs])


def dvt_block(R, n):
    cs = pl.ds(n * CH, CH)
    R.m[0:768, cs] = tdot(R, 1536, R.m, cs).astype(bf16)


def dw1_block(R, n):
    cs = pl.ds(n * CH, CH)
    R.wall[1, :, cs] = tdot(R, 0, R.gp, cs).astype(bf16)


def ln0_back(R):
    def body(i):
        rs = cut(i * 128, 128)
        dy = R.da0[rs, :].astype(bf16).astype(f32)
        xh = R.xh0[rs, :].astype(f32)
        R.gsum[0:1, :] += jnp.sum(dy * xh, axis=0, keepdims=True)
        R.gsum[1:2, :] += jnp.sum(dy, axis=0, keepdims=True)
        dr = norm_back(dy, xh, R.rs[rs, 0:1], R.gains[0, 0:1, :])
        R.da0[rs, :] = dr
        R.a1[rs, :] = dr.astype(bf16)

    loop(8, body)


def dctx_pass(R):
    def body(k):
        rs = cut(k * 512, 512)
        R.xh1[rs, :] = nn(R.a1[rs, :], R.wall[0, :, 2304:]).astype(bf16)

    loop(2, body)


def transposes2(R):
    for c0, ref in ((0, R.x), (1024, R.a1)):

        def body(k, c0=c0, ref=ref):
            R.gp[0:768, cut(c0 + k * 256, 256)] = ref[cut(k * 256, 256), :].T

        loop(4, body)


def dx_pass(R):
    def body(k):
        rs = cut(k * 512, 512)
        R.cot[rs, :] = (R.da0[rs, :] + nt(R.qkv[rs, :], R.wall[0, :, :2304])).astype(bf16)

    loop(2, body)


def dw0_block(R, n):
    edges = [n * CH, 2304, (n + 1) * CH] if n == 4 else [n * CH, (n + 1) * CH]
    for lo, hi in zip(edges, edges[1:]):
        if hi <= 2304:
            out = nn(R.gp[0:768, 0:1024], R.qkv[:, lo:hi])
        else:
            out = nn(R.gp[0:768, 1024:2048], R.ctx[:, lo - 2304 : hi - 2304])
        R.wall[0, :, lo:hi] = out.astype(bf16)


def cross_attn(R, pos_rows):
    cp = (R.da0[256:384, :] + jnp.concatenate([pos_rows] * 8, axis=0)).astype(bf16)
    R.x[0:128, :] = cp
    live = R.flags[...].T
    row = lax.broadcasted_iota(jnp.int32, (128, 128), 0)
    col = lax.broadcasted_iota(jnp.int32, (128, 128), 1)
    same = (row & 0x72) == (col & 0x72)
    vis = same & (live > 0.5)
    R.da0[384:512, 0:128] = jnp.where(vis, 1.0, 0.0)

    def qkv(n):
        cs = cut(n * 768, 768)
        R.qkv[0:128, cs] = nn(R.x[0:128, :], R.wall[1, :, cs]).astype(bf16)

    loop(3, qkv)
    mask = R.da0[384:512, 0:128] > 0.5
    attn_block(R, 0, jnp.concatenate([mask, mask], axis=0))
    att = nt(R.ctx[0:128, :], R.wall[1, :, 2304:])
    xh, rstd = norm_stats(R.x[0:128, :].astype(f32) + att)
    R.da0[0:128, :] = xh
    R.rs[0:128, 0:1] = rstd
    R.a0[0:128, :] = (xh * R.gains[0, 0:1, :] + R.gains[0, 1:2, :]).astype(bf16)


def cross_attn_back(R):
    dy = R.cot[0:128, :].astype(f32)
    xh = R.da0[0:128, :]
    R.gsum[0:1, :] = jnp.sum(dy * xh, axis=0, keepdims=True)
    R.gsum[1:2, :] = jnp.sum(dy, axis=0, keepdims=True)
    dr = norm_back(dy, xh, R.rs[0:128, 0:1], R.gains[0, 0:1, :])
    R.da0[0:128, :] = dr
    R.a1[0:128, :] = dr.astype(bf16)
    R.xh1[0:128, :] = nn(R.a1[0:128, :], R.wall[1, :, 2304:]).astype(bf16)
    attn_block_back(R, 0)
    dcp = R.da0[0:128, :] + nt(R.qkv[0:128, :], R.wall[1, :, :2304])
    R.da0[128:256, :] = dcp.astype(bf16).astype(f32)


def cross_attn_weights(R):
    R.gp[128:896, 0:128] = R.x[0:128, :].T
    R.gp[128:896, 128:256] = R.a1[0:128, :].T

    def one(n):
        cs = cut(n * 256, 256)
        R.wall[1, :, cs] = nn(R.gp[128:896, 0:128], R.qkv[0:128, cs]).astype(bf16)

    loop(9, one)

    def two(n):
        c2 = cut(n * 256, 256)
        cs = cut(2304 + n * 256, 256)
        R.wall[1, :, cs] = nn(R.gp[128:896, 128:256], R.ctx[0:128, c2]).astype(bf16)

    loop(3, two)


def cross_ffn(R):
    def up(n):
        cs = cut(n * 768, 768)
        mm, gg = gelu_parts(nn(R.a0[0:128, :], R.wall[0, :, cs]))
        R.gp[896:1024, cs] = mm.astype(bf16)
        R.gp[0:128, cs] = gg.astype(bf16)

    loop(4, up)
    xh, rstd = norm_stats(R.a0[0:128, :].astype(f32) + nn(R.gp[896:1024, :], R.v0[...]))
    R.da0[0:128, :] = xh
    R.rs[0:128, 0:1] = rstd
    R.da0[128:256, :] = xh * R.gains[0, 0:1, :] + R.gains[0, 1:2, :]


def cross_ffn_back(R):
    dy = R.da0[256:384, :]
    xh = R.da0[0:128, :]
    R.gsum[0:1, :] = jnp.sum(dy * xh, axis=0, keepdims=True)
    R.gsum[1:2, :] = jnp.sum(dy, axis=0, keepdims=True)
    dr = norm_back(dy, xh, R.rs[0:128, 0:1], R.gains[0, 0:1, :])
    R.da0[0:128, :] = dr
    R.cot[0:128, :] = dr.astype(bf16)

    def hid(n):
        cs = cut(n * 768, 768)
        dm = nt(R.cot[0:128, :], R.v0[cs, :])
        R.gp[0:128, cs] = (dm * R.gp[0:128, cs].astype(f32)).astype(bf16)

    loop(4, hid)
    R.a1[0:128, :] = (R.da0[0:128, :] + nt(R.gp[0:128, :], R.wall[0])).astype(bf16)


def cross_ffn_weights(R):
    R.qkv[0:768, 0:128] = R.a0[0:128, :].T
    R.qkv[0:768, 128:256] = R.cot[0:128, :].T

    def body(n):
        cs = cut(n * 256, 256)
        R.wall[0, :, cs] = nn(R.qkv[0:768, 0:128], R.gp[0:128, cs]).astype(bf16)
        R.gp[128:896, cs] = nn(R.qkv[0:768, 128:256], R.gp[896:1024, cs]).astype(bf16)

    loop(12, body)


SCRATCH = dict(
    wall=((2, D, FF), bf16),
    v0=((FF, D), bf16),
    x=((ROWS, D), bf16),
    qkv=((ROWS, 2304), bf16),
    p=((12288, 128), bf16),
    ctx=((ROWS, D), bf16),
    xh0=((ROWS, D), bf16),
    rs=((ROWS, 2), f32),
    a0=((ROWS, D), bf16),
    m=((ROWS, FF), bf16),
    gp=((ROWS, FF), bf16),
    xh1=((ROWS, D), bf16),
    a1=((ROWS, D), bf16),
    cot=((ROWS, D), bf16),
    da0=((ROWS, D), f32),
    gains=((2, 8, D), f32),
    gsum=((8, D), f32),
    gtot=((8, D), f32),
    gsr=((8, 8, D), f32),
    fm=((16, FF), bf16),
    fg=((16, FF), bf16),
    fdu=((16, FF), bf16),
    fxh=((8, D), f32),
    frs=((8, 1), f32),
    flags=((128, 128), f32),
    cx=((8, 896), f32),
    cxr=((2, 8, 896), f32),
    ctmp=((4, 16, D), bf16),
    cfs=((8, D), f32),
    cfr=((4, 8, D), f32),
    dcr=((8, D), f32),
    posf=((8, 192), f32),
    posr=((4, 8, 192), f32),
    gps=((4, 8, 192), f32),
    rx=((D, 4608), bf16),
    yb=((5, 384, CH), bf16),
    zb=((5, 3, 96, CH), bf16),
)
SEMS = dict(
    load=16, ctmp=4, ws=2, wr=2, vs=1, vr=1, gns=1, gnr=1, tks=2, tkr=2, pos_s=1, pos_r=4, cfs_s=1, cfr_r=4,
    cx_s=1, cx_r=2, gat_s=16, gat_r=16, a2_s=1, a2_r=1, a3_s=4, a3_r=1, da2_s=1, da2_r=1, dc_s=2, dc_r=1,
    gp_s=4, gp_r=1, dv_s=1, dv_r=1, a1_s=1, a1_r=1, a1_l=1, gt_s=1, gt_r=1, gt_l=1, gs_s=8, gs_r=8, og=1, ow=2,
    s1_s=9, s1_r=9, xf_s=9, xf_r=9, y_s=9, y_r=9, z_s=27, z_r=27, g_s=27, g_r=27, h_s=9, h_r=9, b_s=9, b_r=9, out=9,
)


def kernel(
    counts, tokens, cotan, w_in, w_down, gain, bias, pos,
    o_a1, o_a3, o_gt, o_gw, o_gv, o_gg, o_pos, *scratch,
):
    R, S = Refs(), Refs()
    for name, ref in zip(SCRATCH, scratch):
        setattr(R, name, ref)
    for name, ref in zip(SEMS, scratch[len(SCRATCH) :]):
        setattr(S, name, ref)

    group = lax.axis_index("dp")
    dp = lax.rem(group, 8)
    sec = lax.axis_index("section")
    z, y = lax.div(dp, 2), lax.rem(dp, 2)
    xx, c = lax.div(sec, 2), lax.rem(sec, 2)

    def at(px, pc):
        return {"section": px * 2 + pc}

    def at_dp(pz, py):
        return {"dp": group - dp + pz * 2 + py}

    core_peer, x_peer, diag = at(xx, 1 - c), at(1 - xx, c), at(1 - xx, 1 - c)
    y_peer = at_dp(z, 1 - y)
    z_peers = [at_dp(z ^ d, y) for d in (1, 2, 3)]
    dp_peers = [{"dp": group - dp + (dp ^ d)} for d in range(1, 8)]

    def rcopy(src, dst, ss, rs, dev):
        return pltpu.make_async_remote_copy(
            src_ref=src, dst_ref=dst, send_sem=ss, recv_sem=rs, device_id=dev, device_id_type=MESH
        )

    def lcopy(src, dst, sem):
        return pltpu.make_async_copy(src, dst, sem)

    def count_of(i):
        return counts[lax.rem(lax.div(i, 2), 2), 2 * (c + 2 * lax.div(i, 4)) + lax.rem(i, 2)]

    R.count_of = count_of
    is0, is1 = xx == 0, xx == 1
    c0, c1 = c == 0, c == 1

    barrier = pltpu.get_barrier_semaphore()
    partners = [core_peer, x_peer, diag] + dp_peers
    for dev in partners:
        pl.semaphore_signal(barrier, inc=1, device_id=dev, device_id_type=MESH)

    own_w = lcopy(w_in, R.wall.at[jnp.where(is0, c, 1 - c)], S.load.at[0])
    own_v = lcopy(w_down, R.v0.at[cut(c * 1536, 1536)], S.load.at[1])
    own_x = lcopy(tokens, R.x.at[0:512], S.load.at[2])
    own_ct = lcopy(cotan, R.cot.at[0:512], S.load.at[3])
    heads = [lcopy(cotan.at[pl.ds(k * 128, 16)], R.ctmp.at[k], S.ctmp.at[k]) for k in range(4)]

    @pl.when(is0)
    def _():
        own_x.start()

    own_w.start()

    @pl.when(is0 | c1)
    def _():
        own_v.start()

    for cp in heads:
        cp.start()
    R.gsum[...] = jnp.zeros_like(R.gsum)
    gslot = jnp.where(is0, c, 0)
    R.gains[gslot, 0:1, :] = gain[...].astype(f32)
    R.gains[gslot, 1:2, :] = bias[...].astype(f32)
    R.posf[...] = pos[...].astype(f32)
    for cp in heads:
        cp.wait()
    first_rows = []
    for k in range(4):
        n = counts[k // 2, 2 * sec + k % 2]
        r = R.ctmp[k].astype(f32)[0:1, :]
        first_rows.append(jnp.where(n > 0, r, 0.0))
    R.cfs[...] = jnp.concatenate(first_rows + first_rows, axis=0)

    pl.semaphore_wait(barrier, len(partners))

    send_w = rcopy(w_in, R.wall.at[c], S.ws.at[0], S.wr.at[0], core_peer)
    send_v = rcopy(w_down, R.v0.at[cut(c * 1536, 1536)], S.vs.at[0], S.vr.at[0], core_peer)
    send_g = rcopy(R.gains.at[c], R.gains.at[c], S.gns.at[0], S.gnr.at[0], core_peer)
    send_x = rcopy(tokens, R.x.at[512:1024], S.tks.at[0], S.tkr.at[0], x_peer)
    send_ct = rcopy(cotan, R.cot.at[512:1024], S.tks.at[1], S.tkr.at[1], x_peer)
    other_w = rcopy(w_in, R.wall.at[1 - c], S.ws.at[0], S.wr.at[0], core_peer)
    other_v = rcopy(w_down, R.v0.at[cut((1 - c) * 1536, 1536)], S.vs.at[0], S.vr.at[0], core_peer)
    other_g = rcopy(R.gains.at[1 - c], R.gains.at[1 - c], S.gns.at[0], S.gnr.at[0], core_peer)

    def pos_copy(dev):
        return rcopy(R.posf, R.posr.at[sec], S.pos_s.at[0], S.pos_r.at[sec], dev)

    def cf_copy(dev):
        return rcopy(R.cfs, R.cfr.at[sec], S.cfs_s.at[0], S.cfr_r.at[sec], dev)

    def each_to(make, target):
        by = {2: (x_peer, diag, core_peer), 3: (diag, x_peer, core_peer)}[target]
        for s, dev in zip((0, 1, 5 - target), by):

            @pl.when(sec == s)
            def _(dev=dev):
                make(dev).start()

    def each_sent(make, target):
        @pl.when(sec != target)
        def _():
            make(core_peer).wait_send()

    @pl.when(is0)
    def _():
        send_w.start()
        send_g.start()
        send_v.start()

    @pl.when(is1)
    def _():
        send_x.start()

    each_to(pos_copy, 2)
    each_to(cf_copy, 3)

    def part_of(own, q):
        if q < 3:
            return R.m.at[0:768, pl.ds(pl.multiple_of(own * 1536 + q * CH, CH), CH)]
        return R.wall.at[own, :, pl.ds((q - 3) * CH, CH)]

    def add_rows(dst, r0, terms, n, step):
        def body(k):
            rs = pl.ds(pl.multiple_of(r0 + k * step, 32), step)
            total = dst[rs, :].astype(f32)
            for ref in terms:
                total = total + ref[pl.ds(pl.multiple_of(k * step, 32), step), :].astype(f32)
            dst[rs, :] = total.astype(bf16)

        loop(n // step, body)

    def s1_copy(q):
        return rcopy(
            part_of(1 - c, q), R.rx.at[:, pl.ds(q * CH, CH)], S.s1_s.at[q], S.s1_r.at[q], core_peer
        )

    def xf_copy(q):
        return rcopy(part_of(c, q), part_of(c, q), S.xf_s.at[q], S.xf_r.at[q], x_peer)

    def spot(k, q):
        return PLANE[k][:q].count(PLANE[k][q])

    def y_copy(k, q):
        half = part_of(c, q).at[pl.ds(pl.multiple_of((1 - y) * 384, 384), 384), :]
        return rcopy(half, R.yb.at[spot(k, q)], S.y_s.at[q], S.y_r.at[q], y_peer)

    def z_copies(k, q):
        made = []
        for d in (1, 2, 3):
            piece = part_of(c, q).at[pl.ds(pl.multiple_of(y * 384 + (z ^ d) * 96, 96), 96), :]
            n = q * 3 + d - 1
            made.append(
                rcopy(piece, R.zb.at[spot(k, q), d - 1], S.z_s.at[n], S.z_r.at[n], z_peers[d - 1])
            )
        return made

    def g_copies(q):
        made = []
        piece = R.rx.at[pl.ds(pl.multiple_of(y * 384 + z * 96, 96), 96), pl.ds(q * CH, CH)]
        for d in (1, 2, 3):
            k = q * 3 + d - 1
            made.append(rcopy(piece, piece, S.g_s.at[k], S.g_r.at[k], z_peers[d - 1]))
        return made

    def h_copy(q):
        half = R.rx.at[pl.ds(pl.multiple_of(y * 384, 384), 384), pl.ds(q * CH, CH)]
        return rcopy(half, half, S.h_s.at[q], S.h_r.at[q], y_peer)

    def final(q):
        return o_gv.at[:, pl.ds(q * CH, CH)] if q < 3 else o_gw.at[:, pl.ds((q - 3) * CH, CH)]

    def b_copy(q):
        cs = pl.ds(q * CH, CH)
        return rcopy(R.rx.at[:, cs], final(q), S.b_s.at[q], S.b_r.at[q], x_peer)

    def out_copy(q):
        cs = pl.ds(q * CH, CH)
        return lcopy(R.rx.at[:, cs], final(q), S.out.at[q])

    def on(k, *steps):
        @pl.when(c == k)
        def _():
            for step, q in steps:
                step(k, q)

    def chip_sum(k, q):
        s1_copy(q).wait_recv()
        add_rows(part_of(c, q), 0, [R.rx.at[:, pl.ds(q * CH, CH)]], 768, 64)
        if PLANE[k][q] == 0:
            y_copy(k, q).start()
        else:
            xf_copy(q).start()

    def step_a(k, q):
        xf_copy(q).wait_recv()
        y_copy(k, q).start()

    def step_b(k, q):
        y_copy(k, q).wait()
        mine = part_of(c, q)
        add_rows(mine, y * 384, [R.yb.at[spot(k, q)]], 384, 64)
        for cp in z_copies(k, q):
            cp.start()

    def step_c(k, q):
        for cp in z_copies(k, q):
            cp.wait()
        r0 = pl.multiple_of(y * 384 + z * 96, 96)
        total = part_of(c, q)[pl.ds(r0, 96), :].astype(f32)
        for d in range(3):
            total = total + R.zb[spot(k, q), d].astype(f32)
        R.rx[pl.ds(r0, 96), pl.ds(q * CH, CH)] = total.astype(bf16)
        for cp in g_copies(q):
            cp.start()

    def step_d(k, q):
        for cp in g_copies(q):
            cp.wait()
        h_copy(q).start()

    def step_e0(k, q):
        h_copy(q).wait()
        out_copy(q).start()

    def step_e1(k, q):
        h_copy(q).wait()
        b_copy(q).start()

    def staged(k, qs, steps):
        for t in range(len(qs) + len(steps) - 1):
            for n, step in enumerate(steps):
                if 0 <= t - n < len(qs):
                    step(k, qs[t - n])

    def cx_copy(dev):
        return rcopy(R.cx, R.cxr.at[c], S.cx_s.at[0], S.cx_r.at[c], dev)

    def own_rows(r0, n):
        return R.da0.at[pl.ds(pl.multiple_of(128 + dp * 16 + r0, 8), n), :]

    def dc_copy(k, dev):
        return rcopy(own_rows(k * 8, 8), R.dcr, S.dc_s.at[k], S.dc_r.at[0], dev)

    def a3_copy(k, dev):
        return rcopy(own_rows(0, 16), o_a3, S.a3_s.at[k], S.a3_r.at[0], dev)

    def gp_copy(s, dev):
        return rcopy(R.gps.at[s], o_pos, S.gp_s.at[s], S.gp_r.at[0], dev)

    a1_copy = rcopy(R.a1.at[512:1024], o_a1, S.a1_s.at[0], S.a1_r.at[0], x_peer)
    gt_copy = rcopy(R.cot.at[512:1024], o_gt, S.gt_s.at[0], S.gt_r.at[0], x_peer)
    a1_own = lcopy(R.a1.at[0:512], o_a1, S.a1_l.at[0])
    gt_own = lcopy(R.cot.at[0:512], o_gt, S.gt_l.at[0])
    gg_own = lcopy(R.gtot, o_gg, S.og.at[0])

    @pl.when(is0)
    def _():
        own_x.wait()
        own_ct.start()

        @pl.when(c0)
        def _():
            own_w.wait()

        @pl.when(c1)
        def _():
            other_w.wait_recv()

        other_g.wait_recv()
        qkv_half(R, 0)
        attn_half(R, 0)
        attn_out(R, 0)
        send_x.wait_recv()
        qkv_half(R, 512)
        attn_half(R, 1)
        attn_out(R, 1)

        @pl.when(c1)
        def _():
            own_w.wait()

        @pl.when(c0)
        def _():
            other_w.wait_recv()

        own_v.wait()
        other_v.wait_recv()
        R.cx[:, 0:768] = first_ffn(R)
        it = lax.broadcasted_iota(jnp.int32, (8, 128), 0)
        flags = jnp.zeros((8, 128), f32)
        for i in range(8):
            flags = jnp.where((it == i) & (count_of(jnp.int32(i)) > 0), 1.0, flags)
        R.cx[:, 768:896] = flags

        @pl.when(c0)
        def _():
            cx_copy(x_peer).start()

        @pl.when(c1)
        def _():
            cx_copy(diag).start()

        ffn_half(R, 0)
        ffn_half(R, 1)
        a1_copy.start()
        a1_own.start()
        own_ct.wait()
        send_ct.wait_recv()
        ln1_back(R)
        row_pass(R)
        dc_copy(0, core_peer).wait_recv()
        first_back(R, R.dcr[...])
        transposes1(R)
        for q in range(3):
            dvt_block(R, q)
            dvt_block(R, 3 + q)
            s1_copy(q).start()
            if q > 0:
                on(0, (chip_sum, q - 1))
                on(1, (chip_sum, q - 1))
        for q in range(3, 9):
            dw1_block(R, q - 3)

            @pl.when(c0)
            def _(q=q):
                s1_copy(q).start()

            if q == 3:
                on(0, (chip_sum, 2))
            if q == 6:
                on(0, (step_b, 0))
            on(1, (chip_sum, q - 1))
            if q == 7:
                on(1, (step_b, 1))
        on(0, (step_c, 0))
        a1_copy.wait_send()
        a1_own.wait()
        ln0_back(R)
        on(1, (chip_sum, 8), (step_c, 1), (step_b, 3))
        on(0, (step_d, 0))
        chip_g = rcopy(R.gsum, R.gsr.at[0], S.gs_s.at[0], S.gs_r.at[0], core_peer)
        chip_g.start()
        dctx_pass(R)
        chip_g.wait_recv()
        R.gtot[...] = R.gsum[...] + R.gsr[0]
        gsends = [
            rcopy(R.gtot, R.gsr.at[d], S.gs_s.at[d], S.gs_r.at[d], dp_peers[d - 1])
            for d in range(1, 8)
        ]
        for cp in gsends:
            cp.start()
        transposes2(R)
        on(1, (step_d, 1), (step_c, 3), (step_b, 5))

        def seg(i):
            attn_block_back(R, i)

            @pl.when(i == 1)
            def _():
                on(0, (step_e0, 0))
                on(1, (step_e0, 1), (step_d, 3), (step_c, 5), (step_b, 7))

            @pl.when(i == 3)
            def _():
                on(1, (step_e0, 3), (step_d, 5), (step_c, 7), (step_b, 8))

            @pl.when(i == 5)
            def _():
                on(1, (step_e0, 5), (step_d, 7), (step_c, 8))

            @pl.when(i == 7)
            def _():
                on(1, (step_e0, 7), (step_d, 8))

        loop(8, seg)
        dx_pass(R)
        gt_own.start()
        for q in range(3, 9):
            dw0_block(R, q - 3)

            @pl.when(c1)
            def _(q=q):
                s1_copy(q).start()

            if q > 3:
                on(0, (chip_sum, q - 1))
            if q == 5:
                on(1, (step_e0, 8))
        gt_copy.start()

        @pl.when(c0)
        def _():
            chip_sum(0, 8)
            staged(0, [5, 6, 7, 8], [step_b, step_c, step_d, step_e0])

        for cp in gsends:
            cp.wait()
        total = R.gsum[...] + R.gsr[0]
        for d in range(1, 8):
            total = total + R.gsr[d]
        pair = jnp.where(c0, total[0:2], total[2:4])
        R.gtot[...] = jnp.concatenate([pair] * 4, axis=0)
        gg_own.start()
        send_w.wait_send()
        send_g.wait_send()
        send_v.wait_send()
        each_sent(pos_copy, 2)
        each_sent(cf_copy, 3)
        cx_copy(diag).wait_send()
        chip_g.wait_send()
        gt_copy.wait_send()
        gt_own.wait()
        for q in range(9):
            if q < 3:
                s1_copy(q).wait_send()
            else:

                @pl.when(c0)
                def _(q=q):
                    s1_copy(q).wait_send()

                @pl.when(c1)
                def _(q=q):
                    s1_copy(q).wait_send()

            for k in range(2):

                @pl.when(c == k)
                def _(q=q, k=k):
                    if PLANE[k][q] == 1:
                        xf_copy(q).wait_send()
                        b_copy(q).wait_recv()
                    else:
                        out_copy(q).wait()

        a3_copy(0, diag).wait_recv()
        gp_copy(0, diag).wait_recv()
        gg_own.wait()

    def share(block, flags):
        def both(g, d):
            rows = R.da0.at[pl.ds(pl.multiple_of(256 + g * 16, 16), 16), :]
            flag = R.flags.at[pl.ds(pl.multiple_of(g * 16, 16), 16), :]
            return [
                rcopy(ref, ref, S.gat_s.at[d + 8 * k], S.gat_r.at[d + 8 * k], dp_peers[d - 1])
                for k, ref in enumerate((rows, flag))
            ]

        R.da0[pl.ds(pl.multiple_of(256 + dp * 16, 16), 16), :] = block
        R.flags[pl.ds(pl.multiple_of(dp * 16, 16), 16), :] = flags
        made = [cp for d in range(1, 8) for cp in both(dp, d)]
        for cp in made:
            cp.start()
        for d in range(1, 8):
            for cp in both(dp ^ d, d):
                cp.wait_recv()
        return made

    @pl.when(is1)
    def _():
        send_x.wait_send()
        send_ct.start()

    @pl.when(is1 & c0)
    def _():
        rcopy(w_down, R.v0.at[0:1536], S.vs.at[0], S.vr.at[0], core_peer).start()
        for s in (0, 1, 3):
            rcopy(R.posf, R.posr.at[s], S.pos_s.at[0], S.pos_r.at[s], core_peer).wait_recv()
        R.posr[2] = R.posf[...]
        table = jnp.concatenate([R.posr[s] for s in range(4)], axis=1)
        picks = []
        for r in range(16):
            j = 2 * (r // 8 + 2 * ((r // 4) % 2)) + r % 2
            picks.append(table[j : j + 1, :])
        pos_rows = jnp.concatenate(picks, axis=0)
        for k in range(2):
            rcopy(R.cx, R.cxr.at[k], S.cx_s.at[0], S.cx_r.at[k], x_peer).wait_recv()
        own_w.wait()
        block = jnp.concatenate([R.cxr[0], R.cxr[1]], axis=0)
        made = share(block[:, 0:768], block[:, 768:896])
        cross_attn(R, pos_rows)
        a2 = rcopy(R.a0.at[0:128], R.a0.at[0:128], S.a2_s.at[0], S.a2_r.at[0], core_peer)
        a2.start()
        da2 = rcopy(R.a1.at[0:128], R.cot.at[0:128], S.da2_s.at[0], S.da2_r.at[0], core_peer)
        da2.wait_recv()
        cross_attn_back(R)
        dc_copy(0, x_peer).start()
        dc_copy(1, diag).start()
        rr = lax.broadcasted_iota(jnp.int32, (8, 128), 1)
        jj = lax.broadcasted_iota(jnp.int32, (8, 128), 0)
        seg_of = 2 * (((rr >> 3) & 1) + 2 * ((rr >> 2) & 1)) + (rr & 1)
        pick = jnp.where(seg_of == jj, 1.0, 0.0).astype(bf16)
        dpos = nn(pick, R.da0[128:256, :].astype(bf16))
        for s in range(4):
            R.gps[s] = dpos[:, 192 * s : 192 * s + 192]
        gp_copy(0, x_peer).start()
        gp_copy(1, diag).start()
        gp_copy(3, core_peer).start()
        gp_own = lcopy(R.gps.at[2], o_pos, S.gp_s.at[2])
        gp_own.start()
        R.gtot[...] = R.gsum[...]
        gg_own.start()
        cross_attn_weights(R)
        w_out = lcopy(R.wall.at[1], o_gw, S.ow.at[0])
        w_out.start()
        rcopy(w_down, R.v0.at[0:1536], S.vs.at[0], S.vr.at[0], core_peer).wait_send()
        each_sent(cf_copy, 3)
        for cp in made:
            cp.wait_send()
        a2.wait_send()
        dc_copy(0, x_peer).wait_send()
        dc_copy(1, diag).wait_send()
        gp_copy(0, x_peer).wait_send()
        gp_copy(1, diag).wait_send()
        gp_copy(3, core_peer).wait_send()
        gp_own.wait()
        gg_own.wait()
        w_out.wait()
        a3_copy(0, core_peer).wait_recv()

    @pl.when(is1 & c1)
    def _():
        for s in (0, 1, 2):
            rcopy(R.cfs, R.cfr.at[s], S.cfs_s.at[0], S.cfr_r.at[s], core_peer).wait_recv()
        R.cfr[3] = R.cfs[...]
        block = jnp.concatenate([R.cfr[k, 0:4] for k in (0, 2, 1, 3)], axis=0)
        made = share(block, jnp.zeros((16, 128), f32))
        own_w.wait()
        own_v.wait()
        rcopy(w_down, R.v0.at[0:1536], S.vs.at[0], S.vr.at[0], core_peer).wait_recv()
        rcopy(R.a0.at[0:128], R.a0.at[0:128], S.a2_s.at[0], S.a2_r.at[0], core_peer).wait_recv()
        cross_ffn(R)
        a3_copy(0, diag).start()
        a3_copy(1, x_peer).start()
        a3_copy(2, core_peer).start()
        a3_own = lcopy(own_rows(0, 16), o_a3, S.a3_s.at[3])
        a3_own.start()
        cross_ffn_back(R)
        da2 = rcopy(R.a1.at[0:128], R.cot.at[0:128], S.da2_s.at[0], S.da2_r.at[0], core_peer)
        da2.start()
        R.gtot[...] = R.gsum[...]
        gg_own.start()
        cross_ffn_weights(R)
        dv = rcopy(
            R.gp.at[128:896, 0:1536], o_gv, S.dv_s.at[0], S.dv_r.at[0], core_peer
        )
        dv.start()
        w_out = lcopy(R.wall.at[0], o_gw, S.ow.at[0])
        v_out = lcopy(R.gp.at[128:896, 1536:3072], o_gv, S.ow.at[1])
        w_out.start()
        v_out.start()
        each_sent(pos_copy, 2)
        for cp in made:
            cp.wait_send()
        a3_copy(0, diag).wait_send()
        a3_copy(1, x_peer).wait_send()
        a3_copy(2, core_peer).wait_send()
        a3_own.wait()
        da2.wait_send()
        gg_own.wait()
        dv.wait_send()
        w_out.wait()
        v_out.wait()
        gp_copy(0, core_peer).wait_recv()

    @pl.when(is1)
    def _():
        send_ct.wait_send()
        for k, sets in enumerate((([1, 2], [3, 4]), ([0, 2, 4, 6],))):

            @pl.when(c == k)
            def _(k=k, sets=sets):
                for qs in sets:
                    staged(k, qs, [step_a, step_b, step_c, step_d, step_e1])
                for q in [q for qs in sets for q in qs]:
                    b_copy(q).wait_send()

        a1_copy.wait_recv()
        gt_copy.wait_recv()

        @pl.when(c0)
        def _():
            dv = rcopy(
                R.gp.at[128:896, 0:1536], o_gv, S.dv_s.at[0], S.dv_r.at[0], core_peer
            )
            dv.wait_recv()


def fused(counts, tokens, cotan, w_in, w_down, gain, bias, pos):
    hbm = pl.BlockSpec(memory_space=pl.ANY)
    vmem = pl.BlockSpec(memory_space=pltpu.VMEM)
    out = jax.ShapeDtypeStruct
    return pl.pallas_call(
        kernel,
        in_specs=[pl.BlockSpec(memory_space=pltpu.SMEM), hbm, hbm, hbm, hbm, vmem, vmem, vmem],
        out_specs=[hbm] * 7,
        out_shape=[
            out((512, D), bf16),
            out((16, D), f32),
            out((512, D), bf16),
            out((D, FF), bf16),
            out((D, 1536), bf16),
            out((8, D), f32),
            out((8, 192), f32),
        ],
        scratch_shapes=[pltpu.VMEM(s, d) for s, d in SCRATCH.values()]
        + [pltpu.SemaphoreType.DMA((n,)) for n in SEMS.values()],
        compiler_params=pltpu.CompilerParams(
            collective_id=0, has_side_effects=True, vmem_limit_bytes=64 * 2**20 - 2**17
        ),
        name="layers",
    )(counts, tokens, cotan, w_in, w_down, gain, bias, pos)


def finish(counts, a1, a3, gt, gw, gv):
    def body(cnt, a1_ref, a3_ref, gt_ref, w_ref, v_ref, o_mixed, o_gt, o_w, o_v):
        sec = lax.axis_index("section")
        k = jnp.minimum(pl.program_id(0), 3)
        n = cnt[lax.div(k, 2), 2 * sec + lax.rem(k, 2)]
        row = lax.broadcasted_iota(jnp.int32, (128, 1), 0)
        pick = lax.rem(sec, 2) * 8 + lax.div(sec, 2) * 4 + k
        it = lax.broadcasted_iota(jnp.int32, (16, 1), 0)
        top = jnp.sum(jnp.where(it == pick, a3_ref[...], 0.0), axis=0, keepdims=True)
        both = jnp.where(row == 0, top, a1_ref[...].astype(f32))
        o_mixed[...] = jnp.where(row < n, both, 0.0).astype(bf16)
        o_gt[...] = gt_ref[...].astype(f32)
        o_w[...] = w_ref[...].astype(f32)
        o_v[...] = v_ref[...].astype(f32).T

    out = jax.ShapeDtypeStruct
    rows4 = pl.BlockSpec((128, D), lambda i: (jnp.minimum(i, 3), 0))
    return pl.pallas_call(
        body,
        grid=(12,),
        in_specs=[
            pl.BlockSpec(memory_space=pltpu.SMEM),
            rows4,
            pl.BlockSpec((16, D), lambda i: (0, 0)),
            rows4,
            pl.BlockSpec((64, FF), lambda i: (i, 0)),
            pl.BlockSpec((D, 128), lambda i: (0, i)),
        ],
        out_specs=[
            rows4,
            rows4,
            pl.BlockSpec((64, FF), lambda i: (i, 0)),
            pl.BlockSpec((128, D), lambda i: (i, 0)),
        ],
        out_shape=[
            out((512, D), bf16),
            out((512, D), f32),
            out((D, FF), f32),
            out((1536, D), f32),
        ],
        compiler_params=pltpu.CompilerParams(vmem_limit_bytes=60 * 2**20),
        name="finish",
    )(counts, a1, a3, gt, gw, gv)


def shards(tokens, seg_counts, w_in, w_down, ln_gain, ln_bias, pos_table, cotangent):
    a1, a3, gt, gw, gv, gg, gpos = fused(
        seg_counts,
        tokens.reshape(512, D),
        cotangent.reshape(512, D),
        w_in[0],
        w_down,
        ln_gain,
        ln_bias,
        pos_table,
    )
    size = lax.axis_size("dp")
    if size > 8:
        rings = [[i + 8 * k for k in range(size // 8)] for i in range(8)]
        gw, gv, gg, gpos = lax.psum((gw, gv, gg, gpos), "dp", axis_index_groups=rings)
    mixed, gtok, gw, gv = finish(seg_counts, a1, a3, gt, gw, gv)
    return (
        mixed.reshape(2, 256, D),
        gtok.reshape(2, 256, D),
        gw[None],
        gv,
        gg[0:1],
        gg[1:2],
        gpos,
    )


def solution(mesh):
    return jax.shard_map(
        shards,
        mesh=mesh,
        in_specs=(
            P("dp", "section", None),
            P("dp", None),
            P("section", None, None),
            P("section", None),
            P("section", None),
            P("section", None),
            P(None, "section"),
            P("dp", "section", None),
        ),
        out_specs=(
            P("dp", "section", None),
            P("dp", "section", None),
            P("section", None, None),
            P("section", None),
            P("section", None),
            P("section", None),
            P(None, "section"),
        ),
        check_vma=False,
    )
```

```python
import functools

import jax
import jax.numpy as jnp
from jax import lax
from jax.experimental import pallas as pl
from jax.experimental.pallas import tpu as pltpu
from jax.sharding import PartitionSpec as P

bf16 = jnp.bfloat16
f32 = jnp.float32
D = 768
FF = 3072
ROWS = 1024
WB = 512
CH = 256
SLOTS = 18
EARLY = 12
PLANE = (
    (0, 1, 0, 1, 0, 1, 0, 1, 0, 1, 0, 1, 0, 0, 1, 0, 0, 0),
    (1, 0, 1, 0, 1, 0, 1, 0, 1, 0, 1, 0, 0, 1, 0, 0, 0, 0),
)
ZONES = max(p.count(x) for p in PLANE for x in (0, 1))
MESH = pl.DeviceIdType.MESH


class Refs:
    pass


def nn(a, b):
    return lax.dot_general(a, b, (((1,), (0,)), ((), ())), preferred_element_type=f32)


def nt(a, b):
    return lax.dot_general(a, b, (((1,), (1,)), ((), ())), preferred_element_type=f32)


def tn(a, b):
    return lax.dot_general(a, b, (((0,), (0,)), ((), ())), preferred_element_type=f32)


def cut(start, size):
    return pl.ds(pl.multiple_of(start, size), size)


def loop(n, body):
    def step(i, carry):
        body(i)
        return carry

    lax.fori_loop(0, n, step, 0)


def norm_stats(r):
    mean = jnp.mean(r, axis=-1, keepdims=True)
    cen = r - mean
    var = jnp.mean(cen * cen, axis=-1, keepdims=True)
    rstd = lax.rsqrt(var + 1e-5)
    return cen * rstd, rstd


def norm_back(dy, xhat, rstd, gain):
    dx = dy * gain
    m1 = jnp.mean(dx, axis=-1, keepdims=True)
    m2 = jnp.mean(dx * xhat, axis=-1, keepdims=True)
    return rstd * (dx - m1 - xhat * m2)


def gelu_parts(u):
    phi = 0.5 * lax.erf(u * 0.7071067811865476) + 0.5
    density = jnp.exp2(u * u * -0.7213475204444817 - 1.3257480647361595)
    return u * phi, phi + u * density


def stacked(v):
    low = lax.broadcasted_iota(jnp.int32, v.shape, 1) < 64
    z = jnp.zeros_like(v)
    return jnp.concatenate([jnp.where(low, v, z), jnp.where(low, z, v)], axis=0)


def beside(v):
    low = lax.broadcasted_iota(jnp.int32, (128, 128), 1) < 64
    return jnp.where(low, v[:128], v[128:])


def attn_block(R, i, vis):
    rs = cut(i * 128, 128)
    for j in range(6):
        q2 = R.qkv[rs, 128 * j : 128 * j + 128]
        k2 = R.qkv[rs, 768 + 128 * j : 768 + 128 * j + 128]
        v2 = R.qkv[rs, 1536 + 128 * j : 1536 + 128 * j + 128]
        s = jnp.where(vis, nt(stacked(q2), k2) * 0.125, -1e30)
        s = jnp.exp(s - jnp.max(s, axis=-1, keepdims=True))
        pr = (s / jnp.sum(s, axis=-1, keepdims=True)).astype(bf16)
        R.p[cut(i * 1536 + 256 * j, 256), :] = pr
        R.ctx[rs, 128 * j : 128 * j + 128] = beside(nn(pr, v2)).astype(bf16)


def attn_block_back(R, i):
    rs = cut(i * 128, 128)
    for j in range(6):
        sq, sk, sv = [slice(b + 128 * j, b + 128 * j + 128) for b in (0, 768, 1536)]
        q2 = R.qkv[rs, sq]
        k2 = R.qkv[rs, sk]
        v2 = R.qkv[rs, sv]
        qs = stacked(q2)
        dos = stacked(R.xh1[rs, sq])
        pr = R.p[cut(i * 1536 + 256 * j, 256), :]
        pf = pr.astype(f32)
        dp = nt(dos, v2)
        ds = (pf * (dp - jnp.sum(dp * pf, axis=-1, keepdims=True))).astype(bf16)
        R.qkv[rs, sv] = tn(pr, dos).astype(bf16)
        R.qkv[rs, sq] = beside(nn(ds, k2) * 0.125).astype(bf16)
        R.qkv[rs, sk] = (tn(ds, qs) * 0.125).astype(bf16)


def qkv_half(R, r0):
    def body(n):
        cs = cut(n * 768, 768)
        R.qkv[pl.ds(r0, 512), cs] = nn(R.x[pl.ds(r0, 512), :], R.wall[0, :, cs]).astype(bf16)

    loop(3, body)


def attn_half(R, h):
    key = lax.broadcasted_iota(jnp.int32, (256, 128), 1)

    def seg(k):
        i = h * 4 + k
        attn_block(R, i, key < jnp.maximum(R.count_of(i), 1))

    loop(4, seg)


def attn_out(R, h):
    rs = pl.ds(h * 512, 512)
    R.da0[rs, :] = nt(R.ctx[rs, :], R.wall[0, :, 2304:])

    def norm(k):
        rs = cut(h * 512 + k * 128, 128)
        xh, rstd = norm_stats(R.x[rs, :].astype(f32) + R.da0[rs, :])
        R.xh0[rs, :] = xh.astype(bf16)
        R.rs[rs, 0:1] = rstd
        R.a0[rs, :] = (xh * R.gains[0, 0:1, :] + R.gains[0, 1:2, :]).astype(bf16)

    loop(4, norm)


def ffn_half(R, h):
    rs = pl.ds(h * 512, 512)

    def up(n):
        cs = cut(n * WB, WB)
        mm, gg = gelu_parts(nn(R.a0[rs, :], R.wall[1, :, cs]))
        R.m[rs, cs] = mm.astype(bf16)
        R.gp[rs, cs] = gg.astype(bf16)

    loop(6, up)
    R.da0[rs, :] = nn(R.m[rs, :], R.v0[...])

    def norm(k):
        rs = cut(h * 512 + k * 128, 128)
        xh, rstd = norm_stats(R.a0[rs, :].astype(f32) + R.da0[rs, :])
        R.xh1[rs, :] = xh.astype(bf16)
        R.rs[rs, 1:2] = rstd
        R.a1[rs, :] = (xh * R.gains[1, 0:1, :] + R.gains[1, 1:2, :]).astype(bf16)

    loop(4, norm)


def pad16(v):
    return jnp.concatenate([v, jnp.zeros_like(v)], axis=0).astype(bf16)


def first_ffn(R):
    rows = [R.a0[i * 128 : i * 128 + 16, :].astype(f32)[0:1, :] for i in range(8)]
    af = jnp.concatenate(rows, axis=0)
    a16 = pad16(af)

    def up(n):
        cs = cut(n * 1536, 1536)
        mm, gg = gelu_parts(nn(a16, R.wall[1, :, cs]))
        R.fm[:, cs] = mm.astype(bf16)
        R.fg[:, cs] = gg.astype(bf16)

    loop(2, up)
    xh, rstd = norm_stats(af + nn(R.fm[...], R.v0[...])[0:8])
    R.fxh[...] = xh
    R.frs[...] = rstd
    return (xh * R.gains[1, 0:1, :] + R.gains[1, 1:2, :]).astype(bf16).astype(f32)


def ln1_back(R):
    row = lax.broadcasted_iota(jnp.int32, (128, 1), 0)

    def body(i):
        rs = cut(i * 128, 128)
        live = (row < R.count_of(i)) & (row > 0)
        dy = jnp.where(live, R.cot[rs, :].astype(f32), 0.0)
        xh = R.xh1[rs, :].astype(f32)
        R.gsum[2:3, :] += jnp.sum(dy * xh, axis=0, keepdims=True)
        R.gsum[3:4, :] += jnp.sum(dy, axis=0, keepdims=True)
        dr = norm_back(dy, xh, R.rs[rs, 1:2], R.gains[1, 0:1, :])
        R.da0[rs, :] = dr
        R.cot[rs, :] = dr.astype(bf16)

    loop(8, body)


def row_pass(R):
    def hid(n):
        cs = cut(n * WB, WB)
        dm = nt(R.cot[...], R.v0[cs, :])
        R.gp[:, cs] = (dm * R.gp[:, cs].astype(f32)).astype(bf16)

    loop(6, hid)

    def back(k):
        rs = cut(k * 512, 512)
        R.da0[rs, :] += nt(R.gp[rs, :], R.wall[1])

    loop(2, back)


def put_first(ref, i, rowval):
    rs = slice(i * 128, i * 128 + 16)
    blk = ref[rs, :]
    it = lax.broadcasted_iota(jnp.int32, blk.shape, 0)
    ref[rs, :] = jnp.where(it == 0, rowval.astype(f32), blk.astype(f32)).astype(blk.dtype)


def first_back(R, dc):
    xh = R.fxh[...]
    R.gsum[2:3, :] += jnp.sum(dc * xh, axis=0, keepdims=True)
    R.gsum[3:4, :] += jnp.sum(dc, axis=0, keepdims=True)
    dr = norm_back(dc, xh, R.frs[...], R.gains[1, 0:1, :])
    dz = pad16(dr)

    def hid(n):
        cs = cut(n * 1536, 1536)
        R.fdu[:, cs] = (nt(dz, R.v0[cs, :]) * R.fg[:, cs].astype(f32)).astype(bf16)

    loop(2, hid)
    da = dr + nt(R.fdu[...], R.wall[1])[0:8]
    for i in range(8):
        put_first(R.cot, i, dr[i : i + 1, :].astype(bf16))
        put_first(R.gp, i, R.fdu[...].astype(f32)[i : i + 1, :])
        put_first(R.da0, i, da[i : i + 1, :])


def transposes1(R):
    for b, ref in ((0, R.a0), (1536, R.cot)):

        def body(k, b=b, ref=ref):
            R.v0[b : b + 768, cut(k * 256, 256)] = ref[cut(k * 256, 256), :].T

        loop(3, body)
        R.v0[b + 768 : b + 1536, 0:256] = ref[768:1024, :].T


def tdot(R, b, rhs, cs):
    head = nn(R.v0[b : b + 768, :], rhs[0:768, cs])
    return head + nn(R.v0[b + 768 : b + 1536, 0:256], rhs[768:1024, cs])


def dvt_block(R, n):
    cs = pl.ds(n * WB, WB)
    R.m[0:768, cs] = tdot(R, 1536, R.m, cs).astype(bf16)


def dw1_block(R, n):
    cs = pl.ds(n * WB, WB)
    R.wall[1, :, cs] = tdot(R, 0, R.gp, cs).astype(bf16)


def ln0_back(R):
    def body(i):
        rs = cut(i * 128, 128)
        dy = R.da0[rs, :].astype(bf16).astype(f32)
        xh = R.xh0[rs, :].astype(f32)
        R.gsum[0:1, :] += jnp.sum(dy * xh, axis=0, keepdims=True)
        R.gsum[1:2, :] += jnp.sum(dy, axis=0, keepdims=True)
        dr = norm_back(dy, xh, R.rs[rs, 0:1], R.gains[0, 0:1, :])
        R.da0[rs, :] = dr
        R.a1[rs, :] = dr.astype(bf16)

    loop(8, body)


def dctx_pass(R):
    def body(k):
        rs = cut(k * 512, 512)
        R.xh1[rs, :] = nn(R.a1[rs, :], R.wall[0, :, 2304:]).astype(bf16)

    loop(2, body)


def transposes2(R):
    for c0, ref in ((0, R.x), (1024, R.a1)):

        def body(k, c0=c0, ref=ref):
            R.gp[0:768, cut(c0 + k * 256, 256)] = ref[cut(k * 256, 256), :].T

        loop(4, body)


def dx_pass(R):
    def body(k):
        rs = cut(k * 512, 512)
        R.cot[rs, :] = (R.da0[rs, :] + nt(R.qkv[rs, :], R.wall[0, :, :2304])).astype(bf16)

    loop(2, body)


def dw0_block(R, n):
    edges = [n * WB, 2304, (n + 1) * WB] if n == 4 else [n * WB, (n + 1) * WB]
    for lo, hi in zip(edges, edges[1:]):
        if hi <= 2304:
            out = nn(R.gp[0:768, 0:1024], R.qkv[:, lo:hi])
        else:
            out = nn(R.gp[0:768, 1024:2048], R.ctx[:, lo - 2304 : hi - 2304])
        R.wall[0, :, lo:hi] = out.astype(bf16)


def cross_attn(R, pos_rows):
    cp = (R.da0[256:384, :] + jnp.concatenate([pos_rows] * 8, axis=0)).astype(bf16)
    R.x[0:128, :] = cp
    live = R.flags[...].T
    row = lax.broadcasted_iota(jnp.int32, (128, 128), 0)
    col = lax.broadcasted_iota(jnp.int32, (128, 128), 1)
    same = (row & 0x72) == (col & 0x72)
    vis = same & (live > 0.5)
    R.da0[384:512, 0:128] = jnp.where(vis, 1.0, 0.0)

    def qkv(n):
        cs = cut(n * 768, 768)
        R.qkv[0:128, cs] = nn(R.x[0:128, :], R.wall[1, :, cs]).astype(bf16)

    loop(3, qkv)
    mask = R.da0[384:512, 0:128] > 0.5
    attn_block(R, 0, jnp.concatenate([mask, mask], axis=0))
    att = nt(R.ctx[0:128, :], R.wall[1, :, 2304:])
    xh, rstd = norm_stats(R.x[0:128, :].astype(f32) + att)
    R.da0[0:128, :] = xh
    R.rs[0:128, 0:1] = rstd
    R.a0[0:128, :] = (xh * R.gains[0, 0:1, :] + R.gains[0, 1:2, :]).astype(bf16)


def cross_attn_back(R):
    dy = R.cot[0:128, :].astype(f32)
    xh = R.da0[0:128, :]
    R.gsum[0:1, :] = jnp.sum(dy * xh, axis=0, keepdims=True)
    R.gsum[1:2, :] = jnp.sum(dy, axis=0, keepdims=True)
    dr = norm_back(dy, xh, R.rs[0:128, 0:1], R.gains[0, 0:1, :])
    R.da0[0:128, :] = dr
    R.a1[0:128, :] = dr.astype(bf16)
    R.xh1[0:128, :] = nn(R.a1[0:128, :], R.wall[1, :, 2304:]).astype(bf16)
    attn_block_back(R, 0)
    dcp = R.da0[0:128, :] + nt(R.qkv[0:128, :], R.wall[1, :, :2304])
    R.da0[128:256, :] = dcp.astype(bf16).astype(f32)


def cross_attn_weights(R):
    R.gp[128:896, 0:128] = R.x[0:128, :].T
    R.gp[128:896, 128:256] = R.a1[0:128, :].T

    def one(n):
        cs = cut(n * 256, 256)
        R.wall[1, :, cs] = nn(R.gp[128:896, 0:128], R.qkv[0:128, cs]).astype(bf16)

    loop(9, one)

    def two(n):
        c2 = cut(n * 256, 256)
        cs = cut(2304 + n * 256, 256)
        R.wall[1, :, cs] = nn(R.gp[128:896, 128:256], R.ctx[0:128, c2]).astype(bf16)

    loop(3, two)


def cross_ffn(R):
    def up(n):
        cs = cut(n * 768, 768)
        mm, gg = gelu_parts(nn(R.a0[0:128, :], R.wall[0, :, cs]))
        R.gp[896:1024, cs] = mm.astype(bf16)
        R.gp[0:128, cs] = gg.astype(bf16)

    loop(4, up)
    xh, rstd = norm_stats(R.a0[0:128, :].astype(f32) + nn(R.gp[896:1024, :], R.v0[...]))
    R.da0[0:128, :] = xh
    R.rs[0:128, 0:1] = rstd
    R.da0[128:256, :] = xh * R.gains[0, 0:1, :] + R.gains[0, 1:2, :]


def cross_ffn_back(R):
    dy = R.da0[256:384, :]
    xh = R.da0[0:128, :]
    R.gsum[0:1, :] = jnp.sum(dy * xh, axis=0, keepdims=True)
    R.gsum[1:2, :] = jnp.sum(dy, axis=0, keepdims=True)
    dr = norm_back(dy, xh, R.rs[0:128, 0:1], R.gains[0, 0:1, :])
    R.da0[0:128, :] = dr
    R.cot[0:128, :] = dr.astype(bf16)

    def hid(n):
        cs = cut(n * 768, 768)
        dm = nt(R.cot[0:128, :], R.v0[cs, :])
        R.gp[0:128, cs] = (dm * R.gp[0:128, cs].astype(f32)).astype(bf16)

    loop(4, hid)
    R.a1[0:128, :] = (R.da0[0:128, :] + nt(R.gp[0:128, :], R.wall[0])).astype(bf16)


def cross_ffn_weights(R):
    R.qkv[0:768, 0:128] = R.a0[0:128, :].T
    R.qkv[0:768, 128:256] = R.cot[0:128, :].T

    def body(n):
        cs = cut(n * 256, 256)
        R.wall[0, :, cs] = nn(R.qkv[0:768, 0:128], R.gp[0:128, cs]).astype(bf16)
        R.gp[128:896, cs] = nn(R.qkv[0:768, 128:256], R.gp[896:1024, cs]).astype(bf16)

    loop(12, body)


SCRATCH = dict(
    wall=((2, D, FF), bf16),
    v0=((FF, D), bf16),
    x=((ROWS, D), bf16),
    qkv=((ROWS, 2304), bf16),
    p=((12288, 128), bf16),
    ctx=((ROWS, D), bf16),
    xh0=((ROWS, D), bf16),
    rs=((ROWS, 2), f32),
    a0=((ROWS, D), bf16),
    m=((ROWS, FF), bf16),
    gp=((ROWS, FF), bf16),
    xh1=((ROWS, D), bf16),
    a1=((ROWS, D), bf16),
    cot=((ROWS, D), bf16),
    da0=((ROWS, D), f32),
    gains=((2, 8, D), f32),
    gsum=((8, D), f32),
    gtot=((8, D), f32),
    gsr=((8, 8, D), f32),
    fm=((16, FF), bf16),
    fg=((16, FF), bf16),
    fdu=((16, FF), bf16),
    fxh=((8, D), f32),
    frs=((8, 1), f32),
    flags=((128, 128), f32),
    cx=((8, 896), f32),
    cxr=((2, 8, 896), f32),
    ctmp=((4, 16, D), bf16),
    cfs=((8, D), f32),
    cfr=((4, 8, D), f32),
    dcr=((8, D), f32),
    posf=((8, 192), f32),
    posr=((4, 8, 192), f32),
    gps=((4, 8, 192), f32),
    rx=((6, D, CH), bf16),
    yb=((ZONES, 384, CH), bf16),
    zb=((ZONES, 2, 384, CH), bf16),
)
SEMS = dict(
    load=16, ctmp=4, ws=2, wr=2, vs=1, vr=1, gns=1, gnr=1, tks=2, tkr=2, pos_s=1, pos_r=4, cfs_s=1, cfr_r=4,
    cx_s=1, cx_r=2, gat_s=16, gat_r=16, a2_s=1, a2_r=1, a3_s=4, a3_r=1, da2_s=1, da2_r=1, dc_s=2, dc_r=1,
    gp_s=4, gp_r=1, dv_s=1, dv_r=1, a1_s=1, a1_r=1, a1_l=1, gt_s=1, gt_r=1, gt_l=1, gs_s=8, gs_r=8, og=1, ow=2,
    s1_s=18, s1_r=18, xf_s=18, xf_r=18, y_s=18, y_r=18, z1_s=18, z1_r=18, z2_s=18, z2_r=18, z3_s=18, z3_r=18,
    h_s=18, h_r=36, b1_s=18, b1_r=36, b2_s=18, b2_r=36, out_s=18, out_r=36, hx_r=18,
)


def kernel(
    counts, tokens, cotan, w_in, w_down, gain, bias, pos,
    o_a1, o_a3, o_gt, o_gw, o_gv, o_gg, o_pos, o_pass, *scratch,
):
    R, S = Refs(), Refs()
    for name, ref in zip(SCRATCH, scratch):
        setattr(R, name, ref)
    free = scratch[-1]
    for name, ref in zip(SEMS, scratch[len(SCRATCH) :]):
        setattr(S, name, ref)

    group = lax.axis_index("dp")
    dp = lax.rem(group, 8)
    sec = lax.axis_index("section")
    z, y = lax.div(dp, 2), lax.rem(dp, 2)
    xx, c = lax.div(sec, 2), lax.rem(sec, 2)

    def at(px, pc):
        return {"section": px * 2 + pc}

    def at_dp(pz, py):
        return {"dp": group - dp + pz * 2 + py}

    core_peer, x_peer, diag = at(xx, 1 - c), at(1 - xx, c), at(1 - xx, 1 - c)
    y_peer = at_dp(z, 1 - y)
    z_near, z_over = at_dp(z ^ 1, y), at_dp(z ^ 3, y)
    middle = (z == 1) | (z == 2)
    dp_peers = [{"dp": group - dp + (dp ^ d)} for d in range(1, 8)]

    def rcopy(src, dst, ss, rs, dev):
        return pltpu.make_async_remote_copy(
            src_ref=src, dst_ref=dst, send_sem=ss, recv_sem=rs, device_id=dev, device_id_type=MESH
        )

    def lcopy(src, dst, sem):
        return pltpu.make_async_copy(src, dst, sem)

    def count_of(i):
        return counts[lax.rem(lax.div(i, 2), 2), 2 * (c + 2 * lax.div(i, 4)) + lax.rem(i, 2)]

    R.count_of = count_of
    is0, is1 = xx == 0, xx == 1
    c0, c1 = c == 0, c == 1

    barrier = pltpu.get_barrier_semaphore()
    partners = [core_peer, x_peer, diag] + dp_peers
    for dev in partners:
        pl.semaphore_signal(barrier, inc=1, device_id=dev, device_id_type=MESH)

    own_w = lcopy(w_in, R.wall.at[jnp.where(is0, c, 1 - c)], S.load.at[0])
    own_v = lcopy(w_down, R.v0.at[cut(c * 1536, 1536)], S.load.at[1])
    own_x = lcopy(tokens, R.x.at[0:512], S.load.at[2])
    own_ct = lcopy(cotan, R.cot.at[0:512], S.load.at[3])
    heads = [lcopy(cotan.at[pl.ds(k * 128, 16)], R.ctmp.at[k], S.ctmp.at[k]) for k in range(4)]

    @pl.when(is0)
    def _():
        own_x.start()

    own_w.start()

    @pl.when(is0 | c1)
    def _():
        own_v.start()

    for cp in heads:
        cp.start()
    R.gsum[...] = jnp.zeros_like(R.gsum)
    gslot = jnp.where(is0, c, 0)
    R.gains[gslot, 0:1, :] = gain[...].astype(f32)
    R.gains[gslot, 1:2, :] = bias[...].astype(f32)
    R.posf[...] = pos[...].astype(f32)
    for cp in heads:
        cp.wait()
    first_rows = []
    for k in range(4):
        n = counts[k // 2, 2 * sec + k % 2]
        r = R.ctmp[k].astype(f32)[0:1, :]
        first_rows.append(jnp.where(n > 0, r, 0.0))
    R.cfs[...] = jnp.concatenate(first_rows + first_rows, axis=0)

    pl.semaphore_wait(barrier, len(partners))

    send_w = rcopy(w_in, R.wall.at[c], S.ws.at[0], S.wr.at[0], core_peer)
    send_v = rcopy(w_down, R.v0.at[cut(c * 1536, 1536)], S.vs.at[0], S.vr.at[0], core_peer)
    send_g = rcopy(R.gains.at[c], R.gains.at[c], S.gns.at[0], S.gnr.at[0], core_peer)
    send_x = rcopy(tokens, R.x.at[512:1024], S.tks.at[0], S.tkr.at[0], x_peer)
    send_ct = rcopy(cotan, R.cot.at[512:1024], S.tks.at[1], S.tkr.at[1], x_peer)
    other_w = rcopy(w_in, R.wall.at[1 - c], S.ws.at[0], S.wr.at[0], core_peer)
    other_v = rcopy(w_down, R.v0.at[cut((1 - c) * 1536, 1536)], S.vs.at[0], S.vr.at[0], core_peer)
    other_g = rcopy(R.gains.at[1 - c], R.gains.at[1 - c], S.gns.at[0], S.gnr.at[0], core_peer)

    def pos_copy(dev):
        return rcopy(R.posf, R.posr.at[sec], S.pos_s.at[0], S.pos_r.at[sec], dev)

    def cf_copy(dev):
        return rcopy(R.cfs, R.cfr.at[sec], S.cfs_s.at[0], S.cfr_r.at[sec], dev)

    def each_to(make, target):
        by = {2: (x_peer, diag, core_peer), 3: (diag, x_peer, core_peer)}[target]
        for s, dev in zip((0, 1, 5 - target), by):

            @pl.when(sec == s)
            def _(dev=dev):
                make(dev).start()

    def each_sent(make, target):
        @pl.when(sec != target)
        def _():
            make(core_peer).wait_send()

    @pl.when(is0)
    def _():
        send_w.start()
        send_g.start()
        send_v.start()

    @pl.when(is1)
    def _():
        send_x.start()

    each_to(pos_copy, 2)
    each_to(cf_copy, 3)

    def block_of(own, q):
        return 2 * (q % 6) + (own if q < EARLY else 1 - own)

    def slot(own, q, index):
        if q < 6:
            return R.m.at[0:768, pl.ds(pl.multiple_of(own * 1536 + q * CH, CH), CH)]
        return R.wall.at[index, :, pl.ds(pl.multiple_of(block_of(own, q) * CH, CH), CH)]

    def part_of(own, q):
        return slot(own, q, jnp.where(is0, 1 if q < EARLY else 0, c))

    def holder(k, q):
        return k if q < 6 else (1 if q < EARLY else 0)

    def add_rows(dst, r0, terms, n, step):
        def body(k):
            rs = pl.ds(pl.multiple_of(r0 + k * step, 32), step)
            total = dst[rs, :].astype(f32)
            for ref in terms:
                total = total + ref[pl.ds(pl.multiple_of(k * step, 32), step), :].astype(f32)
            dst[rs, :] = total.astype(bf16)

        loop(n // step, body)

    def s1_copy(q):
        return rcopy(
            part_of(1 - c, q), R.rx.at[q % 6], S.s1_s.at[q], S.s1_r.at[q], core_peer
        )

    def s1_send(q):
        if q >= 6:
            pl.semaphore_wait(free, 1)
        s1_copy(q).start()

    def xf_copy(q):
        return rcopy(part_of(c, q), slot(c, q, c), S.xf_s.at[q], S.xf_r.at[q], x_peer)

    def spot(k, q):
        return PLANE[k][:q].count(PLANE[k][q])

    def y_copy(k, q):
        half = part_of(c, q).at[pl.ds(pl.multiple_of((1 - y) * 384, 384), 384), :]
        return rcopy(half, R.yb.at[spot(k, q)], S.y_s.at[q], S.y_r.at[q], y_peer)

    def half_of(ref, h):
        return ref.at[pl.ds(pl.multiple_of(h * 384, 384), 384), :]

    def z1_copy(k, q):
        zone = R.zb.at[spot(k, q), 0]
        return rcopy(half_of(part_of(c, q), y), zone, S.z1_s.at[q], S.z1_r.at[q], z_near)

    def z2_copy(k, q):
        zone = R.zb.at[spot(k, q), 1]
        return rcopy(half_of(part_of(c, q), y), zone, S.z2_s.at[q], S.z2_r.at[q], z_over)

    def z3_copy(k, q):
        zone = R.zb.at[spot(k, q), 0]
        return rcopy(zone, zone, S.z3_s.at[q], S.z3_r.at[q], z_near)

    def final(k, q):
        if q < 6:
            return o_gv.at[:, pl.ds(q * CH, CH)]
        return o_gw.at[:, pl.ds(block_of(k, q) * CH, CH)]

    def passing(q):
        return o_pass.at[:, pl.ds(q * CH, CH)]

    def h_copy(k, q):
        zone = R.zb.at[spot(k, q), 0]
        if PLANE[k][q] == 1:
            return rcopy(zone, half_of(passing(q), y), S.h_s.at[q], S.hx_r.at[q], y_peer)
        there = {**y_peer, **at(xx, holder(k, q))}
        return rcopy(zone, half_of(final(k, q), y), S.h_s.at[q], S.h_r.at[SLOTS * k + q], there)

    def out_copy(k, q):
        zone, there = R.zb.at[spot(k, q), 0], half_of(final(k, q), y)
        if holder(k, q) == k:
            return lcopy(zone, there, S.out_s.at[q])
        return rcopy(zone, there, S.out_s.at[q], S.out_r.at[SLOTS * k + q], core_peer)

    def b1_copy(k, q):
        zone = R.zb.at[spot(k, q), 0]
        there = at(1 - xx, holder(k, q))
        return rcopy(zone, half_of(final(k, q), y), S.b1_s.at[q], S.b1_r.at[SLOTS * k + q], there)

    def b2_copy(k, q):
        src, there = half_of(passing(q), 1 - y), at(1 - xx, holder(k, q))
        return rcopy(src, half_of(final(k, q), 1 - y), S.b2_s.at[q], S.b2_r.at[SLOTS * k + q], there)

    def on(k, *steps):
        @pl.when(c == k)
        def _():
            for step, q in steps:
                step(k, q)

    def chip_sum(k, q):
        s1_copy(q).wait_recv()
        add_rows(part_of(c, q), 0, [R.rx.at[q % 6]], 768, 64)
        if q < SLOTS - 6:
            pl.semaphore_signal(free, inc=1, device_id=core_peer, device_id_type=MESH)
        if PLANE[k][q] == 0:
            y_copy(k, q).start()
        else:
            xf_copy(q).start()

    def step_a(k, q):
        xf_copy(q).wait_recv()
        y_copy(k, q).start()

    def step_b(k, q):
        y_copy(k, q).wait()
        add_rows(part_of(c, q), y * 384, [R.yb.at[spot(k, q)]], 384, 64)

        @pl.when(jnp.logical_not(middle))
        def _():
            z1_copy(k, q).start()

    def step_c(k, q):
        @pl.when(middle)
        def _():
            z1_copy(k, q).wait_recv()
            add_rows(part_of(c, q), y * 384, [R.zb.at[spot(k, q), 0]], 384, 64)
            z2_copy(k, q).start()

    def step_d(k, q):
        n = spot(k, q)

        @pl.when(middle)
        def _():
            z2_copy(k, q).wait()
            mine = half_of(part_of(c, q), y)

            def body(r):
                rs = cut(r * 64, 64)
                total = mine[rs, :].astype(f32) + R.zb[n, 1, rs, :].astype(f32)
                R.zb[n, 0, rs, :] = total.astype(bf16)

            loop(6, body)
            z3_copy(k, q).start()

        @pl.when(jnp.logical_not(middle))
        def _():
            z1_copy(k, q).wait_send()
            z3_copy(k, q).wait_recv()

        h_copy(k, q).start()
        if PLANE[k][q] == 0:
            out_copy(k, q).start()
        else:
            b1_copy(k, q).start()

    def step_e(k, q):
        h_copy(k, q).wait_recv()
        b2_copy(k, q).start()

    def step_end(k, q):
        @pl.when(middle)
        def _():
            z3_copy(k, q).wait_send()

        h_copy(k, q).wait_send()
        if PLANE[k][q] == 1:
            b1_copy(k, q).wait_send()
            b2_copy(k, q).wait_send()
        elif holder(k, q) == k:
            out_copy(k, q).wait()
        else:
            out_copy(k, q).wait_send()

    def arrived(k, q):
        if PLANE[k][q] == 1:
            b1_copy(k, q).wait_recv()
            b2_copy(k, q).wait_recv()
            return
        h_copy(k, q).wait_recv()
        if holder(k, q) != k:
            out_copy(k, q).wait_recv()

    def ticks(qs, steps):
        made = []
        for t in range(len(qs) + len(steps) - 1):
            made.append([(f, qs[t - n]) for n, f in enumerate(steps) if 0 <= t - n < len(qs)])
        return made

    early = [[q for q in range(EARLY) if PLANE[k][q] == 0] for k in range(2)]
    late = [[q for q in range(EARLY, SLOTS) if PLANE[k][q] == 0] for k in range(2)]
    planned = [ticks(early[k], [step_b, step_c, step_d]) for k in range(2)]

    def serve(first, last):
        for k in range(2):
            for tick in planned[k][first:last]:
                on(k, *tick)

    def cx_copy(dev):
        return rcopy(R.cx, R.cxr.at[c], S.cx_s.at[0], S.cx_r.at[c], dev)

    def own_rows(r0, n):
        return R.da0.at[pl.ds(pl.multiple_of(128 + dp * 16 + r0, 8), n), :]

    def dc_copy(k, dev):
        return rcopy(own_rows(k * 8, 8), R.dcr, S.dc_s.at[k], S.dc_r.at[0], dev)

    def a3_copy(k, dev):
        return rcopy(own_rows(0, 16), o_a3, S.a3_s.at[k], S.a3_r.at[0], dev)

    def gp_copy(s, dev):
        return rcopy(R.gps.at[s], o_pos, S.gp_s.at[s], S.gp_r.at[0], dev)

    a1_copy = rcopy(R.a1.at[512:1024], o_a1, S.a1_s.at[0], S.a1_r.at[0], x_peer)
    gt_copy = rcopy(R.cot.at[512:1024], o_gt, S.gt_s.at[0], S.gt_r.at[0], x_peer)
    a1_own = lcopy(R.a1.at[0:512], o_a1, S.a1_l.at[0])
    gt_own = lcopy(R.cot.at[0:512], o_gt, S.gt_l.at[0])
    gg_own = lcopy(R.gtot, o_gg, S.og.at[0])

    @pl.when(is0)
    def _():
        own_x.wait()
        own_ct.start()

        @pl.when(c0)
        def _():
            own_w.wait()

        @pl.when(c1)
        def _():
            other_w.wait_recv()

        other_g.wait_recv()
        qkv_half(R, 0)
        attn_half(R, 0)
        attn_out(R, 0)
        send_x.wait_recv()
        qkv_half(R, 512)
        attn_half(R, 1)
        attn_out(R, 1)

        @pl.when(c1)
        def _():
            own_w.wait()

        @pl.when(c0)
        def _():
            other_w.wait_recv()

        own_v.wait()
        other_v.wait_recv()
        R.cx[:, 0:768] = first_ffn(R)
        it = lax.broadcasted_iota(jnp.int32, (8, 128), 0)
        flags = jnp.zeros((8, 128), f32)
        for i in range(8):
            flags = jnp.where((it == i) & (count_of(jnp.int32(i)) > 0), 1.0, flags)
        R.cx[:, 768:896] = flags

        @pl.when(c0)
        def _():
            cx_copy(x_peer).start()

        @pl.when(c1)
        def _():
            cx_copy(diag).start()

        ffn_half(R, 0)
        ffn_half(R, 1)
        a1_copy.start()
        a1_own.start()
        own_ct.wait()
        send_ct.wait_recv()
        ln1_back(R)
        row_pass(R)
        dc_copy(0, core_peer).wait_recv()
        first_back(R, R.dcr[...])
        transposes1(R)

        def chip_sums(q):
            on(0, (chip_sum, q))
            on(1, (chip_sum, q))

        for q in range(EARLY):
            if q in (0, 2, 4):
                dvt_block(R, q // 2)
                dvt_block(R, 3 + q // 2)
            elif q >= 6:
                dw1_block(R, q - 6)
            s1_send(q)
            if q > 0:
                chip_sums(q - 1)
        serve(0, 1)
        a1_copy.wait_send()
        a1_own.wait()
        ln0_back(R)
        chip_sums(EARLY - 1)
        serve(1, 2)
        chip_g = rcopy(R.gsum, R.gsr.at[0], S.gs_s.at[0], S.gs_r.at[0], core_peer)
        chip_g.start()
        dctx_pass(R)
        chip_g.wait_recv()
        R.gtot[...] = R.gsum[...] + R.gsr[0]
        gsends = [
            rcopy(R.gtot, R.gsr.at[d], S.gs_s.at[d], S.gs_r.at[d], dp_peers[d - 1])
            for d in range(1, 8)
        ]
        for cp in gsends:
            cp.start()
        transposes2(R)
        serve(2, 3)

        def seg(i):
            attn_block_back(R, i)
            for n, place in enumerate((1, 3, 5, 7)):

                @pl.when(i == place)
                def _(n=n):
                    serve(3 + n, 4 + n)

        loop(8, seg)
        dx_pass(R)
        serve(7, 99)
        gt_own.start()
        for q in range(EARLY, SLOTS):
            dw0_block(R, q - EARLY)
            s1_send(q)
            if q > EARLY:
                chip_sums(q - 1)
        chip_sums(SLOTS - 1)
        gt_copy.start()
        for k in range(2):
            for tick in ticks(late[k], [step_b, step_c, step_d]):
                on(k, *tick)

        for cp in gsends:
            cp.wait()
        total = R.gsum[...] + R.gsr[0]
        for d in range(1, 8):
            total = total + R.gsr[d]
        pair = jnp.where(c0, total[0:2], total[2:4])
        R.gtot[...] = jnp.concatenate([pair] * 4, axis=0)
        gg_own.start()
        send_w.wait_send()
        send_g.wait_send()
        send_v.wait_send()
        each_sent(pos_copy, 2)
        each_sent(cf_copy, 3)
        cx_copy(diag).wait_send()
        chip_g.wait_send()
        gt_copy.wait_send()
        gt_own.wait()
        for q in range(SLOTS):
            s1_copy(q).wait_send()
            for k in range(2):

                @pl.when(c == k)
                def _(q=q, k=k):
                    if PLANE[k][q] == 1:
                        xf_copy(q).wait_send()
                    else:
                        step_end(k, q)

                @pl.when(c == holder(k, q))
                def _(q=q, k=k):
                    arrived(k, q)

        a3_copy(0, diag).wait_recv()
        gp_copy(0, diag).wait_recv()
        gg_own.wait()

    def share(block, flags):
        def both(g, d):
            rows = R.da0.at[pl.ds(pl.multiple_of(256 + g * 16, 16), 16), :]
            flag = R.flags.at[pl.ds(pl.multiple_of(g * 16, 16), 16), :]
            return [
                rcopy(ref, ref, S.gat_s.at[d + 8 * k], S.gat_r.at[d + 8 * k], dp_peers[d - 1])
                for k, ref in enumerate((rows, flag))
            ]

        R.da0[pl.ds(pl.multiple_of(256 + dp * 16, 16), 16), :] = block
        R.flags[pl.ds(pl.multiple_of(dp * 16, 16), 16), :] = flags
        made = [cp for d in range(1, 8) for cp in both(dp, d)]
        for cp in made:
            cp.start()
        for d in range(1, 8):
            for cp in both(dp ^ d, d):
                cp.wait_recv()
        return made

    @pl.when(is1)
    def _():
        send_x.wait_send()
        send_ct.start()

    @pl.when(is1 & c0)
    def _():
        rcopy(w_down, R.v0.at[0:1536], S.vs.at[0], S.vr.at[0], core_peer).start()
        for s in (0, 1, 3):
            rcopy(R.posf, R.posr.at[s], S.pos_s.at[0], S.pos_r.at[s], core_peer).wait_recv()
        R.posr[2] = R.posf[...]
        table = jnp.concatenate([R.posr[s] for s in range(4)], axis=1)
        picks = []
        for r in range(16):
            j = 2 * (r // 8 + 2 * ((r // 4) % 2)) + r % 2
            picks.append(table[j : j + 1, :])
        pos_rows = jnp.concatenate(picks, axis=0)
        for k in range(2):
            rcopy(R.cx, R.cxr.at[k], S.cx_s.at[0], S.cx_r.at[k], x_peer).wait_recv()
        own_w.wait()
        block = jnp.concatenate([R.cxr[0], R.cxr[1]], axis=0)
        made = share(block[:, 0:768], block[:, 768:896])
        cross_attn(R, pos_rows)
        a2 = rcopy(R.a0.at[0:128], R.a0.at[0:128], S.a2_s.at[0], S.a2_r.at[0], core_peer)
        a2.start()
        da2 = rcopy(R.a1.at[0:128], R.cot.at[0:128], S.da2_s.at[0], S.da2_r.at[0], core_peer)
        da2.wait_recv()
        cross_attn_back(R)
        dc_copy(0, x_peer).start()
        dc_copy(1, diag).start()
        rr = lax.broadcasted_iota(jnp.int32, (8, 128), 1)
        jj = lax.broadcasted_iota(jnp.int32, (8, 128), 0)
        seg_of = 2 * (((rr >> 3) & 1) + 2 * ((rr >> 2) & 1)) + (rr & 1)
        pick = jnp.where(seg_of == jj, 1.0, 0.0).astype(bf16)
        dpos = nn(pick, R.da0[128:256, :].astype(bf16))
        for s in range(4):
            R.gps[s] = dpos[:, 192 * s : 192 * s + 192]
        gp_copy(0, x_peer).start()
        gp_copy(1, diag).start()
        gp_copy(3, core_peer).start()
        gp_own = lcopy(R.gps.at[2], o_pos, S.gp_s.at[2])
        gp_own.start()
        R.gtot[...] = R.gsum[...]
        gg_own.start()
        cross_attn_weights(R)
        w_out = lcopy(R.wall.at[1], o_gw, S.ow.at[0])
        w_out.start()
        rcopy(w_down, R.v0.at[0:1536], S.vs.at[0], S.vr.at[0], core_peer).wait_send()
        each_sent(cf_copy, 3)
        for cp in made:
            cp.wait_send()
        a2.wait_send()
        dc_copy(0, x_peer).wait_send()
        dc_copy(1, diag).wait_send()
        gp_copy(0, x_peer).wait_send()
        gp_copy(1, diag).wait_send()
        gp_copy(3, core_peer).wait_send()
        gp_own.wait()
        gg_own.wait()
        w_out.wait()
        a3_copy(0, core_peer).wait_recv()

    @pl.when(is1 & c1)
    def _():
        for s in (0, 1, 2):
            rcopy(R.cfs, R.cfr.at[s], S.cfs_s.at[0], S.cfr_r.at[s], core_peer).wait_recv()
        R.cfr[3] = R.cfs[...]
        block = jnp.concatenate([R.cfr[k, 0:4] for k in (0, 2, 1, 3)], axis=0)
        made = share(block, jnp.zeros((16, 128), f32))
        own_w.wait()
        own_v.wait()
        rcopy(w_down, R.v0.at[0:1536], S.vs.at[0], S.vr.at[0], core_peer).wait_recv()
        rcopy(R.a0.at[0:128], R.a0.at[0:128], S.a2_s.at[0], S.a2_r.at[0], core_peer).wait_recv()
        cross_ffn(R)
        a3_copy(0, diag).start()
        a3_copy(1, x_peer).start()
        a3_copy(2, core_peer).start()
        a3_own = lcopy(own_rows(0, 16), o_a3, S.a3_s.at[3])
        a3_own.start()
        cross_ffn_back(R)
        da2 = rcopy(R.a1.at[0:128], R.cot.at[0:128], S.da2_s.at[0], S.da2_r.at[0], core_peer)
        da2.start()
        R.gtot[...] = R.gsum[...]
        gg_own.start()
        cross_ffn_weights(R)
        dv = rcopy(
            R.gp.at[128:896, 0:1536], o_gv, S.dv_s.at[0], S.dv_r.at[0], core_peer
        )
        dv.start()
        w_out = lcopy(R.wall.at[0], o_gw, S.ow.at[0])
        v_out = lcopy(R.gp.at[128:896, 1536:3072], o_gv, S.ow.at[1])
        w_out.start()
        v_out.start()
        each_sent(pos_copy, 2)
        for cp in made:
            cp.wait_send()
        a3_copy(0, diag).wait_send()
        a3_copy(1, x_peer).wait_send()
        a3_copy(2, core_peer).wait_send()
        a3_own.wait()
        da2.wait_send()
        gg_own.wait()
        dv.wait_send()
        w_out.wait()
        v_out.wait()
        gp_copy(0, core_peer).wait_recv()

    @pl.when(is1)
    def _():
        send_ct.wait_send()
        for k in range(2):

            @pl.when(c == k)
            def _(k=k):
                mine = [q for q in range(SLOTS) if PLANE[k][q] == 1]
                steps = [step_a, step_b, step_c, step_d, step_e]
                for qs in ([q for q in mine if q < EARLY], [q for q in mine if q >= EARLY]):
                    for tick in ticks(qs, steps):
                        for step, q in tick:
                            step(k, q)
                for q in mine:
                    step_end(k, q)

        a1_copy.wait_recv()
        gt_copy.wait_recv()

        @pl.when(c0)
        def _():
            dv = rcopy(
                R.gp.at[128:896, 0:1536], o_gv, S.dv_s.at[0], S.dv_r.at[0], core_peer
            )
            dv.wait_recv()


def fused(counts, tokens, cotan, w_in, w_down, gain, bias, pos):
    hbm = pl.BlockSpec(memory_space=pl.ANY)
    vmem = pl.BlockSpec(memory_space=pltpu.VMEM)
    out = jax.ShapeDtypeStruct
    return pl.pallas_call(
        kernel,
        in_specs=[pl.BlockSpec(memory_space=pltpu.SMEM), hbm, hbm, hbm, hbm, vmem, vmem, vmem],
        out_specs=[hbm] * 8,
        out_shape=[
            out((512, D), bf16),
            out((16, D), f32),
            out((512, D), bf16),
            out((D, FF), bf16),
            out((D, 1536), bf16),
            out((8, D), f32),
            out((8, 192), f32),
            out((D, 4608), bf16),
        ],
        scratch_shapes=[pltpu.VMEM(s, d) for s, d in SCRATCH.values()]
        + [pltpu.SemaphoreType.DMA((n,)) for n in SEMS.values()]
        + [pltpu.SemaphoreType.REGULAR],
        compiler_params=pltpu.CompilerParams(
            collective_id=0, has_side_effects=True, vmem_limit_bytes=64 * 2**20 - 2**17
        ),
        name="layers",
    )(counts, tokens, cotan, w_in, w_down, gain, bias, pos)


def finish(counts, a1, a3, gt, gw, gv):
    def body(cnt, a1_ref, a3_ref, gt_ref, w_ref, v_ref, o_mixed, o_gt, o_w, o_v):
        sec = lax.axis_index("section")
        k = jnp.minimum(pl.program_id(0), 3)
        n = cnt[lax.div(k, 2), 2 * sec + lax.rem(k, 2)]
        row = lax.broadcasted_iota(jnp.int32, (128, 1), 0)
        pick = lax.rem(sec, 2) * 8 + lax.div(sec, 2) * 4 + k
        it = lax.broadcasted_iota(jnp.int32, (16, 1), 0)
        top = jnp.sum(jnp.where(it == pick, a3_ref[...], 0.0), axis=0, keepdims=True)
        both = jnp.where(row == 0, top, a1_ref[...].astype(f32))
        o_mixed[...] = jnp.where(row < n, both, 0.0).astype(bf16)
        o_gt[...] = gt_ref[...].astype(f32)
        o_w[...] = w_ref[...].astype(f32)
        o_v[...] = v_ref[...].astype(f32).T

    out = jax.ShapeDtypeStruct
    rows4 = pl.BlockSpec((128, D), lambda i: (jnp.minimum(i, 3), 0))
    return pl.pallas_call(
        body,
        grid=(12,),
        in_specs=[
            pl.BlockSpec(memory_space=pltpu.SMEM),
            rows4,
            pl.BlockSpec((16, D), lambda i: (0, 0)),
            rows4,
            pl.BlockSpec((64, FF), lambda i: (i, 0)),
            pl.BlockSpec((D, 128), lambda i: (0, i)),
        ],
        out_specs=[
            rows4,
            rows4,
            pl.BlockSpec((64, FF), lambda i: (i, 0)),
            pl.BlockSpec((128, D), lambda i: (i, 0)),
        ],
        out_shape=[
            out((512, D), bf16),
            out((512, D), f32),
            out((D, FF), f32),
            out((1536, D), f32),
        ],
        compiler_params=pltpu.CompilerParams(vmem_limit_bytes=60 * 2**20),
        name="finish",
    )(counts, a1, a3, gt, gw, gv)


def shards(tokens, seg_counts, w_in, w_down, ln_gain, ln_bias, pos_table, cotangent):
    a1, a3, gt, gw, gv, gg, gpos, _ = fused(
        seg_counts,
        tokens.reshape(512, D),
        cotangent.reshape(512, D),
        w_in[0],
        w_down,
        ln_gain,
        ln_bias,
        pos_table,
    )
    size = lax.axis_size("dp")
    if size > 8:
        rings = [[i + 8 * k for k in range(size // 8)] for i in range(8)]
        gw, gv, gg, gpos = lax.psum((gw, gv, gg, gpos), "dp", axis_index_groups=rings)
    mixed, gtok, gw, gv = finish(seg_counts, a1, a3, gt, gw, gv)
    return (
        mixed.reshape(2, 256, D),
        gtok.reshape(2, 256, D),
        gw[None],
        gv,
        gg[0:1],
        gg[1:2],
        gpos,
    )


def solution(mesh):
    return jax.shard_map(
        shards,
        mesh=mesh,
        in_specs=(
            P("dp", "section", None),
            P("dp", None),
            P("section", None, None),
            P("section", None),
            P("section", None),
            P("section", None),
            P(None, "section"),
            P("dp", "section", None),
        ),
        out_specs=(
            P("dp", "section", None),
            P("dp", "section", None),
            P("section", None, None),
            P("section", None),
            P("section", None),
            P("section", None),
            P(None, "section"),
        ),
        check_vma=False,
    )
```

```python
import functools

import jax
import jax.numpy as jnp
from jax import lax
from jax.experimental import pallas as pl
from jax.experimental.pallas import tpu as pltpu
from jax.sharding import PartitionSpec as P

bf16 = jnp.bfloat16
f32 = jnp.float32
D = 768
FF = 3072
ROWS = 1024
WB = 512
CH = 256
SLOTS = 18
EARLY = 12
PLANE = (
    (0, 1, 0, 1, 0, 1, 0, 1, 0, 1, 0, 1, 0, 0, 1, 0, 0, 0),
    (1, 0, 1, 0, 1, 0, 1, 0, 1, 0, 1, 0, 0, 1, 0, 0, 0, 0),
)
ZONES = max(p.count(x) for p in PLANE for x in (0, 1))
MESH = pl.DeviceIdType.MESH


class Refs:
    pass


def nn(a, b):
    return lax.dot_general(a, b, (((1,), (0,)), ((), ())), preferred_element_type=f32)


def nt(a, b):
    return lax.dot_general(a, b, (((1,), (1,)), ((), ())), preferred_element_type=f32)


def tn(a, b):
    return lax.dot_general(a, b, (((0,), (0,)), ((), ())), preferred_element_type=f32)


def cut(start, size):
    return pl.ds(pl.multiple_of(start, size), size)


def loop(n, body):
    def step(i, carry):
        body(i)
        return carry

    lax.fori_loop(0, n, step, 0)


def norm_stats(r):
    mean = jnp.mean(r, axis=-1, keepdims=True)
    cen = r - mean
    var = jnp.mean(cen * cen, axis=-1, keepdims=True)
    rstd = lax.rsqrt(var + 1e-5)
    return cen * rstd, rstd


def norm_back(dy, xhat, rstd, gain):
    dx = dy * gain
    m1 = jnp.mean(dx, axis=-1, keepdims=True)
    m2 = jnp.mean(dx * xhat, axis=-1, keepdims=True)
    return rstd * (dx - m1 - xhat * m2)


def gelu_parts(u):
    phi = 0.5 * lax.erf(u * 0.7071067811865476) + 0.5
    density = jnp.exp2(u * u * -0.7213475204444817 - 1.3257480647361595)
    return u * phi, phi + u * density


def stacked(v):
    low = lax.broadcasted_iota(jnp.int32, v.shape, 1) < 64
    z = jnp.zeros_like(v)
    return jnp.concatenate([jnp.where(low, v, z), jnp.where(low, z, v)], axis=0)


def beside(v):
    low = lax.broadcasted_iota(jnp.int32, (128, 128), 1) < 64
    return jnp.where(low, v[:128], v[128:])


def attn_block(R, i, vis):
    rs = cut(i * 128, 128)
    for j in range(6):
        q2 = R.qkv[rs, 128 * j : 128 * j + 128]
        k2 = R.qkv[rs, 768 + 128 * j : 768 + 128 * j + 128]
        v2 = R.qkv[rs, 1536 + 128 * j : 1536 + 128 * j + 128]
        s = jnp.where(vis, nt(stacked(q2), k2) * 0.125, -1e30)
        s = jnp.exp(s - jnp.max(s, axis=-1, keepdims=True))
        pr = (s / jnp.sum(s, axis=-1, keepdims=True)).astype(bf16)
        R.p[cut(i * 1536 + 256 * j, 256), :] = pr
        R.ctx[rs, 128 * j : 128 * j + 128] = beside(nn(pr, v2)).astype(bf16)


def attn_block_back(R, i):
    rs = cut(i * 128, 128)
    for j in range(6):
        sq, sk, sv = [slice(b + 128 * j, b + 128 * j + 128) for b in (0, 768, 1536)]
        q2 = R.qkv[rs, sq]
        k2 = R.qkv[rs, sk]
        v2 = R.qkv[rs, sv]
        qs = stacked(q2)
        dos = stacked(R.xh1[rs, sq])
        pr = R.p[cut(i * 1536 + 256 * j, 256), :]
        pf = pr.astype(f32)
        dp = nt(dos, v2)
        ds = (pf * (dp - jnp.sum(dp * pf, axis=-1, keepdims=True))).astype(bf16)
        R.qkv[rs, sv] = tn(pr, dos).astype(bf16)
        R.qkv[rs, sq] = beside(nn(ds, k2) * 0.125).astype(bf16)
        R.qkv[rs, sk] = (tn(ds, qs) * 0.125).astype(bf16)


def qkv_rows(R, r0, n):
    def body(k):
        cs = cut(k * 768, 768)
        R.qkv[pl.ds(r0, n), cs] = nn(R.x[pl.ds(r0, n), :], R.wall[0, :, cs]).astype(bf16)

    loop(3, body)


def attn_rows(R, r0, n):
    key = lax.broadcasted_iota(jnp.int32, (256, 128), 1)

    def seg(k):
        i = r0 // 128 + k
        attn_block(R, i, key < jnp.maximum(R.count_of(i), 1))

    loop(n // 128, seg)
    rs = pl.ds(r0, n)
    R.da0[rs, :] = nt(R.ctx[rs, :], R.wall[0, :, 2304:])

    def norm(k):
        rs = cut(r0 + k * 128, 128)
        xh, rstd = norm_stats(R.x[rs, :].astype(f32) + R.da0[rs, :])
        R.xh0[rs, :] = xh.astype(bf16)
        R.rs[rs, 0:1] = rstd
        R.a0[rs, :] = (xh * R.gains[0, 0:1, :] + R.gains[0, 1:2, :]).astype(bf16)

    loop(n // 128, norm)


def ffn_up(R, h):
    rs = pl.ds(h * 512, 512)

    def up(n):
        cs = cut(n * WB, WB)
        mm, gg = gelu_parts(nn(R.a0[rs, :], R.wall[1, :, cs]))
        R.m[rs, cs] = mm.astype(bf16)
        R.gp[rs, cs] = gg.astype(bf16)

    loop(6, up)


def ffn_down(R, h):
    rs = pl.ds(h * 512, 512)
    R.da0[rs, :] = nn(R.m[rs, :], R.v0[...])

    def norm(k):
        rs = cut(h * 512 + k * 128, 128)
        xh, rstd = norm_stats(R.a0[rs, :].astype(f32) + R.da0[rs, :])
        R.xh1[rs, :] = xh.astype(bf16)
        R.rs[rs, 1:2] = rstd
        R.a1[rs, :] = (xh * R.gains[1, 0:1, :] + R.gains[1, 1:2, :]).astype(bf16)

    loop(4, norm)


def pad16(v):
    return jnp.concatenate([v, jnp.zeros_like(v)], axis=0).astype(bf16)


def first_ffn(R):
    rows = [R.a0[i * 128 : i * 128 + 16, :].astype(f32)[0:1, :] for i in range(8)]
    af = jnp.concatenate(rows, axis=0)
    a16 = pad16(af)

    def up(n):
        cs = cut(n * 1536, 1536)
        mm, gg = gelu_parts(nn(a16, R.wall[1, :, cs]))
        R.fm[:, cs] = mm.astype(bf16)
        R.fg[:, cs] = gg.astype(bf16)

    loop(2, up)
    xh, rstd = norm_stats(af + nn(R.fm[...], R.v0[...])[0:8])
    R.fxh[...] = xh
    R.frs[...] = rstd
    return (xh * R.gains[1, 0:1, :] + R.gains[1, 1:2, :]).astype(bf16).astype(f32)


def ln1_back(R):
    row = lax.broadcasted_iota(jnp.int32, (128, 1), 0)

    def body(i):
        rs = cut(i * 128, 128)
        live = (row < R.count_of(i)) & (row > 0)
        dy = jnp.where(live, R.cot[rs, :].astype(f32), 0.0)
        xh = R.xh1[rs, :].astype(f32)
        R.gsum[2:3, :] += jnp.sum(dy * xh, axis=0, keepdims=True)
        R.gsum[3:4, :] += jnp.sum(dy, axis=0, keepdims=True)
        dr = norm_back(dy, xh, R.rs[rs, 1:2], R.gains[1, 0:1, :])
        R.da0[rs, :] = dr
        R.cot[rs, :] = dr.astype(bf16)

    loop(8, body)


def row_pass(R):
    def hid(n):
        cs = cut(n * WB, WB)
        dm = nt(R.cot[...], R.v0[cs, :])
        R.gp[:, cs] = (dm * R.gp[:, cs].astype(f32)).astype(bf16)

    loop(6, hid)

    def back(k):
        rs = cut(k * 512, 512)
        R.da0[rs, :] += nt(R.gp[rs, :], R.wall[1])

    loop(2, back)


def put_first(ref, i, rowval):
    rs = slice(i * 128, i * 128 + 16)
    blk = ref[rs, :]
    it = lax.broadcasted_iota(jnp.int32, blk.shape, 0)
    ref[rs, :] = jnp.where(it == 0, rowval.astype(f32), blk.astype(f32)).astype(blk.dtype)


def first_back(R, dc):
    xh = R.fxh[...]
    R.gsum[2:3, :] += jnp.sum(dc * xh, axis=0, keepdims=True)
    R.gsum[3:4, :] += jnp.sum(dc, axis=0, keepdims=True)
    dr = norm_back(dc, xh, R.frs[...], R.gains[1, 0:1, :])
    dz = pad16(dr)

    def hid(n):
        cs = cut(n * 1536, 1536)
        R.fdu[:, cs] = (nt(dz, R.v0[cs, :]) * R.fg[:, cs].astype(f32)).astype(bf16)

    loop(2, hid)
    da = dr + nt(R.fdu[...], R.wall[1])[0:8]
    for i in range(8):
        put_first(R.cot, i, dr[i : i + 1, :].astype(bf16))
        put_first(R.gp, i, R.fdu[...].astype(f32)[i : i + 1, :])
        put_first(R.da0, i, da[i : i + 1, :])


def transposes1(R):
    for b, ref in ((0, R.a0), (1536, R.cot)):

        def body(k, b=b, ref=ref):
            R.v0[b : b + 768, cut(k * 256, 256)] = ref[cut(k * 256, 256), :].T

        loop(3, body)
        R.v0[b + 768 : b + 1536, 0:256] = ref[768:1024, :].T


def tdot(R, b, rhs, cs):
    head = nn(R.v0[b : b + 768, :], rhs[0:768, cs])
    return head + nn(R.v0[b + 768 : b + 1536, 0:256], rhs[768:1024, cs])


def dvt_block(R, n):
    cs = pl.ds(n * WB, WB)
    R.m[0:768, cs] = tdot(R, 1536, R.m, cs).astype(bf16)


def dw1_block(R, n):
    cs = pl.ds(n * WB, WB)
    R.wall[1, :, cs] = tdot(R, 0, R.gp, cs).astype(bf16)


def ln0_back(R):
    def body(i):
        rs = cut(i * 128, 128)
        dy = R.da0[rs, :].astype(bf16).astype(f32)
        xh = R.xh0[rs, :].astype(f32)
        R.gsum[0:1, :] += jnp.sum(dy * xh, axis=0, keepdims=True)
        R.gsum[1:2, :] += jnp.sum(dy, axis=0, keepdims=True)
        dr = norm_back(dy, xh, R.rs[rs, 0:1], R.gains[0, 0:1, :])
        R.da0[rs, :] = dr
        R.a1[rs, :] = dr.astype(bf16)

    loop(8, body)


def dctx_pass(R):
    def body(k):
        rs = cut(k * 512, 512)
        R.xh1[rs, :] = nn(R.a1[rs, :], R.wall[0, :, 2304:]).astype(bf16)

    loop(2, body)


def transposes2(R):
    for c0, ref in ((0, R.x), (1024, R.a1)):

        def body(k, c0=c0, ref=ref):
            R.gp[0:768, cut(c0 + k * 256, 256)] = ref[cut(k * 256, 256), :].T

        loop(4, body)


def dx_pass(R):
    def body(k):
        rs = cut(k * 512, 512)
        R.cot[rs, :] = (R.da0[rs, :] + nt(R.qkv[rs, :], R.wall[0, :, :2304])).astype(bf16)

    loop(2, body)


def dw0_block(R, n):
    edges = [n * WB, 2304, (n + 1) * WB] if n == 4 else [n * WB, (n + 1) * WB]
    for lo, hi in zip(edges, edges[1:]):
        if hi <= 2304:
            out = nn(R.gp[0:768, 0:1024], R.qkv[:, lo:hi])
        else:
            out = nn(R.gp[0:768, 1024:2048], R.ctx[:, lo - 2304 : hi - 2304])
        R.wall[0, :, lo:hi] = out.astype(bf16)


def cross_attn(R, pos_rows):
    cp = (R.da0[256:384, :] + jnp.concatenate([pos_rows] * 8, axis=0)).astype(bf16)
    R.x[0:128, :] = cp
    live = R.flags[...].T
    row = lax.broadcasted_iota(jnp.int32, (128, 128), 0)
    col = lax.broadcasted_iota(jnp.int32, (128, 128), 1)
    same = (row & 0x72) == (col & 0x72)
    vis = same & (live > 0.5)
    R.da0[384:512, 0:128] = jnp.where(vis, 1.0, 0.0)

    def qkv(n):
        cs = cut(n * 768, 768)
        R.qkv[0:128, cs] = nn(R.x[0:128, :], R.wall[1, :, cs]).astype(bf16)

    loop(3, qkv)
    mask = R.da0[384:512, 0:128] > 0.5
    attn_block(R, 0, jnp.concatenate([mask, mask], axis=0))
    att = nt(R.ctx[0:128, :], R.wall[1, :, 2304:])
    xh, rstd = norm_stats(R.x[0:128, :].astype(f32) + att)
    R.da0[0:128, :] = xh
    R.rs[0:128, 0:1] = rstd
    R.a0[0:128, :] = (xh * R.gains[0, 0:1, :] + R.gains[0, 1:2, :]).astype(bf16)


def cross_attn_back(R):
    dy = R.cot[0:128, :].astype(f32)
    xh = R.da0[0:128, :]
    R.gsum[0:1, :] = jnp.sum(dy * xh, axis=0, keepdims=True)
    R.gsum[1:2, :] = jnp.sum(dy, axis=0, keepdims=True)
    dr = norm_back(dy, xh, R.rs[0:128, 0:1], R.gains[0, 0:1, :])
    R.da0[0:128, :] = dr
    R.a1[0:128, :] = dr.astype(bf16)
    R.xh1[0:128, :] = nn(R.a1[0:128, :], R.wall[1, :, 2304:]).astype(bf16)
    attn_block_back(R, 0)
    dcp = R.da0[0:128, :] + nt(R.qkv[0:128, :], R.wall[1, :, :2304])
    R.da0[128:256, :] = dcp.astype(bf16).astype(f32)


def cross_attn_weights(R):
    R.gp[128:896, 0:128] = R.x[0:128, :].T
    R.gp[128:896, 128:256] = R.a1[0:128, :].T

    def one(n):
        cs = cut(n * 256, 256)
        R.wall[1, :, cs] = nn(R.gp[128:896, 0:128], R.qkv[0:128, cs]).astype(bf16)

    loop(9, one)

    def two(n):
        c2 = cut(n * 256, 256)
        cs = cut(2304 + n * 256, 256)
        R.wall[1, :, cs] = nn(R.gp[128:896, 128:256], R.ctx[0:128, c2]).astype(bf16)

    loop(3, two)


def cross_ffn(R):
    def up(n):
        cs = cut(n * 768, 768)
        mm, gg = gelu_parts(nn(R.a0[0:128, :], R.wall[0, :, cs]))
        R.gp[896:1024, cs] = mm.astype(bf16)
        R.gp[0:128, cs] = gg.astype(bf16)

    loop(4, up)
    xh, rstd = norm_stats(R.a0[0:128, :].astype(f32) + nn(R.gp[896:1024, :], R.v0[...]))
    R.da0[0:128, :] = xh
    R.rs[0:128, 0:1] = rstd
    R.da0[128:256, :] = xh * R.gains[0, 0:1, :] + R.gains[0, 1:2, :]


def cross_ffn_back(R):
    dy = R.da0[256:384, :]
    xh = R.da0[0:128, :]
    R.gsum[0:1, :] = jnp.sum(dy * xh, axis=0, keepdims=True)
    R.gsum[1:2, :] = jnp.sum(dy, axis=0, keepdims=True)
    dr = norm_back(dy, xh, R.rs[0:128, 0:1], R.gains[0, 0:1, :])
    R.da0[0:128, :] = dr
    R.cot[0:128, :] = dr.astype(bf16)

    def hid(n):
        cs = cut(n * 768, 768)
        dm = nt(R.cot[0:128, :], R.v0[cs, :])
        R.gp[0:128, cs] = (dm * R.gp[0:128, cs].astype(f32)).astype(bf16)

    loop(4, hid)
    R.a1[0:128, :] = (R.da0[0:128, :] + nt(R.gp[0:128, :], R.wall[0])).astype(bf16)


def cross_ffn_weights(R):
    R.qkv[0:768, 0:128] = R.a0[0:128, :].T
    R.qkv[0:768, 128:256] = R.cot[0:128, :].T

    def body(n):
        cs = cut(n * 256, 256)
        R.wall[0, :, cs] = nn(R.qkv[0:768, 0:128], R.gp[0:128, cs]).astype(bf16)
        R.gp[128:896, cs] = nn(R.qkv[0:768, 128:256], R.gp[896:1024, cs]).astype(bf16)

    loop(12, body)


SCRATCH = dict(
    wall=((2, D, FF), bf16),
    v0=((FF, D), bf16),
    x=((ROWS, D), bf16),
    qkv=((ROWS, 2304), bf16),
    p=((12288, 128), bf16),
    ctx=((ROWS, D), bf16),
    xh0=((ROWS, D), bf16),
    rs=((ROWS, 2), f32),
    a0=((ROWS, D), bf16),
    m=((ROWS, FF), bf16),
    gp=((ROWS, FF), bf16),
    xh1=((ROWS, D), bf16),
    a1=((ROWS, D), bf16),
    cot=((ROWS, D), bf16),
    da0=((ROWS, D), f32),
    gains=((2, 8, D), f32),
    gsum=((8, D), f32),
    gtot=((8, D), f32),
    gsr=((8, 8, D), f32),
    fm=((16, FF), bf16),
    fg=((16, FF), bf16),
    fdu=((16, FF), bf16),
    fxh=((8, D), f32),
    frs=((8, 1), f32),
    flags=((128, 128), f32),
    cx=((8, D), f32),
    cxr=((2, 8, D), f32),
    ctmp=((4, 16, D), bf16),
    cfs=((8, D), f32),
    cfr=((4, 8, D), f32),
    dcr=((8, D), f32),
    posf=((8, 192), f32),
    posr=((4, 8, 192), f32),
    gps=((4, 8, 192), f32),
    rx=((6, D, CH), bf16),
    yb=((ZONES, 384, CH), bf16),
    zb=((ZONES, 2, 384, CH), bf16),
)
SEMS = dict(
    load=16, ctmp=4, ws=2, wr=2, vs=1, vr=1, gns=1, gnr=1, tks=3, tkr=3, pos_s=1, pos_r=4, cfs_s=1, cfr_r=4,
    cx_s=1, cx_r=2, gat_s=16, gat_r=16, a2_s=1, a2_r=1, a3_s=4, a3_r=1, da2_s=1, da2_r=1, dc_s=2, dc_r=1,
    gp_s=4, gp_r=1, dv_s=1, dv_r=1, a1_s=1, a1_r=1, a1_l=1, gt_s=1, gt_r=1, gt_l=1, gs_s=8, gs_r=8, og=1, ow=2,
    s1_s=18, s1_r=18, xf_s=18, xf_r=18, y_s=18, y_r=18, z1_s=18, z1_r=18, z2_s=18, z2_r=18, z3_s=18, z3_r=18,
    h_s=18, h_r=36, b1_s=18, b1_r=36, b2_s=18, b2_r=36, out_s=18, out_r=36, hx_r=18,
)


def kernel(
    counts, tokens, cotan, w_in, w_down, gain, bias, pos,
    o_a1, o_a3, o_gt, o_gw, o_gv, o_gg, o_pos, o_pass, *scratch,
):
    R, S = Refs(), Refs()
    for name, ref in zip(SCRATCH, scratch):
        setattr(R, name, ref)
    free = scratch[-1]
    for name, ref in zip(SEMS, scratch[len(SCRATCH) :]):
        setattr(S, name, ref)

    group = lax.axis_index("dp")
    dp = lax.rem(group, 8)
    sec = lax.axis_index("section")
    z, y = lax.div(dp, 2), lax.rem(dp, 2)
    xx, c = lax.div(sec, 2), lax.rem(sec, 2)

    def at(px, pc):
        return {"section": px * 2 + pc}

    def at_dp(pz, py):
        return {"dp": group - dp + pz * 2 + py}

    core_peer, x_peer, diag = at(xx, 1 - c), at(1 - xx, c), at(1 - xx, 1 - c)
    y_peer = at_dp(z, 1 - y)
    z_near, z_over = at_dp(z ^ 1, y), at_dp(z ^ 3, y)
    middle = (z == 1) | (z == 2)
    dp_peers = [{"dp": group - dp + (dp ^ d)} for d in range(1, 8)]

    def rcopy(src, dst, ss, rs, dev):
        return pltpu.make_async_remote_copy(
            src_ref=src, dst_ref=dst, send_sem=ss, recv_sem=rs, device_id=dev, device_id_type=MESH
        )

    def lcopy(src, dst, sem):
        return pltpu.make_async_copy(src, dst, sem)

    def count_of(i):
        return counts[lax.rem(lax.div(i, 2), 2), 2 * (c + 2 * lax.div(i, 4)) + lax.rem(i, 2)]

    R.count_of = count_of
    is0, is1 = xx == 0, xx == 1
    c0, c1 = c == 0, c == 1

    barrier = pltpu.get_barrier_semaphore()
    partners = [core_peer, x_peer, diag] + dp_peers
    for dev in partners:
        pl.semaphore_signal(barrier, inc=1, device_id=dev, device_id_type=MESH)

    own_w = lcopy(w_in, R.wall.at[jnp.where(is0, c, 1 - c)], S.load.at[0])
    own_v = lcopy(w_down, R.v0.at[cut(c * 1536, 1536)], S.load.at[1])
    own_x = lcopy(tokens, R.x.at[0:512], S.load.at[2])
    own_ct = lcopy(cotan, R.cot.at[0:512], S.load.at[3])
    heads = [lcopy(cotan.at[pl.ds(k * 128, 16)], R.ctmp.at[k], S.ctmp.at[k]) for k in range(4)]

    @pl.when(is0)
    def _():
        own_x.start()

    own_w.start()

    @pl.when(is0 | c1)
    def _():
        own_v.start()

    for cp in heads:
        cp.start()
    R.gsum[...] = jnp.zeros_like(R.gsum)
    gslot = jnp.where(is0, c, 0)
    R.gains[gslot, 0:1, :] = gain[...].astype(f32)
    R.gains[gslot, 1:2, :] = bias[...].astype(f32)
    R.posf[...] = pos[...].astype(f32)
    for cp in heads:
        cp.wait()
    first_rows = []
    for k in range(4):
        n = counts[k // 2, 2 * sec + k % 2]
        r = R.ctmp[k].astype(f32)[0:1, :]
        first_rows.append(jnp.where(n > 0, r, 0.0))
    R.cfs[...] = jnp.concatenate(first_rows + first_rows, axis=0)

    pl.semaphore_wait(barrier, len(partners))

    send_w = rcopy(w_in, R.wall.at[c], S.ws.at[0], S.wr.at[0], core_peer)
    send_v = rcopy(w_down, R.v0.at[cut(c * 1536, 1536)], S.vs.at[0], S.vr.at[0], core_peer)
    send_g = rcopy(R.gains.at[c], R.gains.at[c], S.gns.at[0], S.gnr.at[0], core_peer)
    send_x = [
        rcopy(
            tokens.at[256 * k : 256 * k + 256],
            R.x.at[512 + 256 * k : 768 + 256 * k],
            S.tks.at[2 * k],
            S.tkr.at[2 * k],
            x_peer,
        )
        for k in range(2)
    ]
    send_ct = rcopy(cotan, R.cot.at[512:1024], S.tks.at[1], S.tkr.at[1], x_peer)
    other_w = rcopy(w_in, R.wall.at[1 - c], S.ws.at[0], S.wr.at[0], core_peer)
    other_v = rcopy(w_down, R.v0.at[cut((1 - c) * 1536, 1536)], S.vs.at[0], S.vr.at[0], core_peer)
    other_g = rcopy(R.gains.at[1 - c], R.gains.at[1 - c], S.gns.at[0], S.gnr.at[0], core_peer)

    def pos_copy(dev):
        return rcopy(R.posf, R.posr.at[sec], S.pos_s.at[0], S.pos_r.at[sec], dev)

    def cf_copy(dev):
        return rcopy(R.cfs, R.cfr.at[sec], S.cfs_s.at[0], S.cfr_r.at[sec], dev)

    def each_to(make, target):
        by = {2: (x_peer, diag, core_peer), 3: (diag, x_peer, core_peer)}[target]
        for s, dev in zip((0, 1, 5 - target), by):

            @pl.when(sec == s)
            def _(dev=dev):
                make(dev).start()

    def each_sent(make, target):
        @pl.when(sec != target)
        def _():
            make(core_peer).wait_send()

    @pl.when(is0)
    def _():
        send_w.start()
        send_g.start()
        send_v.start()

    @pl.when(is1)
    def _():
        send_x[0].start()
        send_x[1].start()

    each_to(pos_copy, 2)
    each_to(cf_copy, 3)

    def block_of(own, q):
        return 2 * (q % 6) + (own if q < EARLY else 1 - own)

    def slot(own, q, index):
        if q < 6:
            return R.m.at[0:768, pl.ds(pl.multiple_of(own * 1536 + q * CH, CH), CH)]
        return R.wall.at[index, :, pl.ds(pl.multiple_of(block_of(own, q) * CH, CH), CH)]

    def part_of(own, q):
        return slot(own, q, jnp.where(is0, 1 if q < EARLY else 0, c))

    def holder(k, q):
        return k if q < 6 else (1 if q < EARLY else 0)

    def add_rows(dst, r0, terms, n, step):
        def body(k):
            rs = pl.ds(pl.multiple_of(r0 + k * step, 32), step)
            total = dst[rs, :].astype(f32)
            for ref in terms:
                total = total + ref[pl.ds(pl.multiple_of(k * step, 32), step), :].astype(f32)
            dst[rs, :] = total.astype(bf16)

        loop(n // step, body)

    def s1_copy(q):
        return rcopy(
            part_of(1 - c, q), R.rx.at[q % 6], S.s1_s.at[q], S.s1_r.at[q], core_peer
        )

    def s1_send(q):
        if q >= 6:
            pl.semaphore_wait(free, 1)
        s1_copy(q).start()

    def xf_copy(q):
        return rcopy(part_of(c, q), slot(c, q, c), S.xf_s.at[q], S.xf_r.at[q], x_peer)

    def spot(k, q):
        return PLANE[k][:q].count(PLANE[k][q])

    def y_copy(k, q):
        half = part_of(c, q).at[pl.ds(pl.multiple_of((1 - y) * 384, 384), 384), :]
        return rcopy(half, R.yb.at[spot(k, q)], S.y_s.at[q], S.y_r.at[q], y_peer)

    def half_of(ref, h):
        return ref.at[pl.ds(pl.multiple_of(h * 384, 384), 384), :]

    def z1_copy(k, q):
        zone = R.zb.at[spot(k, q), 0]
        return rcopy(half_of(part_of(c, q), y), zone, S.z1_s.at[q], S.z1_r.at[q], z_near)

    def z2_copy(k, q):
        zone = R.zb.at[spot(k, q), 1]
        return rcopy(half_of(part_of(c, q), y), zone, S.z2_s.at[q], S.z2_r.at[q], z_over)

    def z3_copy(k, q):
        zone = R.zb.at[spot(k, q), 0]
        return rcopy(zone, zone, S.z3_s.at[q], S.z3_r.at[q], z_near)

    def final(k, q):
        if q < 6:
            return o_gv.at[:, pl.ds(q * CH, CH)]
        return o_gw.at[:, pl.ds(block_of(k, q) * CH, CH)]

    def passing(q):
        return o_pass.at[:, pl.ds(q * CH, CH)]

    def h_copy(k, q):
        zone = R.zb.at[spot(k, q), 0]
        if PLANE[k][q] == 1:
            return rcopy(zone, half_of(passing(q), y), S.h_s.at[q], S.hx_r.at[q], y_peer)
        there = {**y_peer, **at(xx, holder(k, q))}
        return rcopy(zone, half_of(final(k, q), y), S.h_s.at[q], S.h_r.at[SLOTS * k + q], there)

    def out_copy(k, q):
        zone, there = R.zb.at[spot(k, q), 0], half_of(final(k, q), y)
        if holder(k, q) == k:
            return lcopy(zone, there, S.out_s.at[q])
        return rcopy(zone, there, S.out_s.at[q], S.out_r.at[SLOTS * k + q], core_peer)

    def b1_copy(k, q):
        zone = R.zb.at[spot(k, q), 0]
        there = at(1 - xx, holder(k, q))
        return rcopy(zone, half_of(final(k, q), y), S.b1_s.at[q], S.b1_r.at[SLOTS * k + q], there)

    def b2_copy(k, q):
        src, there = half_of(passing(q), 1 - y), at(1 - xx, holder(k, q))
        return rcopy(src, half_of(final(k, q), 1 - y), S.b2_s.at[q], S.b2_r.at[SLOTS * k + q], there)

    def on(k, *steps):
        @pl.when(c == k)
        def _():
            for step, q in steps:
                step(k, q)

    def chip_sum(k, q):
        s1_copy(q).wait_recv()
        add_rows(part_of(c, q), 0, [R.rx.at[q % 6]], 768, 192)
        if q < SLOTS - 6:
            pl.semaphore_signal(free, inc=1, device_id=core_peer, device_id_type=MESH)
        if PLANE[k][q] == 0:
            y_copy(k, q).start()
        else:
            xf_copy(q).start()

    def step_a(k, q):
        xf_copy(q).wait_recv()
        y_copy(k, q).start()

    def step_b(k, q):
        y_copy(k, q).wait()
        add_rows(part_of(c, q), y * 384, [R.yb.at[spot(k, q)]], 384, 192)

        @pl.when(jnp.logical_not(middle))
        def _():
            z1_copy(k, q).start()

    def step_c(k, q):
        @pl.when(middle)
        def _():
            z1_copy(k, q).wait_recv()
            add_rows(part_of(c, q), y * 384, [R.zb.at[spot(k, q), 0]], 384, 192)
            z2_copy(k, q).start()

    def step_d(k, q):
        n = spot(k, q)

        @pl.when(middle)
        def _():
            z2_copy(k, q).wait()
            mine = half_of(part_of(c, q), y)

            def body(r):
                rs = cut(r * 192, 192)
                total = mine[rs, :].astype(f32) + R.zb[n, 1, rs, :].astype(f32)
                R.zb[n, 0, rs, :] = total.astype(bf16)

            loop(2, body)
            z3_copy(k, q).start()

        @pl.when(jnp.logical_not(middle))
        def _():
            z1_copy(k, q).wait_send()
            z3_copy(k, q).wait_recv()

        h_copy(k, q).start()
        if PLANE[k][q] == 0:
            out_copy(k, q).start()
        else:
            b1_copy(k, q).start()

    def step_e(k, q):
        h_copy(k, q).wait_recv()
        b2_copy(k, q).start()

    def step_end(k, q):
        @pl.when(middle)
        def _():
            z3_copy(k, q).wait_send()

        h_copy(k, q).wait_send()
        if PLANE[k][q] == 1:
            b1_copy(k, q).wait_send()
            b2_copy(k, q).wait_send()
        elif holder(k, q) == k:
            out_copy(k, q).wait()
        else:
            out_copy(k, q).wait_send()

    def arrived(k, q):
        if PLANE[k][q] == 1:
            b1_copy(k, q).wait_recv()
            b2_copy(k, q).wait_recv()
            return
        h_copy(k, q).wait_recv()
        if holder(k, q) != k:
            out_copy(k, q).wait_recv()

    def ticks(qs, steps):
        made = []
        for t in range(len(qs) + len(steps) - 1):
            made.append([(f, qs[t - n]) for n, f in enumerate(steps) if 0 <= t - n < len(qs)])
        return made

    early = [[q for q in range(EARLY) if PLANE[k][q] == 0] for k in range(2)]
    late = [[q for q in range(EARLY, SLOTS) if PLANE[k][q] == 0] for k in range(2)]
    planned = [ticks(early[k], [step_b, step_c, step_d]) for k in range(2)]

    def serve(first, last):
        for k in range(2):
            for tick in planned[k][first:last]:
                on(k, *tick)

    def cx_copy(dev):
        return rcopy(R.cx, R.cxr.at[c], S.cx_s.at[0], S.cx_r.at[c], dev)

    def own_rows(r0, n):
        return R.da0.at[pl.ds(pl.multiple_of(128 + dp * 16 + r0, 8), n), :]

    def dc_copy(k, dev):
        return rcopy(own_rows(k * 8, 8), R.dcr, S.dc_s.at[k], S.dc_r.at[0], dev)

    def a3_copy(k, dev):
        return rcopy(own_rows(0, 16), o_a3, S.a3_s.at[k], S.a3_r.at[0], dev)

    def gp_copy(s, dev):
        return rcopy(R.gps.at[s], o_pos, S.gp_s.at[s], S.gp_r.at[0], dev)

    a1_copy = rcopy(R.a1.at[512:1024], o_a1, S.a1_s.at[0], S.a1_r.at[0], x_peer)
    gt_copy = rcopy(R.cot.at[512:1024], o_gt, S.gt_s.at[0], S.gt_r.at[0], x_peer)
    a1_own = lcopy(R.a1.at[0:512], o_a1, S.a1_l.at[0])
    gt_own = lcopy(R.cot.at[0:512], o_gt, S.gt_l.at[0])
    gg_own = lcopy(R.gtot, o_gg, S.og.at[0])

    @pl.when(is0)
    def _():
        own_x.wait()
        own_ct.start()

        @pl.when(c0)
        def _():
            own_w.wait()

        @pl.when(c1)
        def _():
            other_w.wait_recv()

        other_g.wait_recv()
        qkv_rows(R, 0, 512)
        attn_rows(R, 0, 512)
        send_x[0].wait_recv()
        qkv_rows(R, 512, 256)
        attn_rows(R, 512, 256)

        @pl.when(c1)
        def _():
            own_w.wait()

        @pl.when(c0)
        def _():
            other_w.wait_recv()

        ffn_up(R, 0)
        send_x[1].wait_recv()
        qkv_rows(R, 768, 256)
        attn_rows(R, 768, 256)
        own_v.wait()
        other_v.wait_recv()
        R.cx[...] = first_ffn(R)

        @pl.when(c0)
        def _():
            cx_copy(x_peer).start()

        @pl.when(c1)
        def _():
            cx_copy(diag).start()

        ffn_down(R, 0)
        ffn_up(R, 1)
        ffn_down(R, 1)
        a1_copy.start()
        a1_own.start()
        own_ct.wait()
        send_ct.wait_recv()
        ln1_back(R)
        row_pass(R)
        dc_copy(0, core_peer).wait_recv()
        first_back(R, R.dcr[...])
        transposes1(R)

        def chip_sums(q):
            on(0, (chip_sum, q))
            on(1, (chip_sum, q))

        for q in range(EARLY):
            if q in (0, 2, 4):
                dvt_block(R, q // 2)
                dvt_block(R, 3 + q // 2)
            elif q >= 6:
                dw1_block(R, q - 6)
            s1_send(q)
            if q > 0:
                chip_sums(q - 1)
        serve(0, 1)
        a1_copy.wait_send()
        a1_own.wait()
        ln0_back(R)
        chip_sums(EARLY - 1)
        serve(1, 2)
        chip_g = rcopy(R.gsum, R.gsr.at[0], S.gs_s.at[0], S.gs_r.at[0], core_peer)
        chip_g.start()
        dctx_pass(R)
        chip_g.wait_recv()
        R.gtot[...] = R.gsum[...] + R.gsr[0]
        gsends = [
            rcopy(R.gtot, R.gsr.at[d], S.gs_s.at[d], S.gs_r.at[d], dp_peers[d - 1])
            for d in range(1, 8)
        ]
        for cp in gsends:
            cp.start()
        transposes2(R)
        serve(2, 3)

        def seg(i):
            attn_block_back(R, i)
            for n, place in enumerate((1, 3, 5, 7)):

                @pl.when(i == place)
                def _(n=n):
                    serve(3 + n, 4 + n)

        loop(8, seg)
        dx_pass(R)
        serve(7, 99)
        gt_own.start()
        for q in range(EARLY, SLOTS):
            dw0_block(R, q - EARLY)
            s1_send(q)
            if q > EARLY:
                chip_sums(q - 1)
        chip_sums(SLOTS - 1)
        gt_copy.start()
        for k in range(2):
            for tick in ticks(late[k], [step_b, step_c, step_d]):
                on(k, *tick)

        for cp in gsends:
            cp.wait()
        total = R.gsum[...] + R.gsr[0]
        for d in range(1, 8):
            total = total + R.gsr[d]
        pair = jnp.where(c0, total[0:2], total[2:4])
        R.gtot[...] = jnp.concatenate([pair] * 4, axis=0)
        gg_own.start()
        send_w.wait_send()
        send_g.wait_send()
        send_v.wait_send()
        each_sent(pos_copy, 2)
        each_sent(cf_copy, 3)
        cx_copy(diag).wait_send()
        chip_g.wait_send()
        gt_copy.wait_send()
        gt_own.wait()
        for q in range(SLOTS):
            s1_copy(q).wait_send()
            for k in range(2):

                @pl.when(c == k)
                def _(q=q, k=k):
                    if PLANE[k][q] == 1:
                        xf_copy(q).wait_send()
                    else:
                        step_end(k, q)

                @pl.when(c == holder(k, q))
                def _(q=q, k=k):
                    arrived(k, q)

        a3_copy(0, diag).wait_recv()
        gp_copy(0, diag).wait_recv()
        gg_own.wait()

    def to_groups(part, first):
        def one(g, d):
            return rcopy(part(g), part(g), S.gat_s.at[first + d], S.gat_r.at[first + d], dp_peers[d - 1])

        return [one(dp, d) for d in range(1, 8)], [one(dp ^ d, d) for d in range(1, 8)]

    def rows_of(g):
        return R.da0.at[pl.ds(pl.multiple_of(256 + g * 16, 16), 16), :]

    def flags_of(g):
        return R.flags.at[pl.ds(pl.multiple_of(g * 16, 16), 16), :]

    def share(block):
        rows_of(dp)[...] = block
        sent, awaited = to_groups(rows_of, 0)
        for cp in sent:
            cp.start()
        for cp in awaited:
            cp.wait_recv()
        return sent

    @pl.when(is1)
    def _():
        send_x[0].wait_send()
        send_x[1].wait_send()
        send_ct.start()

    @pl.when(is1 & c0)
    def _():
        it = lax.broadcasted_iota(jnp.int32, (16, 128), 0)
        flags = jnp.zeros((16, 128), f32)
        for r in range(16):
            j = 2 * (r // 8 + 2 * ((r // 4) % 2)) + r % 2
            flags = jnp.where((it == r) & (counts[(r // 2) % 2, j] > 0), 1.0, flags)
        flags_of(dp)[...] = flags
        flags_sent, flags_awaited = to_groups(flags_of, 8)
        for cp in flags_sent:
            cp.start()
        rcopy(w_down, R.v0.at[0:1536], S.vs.at[0], S.vr.at[0], core_peer).start()
        for s in (0, 1, 3):
            rcopy(R.posf, R.posr.at[s], S.pos_s.at[0], S.pos_r.at[s], core_peer).wait_recv()
        R.posr[2] = R.posf[...]
        table = jnp.concatenate([R.posr[s] for s in range(4)], axis=1)
        picks = []
        for r in range(16):
            j = 2 * (r // 8 + 2 * ((r // 4) % 2)) + r % 2
            picks.append(table[j : j + 1, :])
        pos_rows = jnp.concatenate(picks, axis=0)
        own_w.wait()
        for k in range(2):
            rcopy(R.cx, R.cxr.at[k], S.cx_s.at[0], S.cx_r.at[k], x_peer).wait_recv()
        for cp in flags_awaited:
            cp.wait_recv()
        made = flags_sent + share(jnp.concatenate([R.cxr[0], R.cxr[1]], axis=0))
        cross_attn(R, pos_rows)
        a2 = rcopy(R.a0.at[0:128], R.a0.at[0:128], S.a2_s.at[0], S.a2_r.at[0], core_peer)
        a2.start()
        da2 = rcopy(R.a1.at[0:128], R.cot.at[0:128], S.da2_s.at[0], S.da2_r.at[0], core_peer)
        da2.wait_recv()
        cross_attn_back(R)
        dc_copy(0, x_peer).start()
        dc_copy(1, diag).start()
        rr = lax.broadcasted_iota(jnp.int32, (8, 128), 1)
        jj = lax.broadcasted_iota(jnp.int32, (8, 128), 0)
        seg_of = 2 * (((rr >> 3) & 1) + 2 * ((rr >> 2) & 1)) + (rr & 1)
        pick = jnp.where(seg_of == jj, 1.0, 0.0).astype(bf16)
        dpos = nn(pick, R.da0[128:256, :].astype(bf16))
        for s in range(4):
            R.gps[s] = dpos[:, 192 * s : 192 * s + 192]
        gp_copy(0, x_peer).start()
        gp_copy(1, diag).start()
        gp_copy(3, core_peer).start()
        gp_own = lcopy(R.gps.at[2], o_pos, S.gp_s.at[2])
        gp_own.start()
        R.gtot[...] = R.gsum[...]
        gg_own.start()
        cross_attn_weights(R)
        w_out = lcopy(R.wall.at[1], o_gw, S.ow.at[0])
        w_out.start()
        rcopy(w_down, R.v0.at[0:1536], S.vs.at[0], S.vr.at[0], core_peer).wait_send()
        each_sent(cf_copy, 3)
        for cp in made:
            cp.wait_send()
        a2.wait_send()
        dc_copy(0, x_peer).wait_send()
        dc_copy(1, diag).wait_send()
        gp_copy(0, x_peer).wait_send()
        gp_copy(1, diag).wait_send()
        gp_copy(3, core_peer).wait_send()
        gp_own.wait()
        gg_own.wait()
        w_out.wait()
        a3_copy(0, core_peer).wait_recv()

    @pl.when(is1 & c1)
    def _():
        for s in (0, 1, 2):
            rcopy(R.cfs, R.cfr.at[s], S.cfs_s.at[0], S.cfr_r.at[s], core_peer).wait_recv()
        R.cfr[3] = R.cfs[...]
        block = jnp.concatenate([R.cfr[k, 0:4] for k in (0, 2, 1, 3)], axis=0)
        made = share(block)
        own_w.wait()
        own_v.wait()
        rcopy(w_down, R.v0.at[0:1536], S.vs.at[0], S.vr.at[0], core_peer).wait_recv()
        rcopy(R.a0.at[0:128], R.a0.at[0:128], S.a2_s.at[0], S.a2_r.at[0], core_peer).wait_recv()
        cross_ffn(R)
        a3_copy(0, diag).start()
        a3_copy(1, x_peer).start()
        a3_copy(2, core_peer).start()
        a3_own = lcopy(own_rows(0, 16), o_a3, S.a3_s.at[3])
        a3_own.start()
        cross_ffn_back(R)
        da2 = rcopy(R.a1.at[0:128], R.cot.at[0:128], S.da2_s.at[0], S.da2_r.at[0], core_peer)
        da2.start()
        R.gtot[...] = R.gsum[...]
        gg_own.start()
        cross_ffn_weights(R)
        dv = rcopy(
            R.gp.at[128:896, 0:1536], o_gv, S.dv_s.at[0], S.dv_r.at[0], core_peer
        )
        dv.start()
        w_out = lcopy(R.wall.at[0], o_gw, S.ow.at[0])
        v_out = lcopy(R.gp.at[128:896, 1536:3072], o_gv, S.ow.at[1])
        w_out.start()
        v_out.start()
        each_sent(pos_copy, 2)
        for cp in made:
            cp.wait_send()
        a3_copy(0, diag).wait_send()
        a3_copy(1, x_peer).wait_send()
        a3_copy(2, core_peer).wait_send()
        a3_own.wait()
        da2.wait_send()
        gg_own.wait()
        dv.wait_send()
        w_out.wait()
        v_out.wait()
        gp_copy(0, core_peer).wait_recv()

    @pl.when(is1)
    def _():
        send_ct.wait_send()
        for k in range(2):

            @pl.when(c == k)
            def _(k=k):
                mine = [q for q in range(SLOTS) if PLANE[k][q] == 1]
                steps = [step_a, step_b, step_c, step_d, step_e]
                for qs in ([q for q in mine if q < EARLY], [q for q in mine if q >= EARLY]):
                    for tick in ticks(qs, steps):
                        for step, q in tick:
                            step(k, q)
                for q in mine:
                    step_end(k, q)

        a1_copy.wait_recv()
        gt_copy.wait_recv()

        @pl.when(c0)
        def _():
            dv = rcopy(
                R.gp.at[128:896, 0:1536], o_gv, S.dv_s.at[0], S.dv_r.at[0], core_peer
            )
            dv.wait_recv()


def fused(counts, tokens, cotan, w_in, w_down, gain, bias, pos):
    hbm = pl.BlockSpec(memory_space=pl.ANY)
    vmem = pl.BlockSpec(memory_space=pltpu.VMEM)
    out = jax.ShapeDtypeStruct
    return pl.pallas_call(
        kernel,
        in_specs=[pl.BlockSpec(memory_space=pltpu.SMEM), hbm, hbm, hbm, hbm, vmem, vmem, vmem],
        out_specs=[hbm] * 8,
        out_shape=[
            out((512, D), bf16),
            out((16, D), f32),
            out((512, D), bf16),
            out((D, FF), bf16),
            out((D, 1536), bf16),
            out((8, D), f32),
            out((8, 192), f32),
            out((D, 4608), bf16),
        ],
        scratch_shapes=[pltpu.VMEM(s, d) for s, d in SCRATCH.values()]
        + [pltpu.SemaphoreType.DMA((n,)) for n in SEMS.values()]
        + [pltpu.SemaphoreType.REGULAR],
        compiler_params=pltpu.CompilerParams(
            collective_id=0, has_side_effects=True, vmem_limit_bytes=64 * 2**20 - 2**17
        ),
        name="layers",
    )(counts, tokens, cotan, w_in, w_down, gain, bias, pos)


def finish(counts, a1, a3, gt, gw, gv, gg, gpos):
    def body(cnt, a1_ref, a3_ref, gt_ref, w_ref, v_ref, gg_ref, gpos_ref, *outs):
        o_mixed, o_gt, o_w, o_v, o_gain, o_bias, o_pos = outs
        sec = lax.axis_index("section")
        k = pl.program_id(0)
        n = cnt[lax.div(k, 2), 2 * sec + lax.rem(k, 2)]
        row = lax.broadcasted_iota(jnp.int32, (128, 1), 0)
        pick = lax.rem(sec, 2) * 8 + lax.div(sec, 2) * 4 + k
        it = lax.broadcasted_iota(jnp.int32, (16, 1), 0)
        top = jnp.sum(jnp.where(it == pick, a3_ref[...], 0.0), axis=0, keepdims=True)
        both = jnp.where(row == 0, top, a1_ref[...].astype(f32))
        o_mixed[...] = jnp.where(row < n, both, 0.0).astype(bf16)
        o_gt[...] = gt_ref[...].astype(f32)
        o_w[...] = w_ref[...].astype(f32)
        o_v[...] = v_ref[...].T.astype(f32)
        o_gain[...] = gg_ref[0:1, :]
        o_bias[...] = gg_ref[1:2, :]
        o_pos[...] = gpos_ref[...]

    out = jax.ShapeDtypeStruct
    rows = pl.BlockSpec((128, D), lambda i: (i, 0))

    def whole(*shape):
        return pl.BlockSpec(shape, lambda i: (0, 0))

    return pl.pallas_call(
        body,
        grid=(4,),
        in_specs=[
            pl.BlockSpec(memory_space=pltpu.SMEM),
            rows,
            whole(16, D),
            rows,
            pl.BlockSpec((192, FF), lambda i: (i, 0)),
            pl.BlockSpec((D, 384), lambda i: (0, i)),
            whole(8, D),
            whole(8, 192),
        ],
        out_specs=[
            rows,
            rows,
            pl.BlockSpec((192, FF), lambda i: (i, 0)),
            pl.BlockSpec((384, D), lambda i: (i, 0)),
            whole(1, D),
            whole(1, D),
            whole(8, 192),
        ],
        out_shape=[
            out((512, D), bf16),
            out((512, D), f32),
            out((D, FF), f32),
            out((1536, D), f32),
            out((1, D), f32),
            out((1, D), f32),
            out((8, 192), f32),
        ],
        compiler_params=pltpu.CompilerParams(vmem_limit_bytes=60 * 2**20),
        name="finish",
    )(counts, a1, a3, gt, gw, gv, gg, gpos)


def shards(tokens, seg_counts, w_in, w_down, ln_gain, ln_bias, pos_table, cotangent):
    a1, a3, gt, gw, gv, gg, gpos, _ = fused(
        seg_counts,
        tokens.reshape(512, D),
        cotangent.reshape(512, D),
        w_in[0],
        w_down,
        ln_gain,
        ln_bias,
        pos_table,
    )
    size = lax.axis_size("dp")
    if size > 8:
        rings = [[i + 8 * k for k in range(size // 8)] for i in range(8)]
        gw, gv, gg, gpos = lax.psum((gw, gv, gg, gpos), "dp", axis_index_groups=rings)
    made = finish(seg_counts, a1, a3, gt, gw, gv, gg, gpos)
    mixed, gtok, gw, gv, gain, bias, gpos = made
    return (
        mixed.reshape(2, 256, D),
        gtok.reshape(2, 256, D),
        gw[None],
        gv,
        gain,
        bias,
        gpos,
    )


def solution(mesh):
    return jax.shard_map(
        shards,
        mesh=mesh,
        in_specs=(
            P("dp", "section", None),
            P("dp", None),
            P("section", None, None),
            P("section", None),
            P("section", None),
            P("section", None),
            P(None, "section"),
            P("dp", "section", None),
        ),
        out_specs=(
            P("dp", "section", None),
            P("dp", "section", None),
            P("section", None, None),
            P("section", None),
            P("section", None),
            P("section", None),
            P(None, "section"),
        ),
        check_vma=False,
    )
```

```python
import functools

import jax
import jax.numpy as jnp
from jax import lax
from jax.experimental import pallas as pl
from jax.experimental.pallas import tpu as pltpu
from jax.sharding import PartitionSpec as P

bf16 = jnp.bfloat16
f32 = jnp.float32
D = 768
FF = 3072
ROWS = 1024
WB = 512
CH = 256
SLOTS = 18
EARLY = 12
PLANE = (
    (0, 1, 0, 1, 0, 1, 0, 1, 0, 1, 0, 1, 0, 0, 1, 0, 0, 0),
    (1, 0, 1, 0, 1, 0, 1, 0, 1, 0, 1, 0, 0, 1, 0, 0, 0, 0),
)
ZONES = max(p.count(x) for p in PLANE for x in (0, 1))
MESH = pl.DeviceIdType.MESH


class Refs:
    pass


def nn(a, b):
    return lax.dot_general(a, b, (((1,), (0,)), ((), ())), preferred_element_type=f32)


def nt(a, b):
    return lax.dot_general(a, b, (((1,), (1,)), ((), ())), preferred_element_type=f32)


def tn(a, b):
    return lax.dot_general(a, b, (((0,), (0,)), ((), ())), preferred_element_type=f32)


def cut(start, size):
    return pl.ds(pl.multiple_of(start, size), size)


def loop(n, body):
    def step(i, carry):
        body(i)
        return carry

    lax.fori_loop(0, n, step, 0)


def norm_stats(r):
    mean = jnp.mean(r, axis=-1, keepdims=True)
    cen = r - mean
    var = jnp.mean(cen * cen, axis=-1, keepdims=True)
    rstd = lax.rsqrt(var + 1e-5)
    return cen * rstd, rstd


def norm_back(dy, xhat, rstd, gain):
    dx = dy * gain
    m1 = jnp.mean(dx, axis=-1, keepdims=True)
    m2 = jnp.mean(dx * xhat, axis=-1, keepdims=True)
    return rstd * (dx - m1 - xhat * m2)


def gelu_parts(u):
    phi = 0.5 * lax.erf(u * 0.7071067811865476) + 0.5
    density = jnp.exp2(u * u * -0.7213475204444817 - 1.3257480647361595)
    return u * phi, phi + u * density


def stacked(v):
    low = lax.broadcasted_iota(jnp.int32, v.shape, 1) < 64
    z = jnp.zeros_like(v)
    return jnp.concatenate([jnp.where(low, v, z), jnp.where(low, z, v)], axis=0)


def beside(v):
    low = lax.broadcasted_iota(jnp.int32, (128, 128), 1) < 64
    return jnp.where(low, v[:128], v[128:])


def attn_block(R, i, vis):
    rs = cut(i * 128, 128)
    for j in range(6):
        q2 = R.qkv[rs, 128 * j : 128 * j + 128]
        k2 = R.qkv[rs, 768 + 128 * j : 768 + 128 * j + 128]
        v2 = R.qkv[rs, 1536 + 128 * j : 1536 + 128 * j + 128]
        s = jnp.where(vis, nt(stacked(q2), k2) * 0.125, -1e30)
        s = jnp.exp(s - jnp.max(s, axis=-1, keepdims=True))
        pr = (s / jnp.sum(s, axis=-1, keepdims=True)).astype(bf16)
        R.p[cut(i * 1536 + 256 * j, 256), :] = pr
        R.ctx[rs, 128 * j : 128 * j + 128] = beside(nn(pr, v2)).astype(bf16)


def attn_block_back(R, i):
    rs = cut(i * 128, 128)
    for j in range(6):
        sq, sk, sv = [slice(b + 128 * j, b + 128 * j + 128) for b in (0, 768, 1536)]
        q2 = R.qkv[rs, sq]
        k2 = R.qkv[rs, sk]
        v2 = R.qkv[rs, sv]
        qs = stacked(q2)
        dos = stacked(R.xh1[rs, sq])
        pr = R.p[cut(i * 1536 + 256 * j, 256), :]
        pf = pr.astype(f32)
        dp = nt(dos, v2)
        ds = (pf * (dp - jnp.sum(dp * pf, axis=-1, keepdims=True))).astype(bf16)
        R.qkv[rs, sv] = tn(pr, dos).astype(bf16)
        R.qkv[rs, sq] = beside(nn(ds, k2) * 0.125).astype(bf16)
        R.qkv[rs, sk] = (tn(ds, qs) * 0.125).astype(bf16)


def qkv_rows(R, r0, n):
    def body(k):
        cs = cut(k * 768, 768)
        R.qkv[pl.ds(r0, n), cs] = nn(R.x[pl.ds(r0, n), :], R.wall[0, :, cs]).astype(bf16)

    loop(3, body)


def attn_rows(R, r0, n):
    key = lax.broadcasted_iota(jnp.int32, (256, 128), 1)

    def seg(k):
        i = r0 // 128 + k
        attn_block(R, i, key < jnp.maximum(R.count_of(i), 1))

    loop(n // 128, seg)
    rs = pl.ds(r0, n)
    R.da0[rs, :] = nt(R.ctx[rs, :], R.wall[0, :, 2304:])

    def norm(k):
        rs = cut(r0 + k * 128, 128)
        xh, rstd = norm_stats(R.x[rs, :].astype(f32) + R.da0[rs, :])
        R.xh0[rs, :] = xh.astype(bf16)
        R.rs[rs, 0:1] = rstd
        R.a0[rs, :] = (xh * R.gains[0, 0:1, :] + R.gains[0, 1:2, :]).astype(bf16)

    loop(n // 128, norm)


def ffn_up(R, h):
    rs = pl.ds(h * 512, 512)

    def up(n):
        cs = cut(n * WB, WB)
        mm, gg = gelu_parts(nn(R.a0[rs, :], R.wall[1, :, cs]))
        R.m[rs, cs] = mm.astype(bf16)
        R.gp[rs, cs] = gg.astype(bf16)

    loop(6, up)


def ffn_down(R, h):
    rs = pl.ds(h * 512, 512)
    R.da0[rs, :] = nn(R.m[rs, :], R.v0[...])

    def norm(k):
        rs = cut(h * 512 + k * 128, 128)
        xh, rstd = norm_stats(R.a0[rs, :].astype(f32) + R.da0[rs, :])
        R.xh1[rs, :] = xh.astype(bf16)
        R.rs[rs, 1:2] = rstd
        R.a1[rs, :] = (xh * R.gains[1, 0:1, :] + R.gains[1, 1:2, :]).astype(bf16)

    loop(4, norm)


def pad16(v):
    return jnp.concatenate([v, jnp.zeros_like(v)], axis=0).astype(bf16)


def first_ffn(R):
    rows = [R.a0[i * 128 : i * 128 + 16, :].astype(f32)[0:1, :] for i in range(8)]
    af = jnp.concatenate(rows, axis=0)
    a16 = pad16(af)

    def up(n):
        cs = cut(n * 1536, 1536)
        mm, gg = gelu_parts(nn(a16, R.wall[1, :, cs]))
        R.fm[:, cs] = mm.astype(bf16)
        R.fg[:, cs] = gg.astype(bf16)

    loop(2, up)
    xh, rstd = norm_stats(af + nn(R.fm[...], R.v0[...])[0:8])
    R.fxh[...] = xh
    R.frs[...] = rstd
    return (xh * R.gains[1, 0:1, :] + R.gains[1, 1:2, :]).astype(bf16).astype(f32)


def ln1_back(R):
    row = lax.broadcasted_iota(jnp.int32, (128, 1), 0)

    def body(i):
        rs = cut(i * 128, 128)
        live = (row < R.count_of(i)) & (row > 0)
        dy = jnp.where(live, R.cot[rs, :].astype(f32), 0.0)
        xh = R.xh1[rs, :].astype(f32)
        R.gsum[2:3, :] += jnp.sum(dy * xh, axis=0, keepdims=True)
        R.gsum[3:4, :] += jnp.sum(dy, axis=0, keepdims=True)
        dr = norm_back(dy, xh, R.rs[rs, 1:2], R.gains[1, 0:1, :])
        R.da0[rs, :] = dr
        R.cot[rs, :] = dr.astype(bf16)

    loop(8, body)


def row_pass(R):
    def hid(n):
        cs = cut(n * WB, WB)
        dm = nt(R.cot[...], R.v0[cs, :])
        R.gp[:, cs] = (dm * R.gp[:, cs].astype(f32)).astype(bf16)

    loop(6, hid)

    def back(k):
        rs = cut(k * 512, 512)
        R.da0[rs, :] += nt(R.gp[rs, :], R.wall[1])

    loop(2, back)


def put_first(ref, i, rowval):
    rs = slice(i * 128, i * 128 + 16)
    blk = ref[rs, :]
    it = lax.broadcasted_iota(jnp.int32, blk.shape, 0)
    ref[rs, :] = jnp.where(it == 0, rowval.astype(f32), blk.astype(f32)).astype(blk.dtype)


def first_back(R, dc):
    xh = R.fxh[...]
    R.gsum[2:3, :] += jnp.sum(dc * xh, axis=0, keepdims=True)
    R.gsum[3:4, :] += jnp.sum(dc, axis=0, keepdims=True)
    dr = norm_back(dc, xh, R.frs[...], R.gains[1, 0:1, :])
    dz = pad16(dr)

    def hid(n):
        cs = cut(n * 1536, 1536)
        R.fdu[:, cs] = (nt(dz, R.v0[cs, :]) * R.fg[:, cs].astype(f32)).astype(bf16)

    loop(2, hid)
    for i in range(8):
        put_first(R.cot, i, dr[i : i + 1, :].astype(bf16))
    R.fxh[...] = dr


def first_back_rest(R):
    da = R.fxh[...] + nt(R.fdu[...], R.wall[1])[0:8]
    du = R.fdu[...].astype(f32)
    for i in range(8):
        put_first(R.gp, i, du[i : i + 1, :])
        put_first(R.da0, i, da[i : i + 1, :])


def transposes1(R):
    for b, ref in ((0, R.a0), (1536, R.cot)):

        def body(k, b=b, ref=ref):
            R.v0[b : b + 768, cut(k * 256, 256)] = ref[cut(k * 256, 256), :].T

        loop(3, body)
        R.v0[b + 768 : b + 1536, 0:256] = ref[768:1024, :].T


def tdot(R, b, rhs, cs):
    head = nn(R.v0[b : b + 768, :], rhs[0:768, cs])
    return head + nn(R.v0[b + 768 : b + 1536, 0:256], rhs[768:1024, cs])


def dvt_block(R, n):
    cs = pl.ds(n * WB, WB)
    R.m[0:768, cs] = tdot(R, 1536, R.m, cs).astype(bf16)


def dw1_block(R, n):
    cs = pl.ds(n * WB, WB)
    R.wall[1, :, cs] = tdot(R, 0, R.gp, cs).astype(bf16)


def ln0_back(R):
    def body(i):
        rs = cut(i * 128, 128)
        dy = R.da0[rs, :].astype(bf16).astype(f32)
        xh = R.xh0[rs, :].astype(f32)
        R.gsum[0:1, :] += jnp.sum(dy * xh, axis=0, keepdims=True)
        R.gsum[1:2, :] += jnp.sum(dy, axis=0, keepdims=True)
        dr = norm_back(dy, xh, R.rs[rs, 0:1], R.gains[0, 0:1, :])
        R.da0[rs, :] = dr
        R.a1[rs, :] = dr.astype(bf16)

    loop(8, body)


def dctx_pass(R):
    def body(k):
        rs = cut(k * 512, 512)
        R.xh1[rs, :] = nn(R.a1[rs, :], R.wall[0, :, 2304:]).astype(bf16)

    loop(2, body)


def transposes2(R):
    for c0, ref in ((0, R.x), (1024, R.a1)):

        def body(k, c0=c0, ref=ref):
            R.gp[0:768, cut(c0 + k * 256, 256)] = ref[cut(k * 256, 256), :].T

        loop(4, body)


def dx_pass(R):
    def body(k):
        rs = cut(k * 512, 512)
        R.cot[rs, :] = (R.da0[rs, :] + nt(R.qkv[rs, :], R.wall[0, :, :2304])).astype(bf16)

    loop(2, body)


def dw0_block(R, n):
    edges = [n * WB, 2304, (n + 1) * WB] if n == 4 else [n * WB, (n + 1) * WB]
    for lo, hi in zip(edges, edges[1:]):
        if hi <= 2304:
            out = nn(R.gp[0:768, 0:1024], R.qkv[:, lo:hi])
        else:
            out = nn(R.gp[0:768, 1024:2048], R.ctx[:, lo - 2304 : hi - 2304])
        R.wall[0, :, lo:hi] = out.astype(bf16)


def cross_attn(R, pos_rows):
    cp = (R.da0[256:384, :] + jnp.concatenate([pos_rows] * 8, axis=0)).astype(bf16)
    R.x[0:128, :] = cp
    live = R.flags[...].T
    row = lax.broadcasted_iota(jnp.int32, (128, 128), 0)
    col = lax.broadcasted_iota(jnp.int32, (128, 128), 1)
    same = (row & 0x72) == (col & 0x72)
    vis = same & (live > 0.5)
    R.da0[384:512, 0:128] = jnp.where(vis, 1.0, 0.0)

    def qkv(n):
        cs = cut(n * 768, 768)
        R.qkv[0:128, cs] = nn(R.x[0:128, :], R.wall[1, :, cs]).astype(bf16)

    loop(3, qkv)
    mask = R.da0[384:512, 0:128] > 0.5
    attn_block(R, 0, jnp.concatenate([mask, mask], axis=0))
    att = nt(R.ctx[0:128, :], R.wall[1, :, 2304:])
    xh, rstd = norm_stats(R.x[0:128, :].astype(f32) + att)
    R.da0[0:128, :] = xh
    R.rs[0:128, 0:1] = rstd
    R.a0[0:128, :] = (xh * R.gains[0, 0:1, :] + R.gains[0, 1:2, :]).astype(bf16)


def cross_attn_back(R):
    dy = R.cot[0:128, :].astype(f32)
    xh = R.da0[0:128, :]
    R.gsum[0:1, :] = jnp.sum(dy * xh, axis=0, keepdims=True)
    R.gsum[1:2, :] = jnp.sum(dy, axis=0, keepdims=True)
    dr = norm_back(dy, xh, R.rs[0:128, 0:1], R.gains[0, 0:1, :])
    R.da0[0:128, :] = dr
    R.a1[0:128, :] = dr.astype(bf16)
    R.xh1[0:128, :] = nn(R.a1[0:128, :], R.wall[1, :, 2304:]).astype(bf16)
    attn_block_back(R, 0)
    dcp = R.da0[0:128, :] + nt(R.qkv[0:128, :], R.wall[1, :, :2304])
    R.da0[128:256, :] = dcp.astype(bf16).astype(f32)


def cross_attn_weights(R):
    R.gp[128:896, 0:128] = R.x[0:128, :].T
    R.gp[128:896, 128:256] = R.a1[0:128, :].T

    def one(n):
        cs = cut(n * 256, 256)
        R.wall[1, :, cs] = nn(R.gp[128:896, 0:128], R.qkv[0:128, cs]).astype(bf16)

    loop(9, one)

    def two(n):
        c2 = cut(n * 256, 256)
        cs = cut(2304 + n * 256, 256)
        R.wall[1, :, cs] = nn(R.gp[128:896, 128:256], R.ctx[0:128, c2]).astype(bf16)

    loop(3, two)


def cross_ffn(R):
    def up(n):
        cs = cut(n * 768, 768)
        mm, gg = gelu_parts(nn(R.a0[0:128, :], R.wall[0, :, cs]))
        R.gp[896:1024, cs] = mm.astype(bf16)
        R.gp[0:128, cs] = gg.astype(bf16)

    loop(4, up)
    xh, rstd = norm_stats(R.a0[0:128, :].astype(f32) + nn(R.gp[896:1024, :], R.v0[...]))
    R.da0[0:128, :] = xh
    R.rs[0:128, 0:1] = rstd
    R.da0[128:256, :] = xh * R.gains[0, 0:1, :] + R.gains[0, 1:2, :]


def cross_ffn_back(R):
    dy = R.da0[256:384, :]
    xh = R.da0[0:128, :]
    R.gsum[0:1, :] = jnp.sum(dy * xh, axis=0, keepdims=True)
    R.gsum[1:2, :] = jnp.sum(dy, axis=0, keepdims=True)
    dr = norm_back(dy, xh, R.rs[0:128, 0:1], R.gains[0, 0:1, :])
    R.da0[0:128, :] = dr
    R.cot[0:128, :] = dr.astype(bf16)

    def hid(n):
        cs = cut(n * 768, 768)
        dm = nt(R.cot[0:128, :], R.v0[cs, :])
        R.gp[0:128, cs] = (dm * R.gp[0:128, cs].astype(f32)).astype(bf16)

    loop(4, hid)
    R.a1[0:128, :] = (R.da0[0:128, :] + nt(R.gp[0:128, :], R.wall[0])).astype(bf16)


def cross_ffn_weights(R):
    R.qkv[0:768, 0:128] = R.a0[0:128, :].T
    R.qkv[0:768, 128:256] = R.cot[0:128, :].T

    def body(n):
        cs = cut(n * 256, 256)
        R.wall[0, :, cs] = nn(R.qkv[0:768, 0:128], R.gp[0:128, cs]).astype(bf16)
        R.gp[128:896, cs] = nn(R.qkv[0:768, 128:256], R.gp[896:1024, cs]).astype(bf16)

    loop(12, body)


SCRATCH = dict(
    wall=((2, D, FF), bf16),
    v0=((FF, D), bf16),
    x=((ROWS, D), bf16),
    qkv=((ROWS, 2304), bf16),
    p=((12288, 128), bf16),
    ctx=((ROWS, D), bf16),
    xh0=((ROWS, D), bf16),
    rs=((ROWS, 2), f32),
    a0=((ROWS, D), bf16),
    m=((ROWS, FF), bf16),
    gp=((ROWS, FF), bf16),
    xh1=((ROWS, D), bf16),
    a1=((ROWS, D), bf16),
    cot=((ROWS, D), bf16),
    da0=((ROWS, D), f32),
    gains=((2, 8, D), f32),
    gsum=((8, D), f32),
    gtot=((8, D), f32),
    gsr=((8, 8, D), f32),
    fm=((16, FF), bf16),
    fg=((16, FF), bf16),
    fdu=((16, FF), bf16),
    fxh=((8, D), f32),
    frs=((8, 1), f32),
    flags=((128, 128), f32),
    cx=((8, D), f32),
    cxr=((2, 8, D), f32),
    ctmp=((4, 16, D), bf16),
    cfs=((8, D), f32),
    cfr=((4, 8, D), f32),
    dcr=((8, D), f32),
    posf=((8, 192), f32),
    posr=((4, 8, 192), f32),
    gps=((4, 8, 192), f32),
    rx=((6, D, CH), bf16),
    yb=((ZONES, 384, CH), bf16),
    zb=((ZONES, 2, 384, CH), bf16),
)
SEMS = dict(
    load=16, ctmp=4, ws=2, wr=2, vs=1, vr=1, gns=1, gnr=1, tks=3, tkr=3, pos_s=1, pos_r=4, cfs_s=1, cfr_r=4,
    cx_s=1, cx_r=2, gat_s=16, gat_r=16, a2_s=1, a2_r=1, a3_s=4, a3_r=1, da2_s=1, da2_r=1, dc_s=2, dc_r=1,
    gp_s=4, gp_r=1, dv_s=1, dv_r=1, a1_s=1, a1_r=1, a1_l=1, gt_s=1, gt_r=1, gt_l=1, gs_s=8, gs_r=8, og=1, ow=2,
    s1_s=18, s1_r=18, xf_s=18, xf_r=18, y_s=18, y_r=18, z1_s=18, z1_r=18, z2_s=18, z2_r=18, z3_s=18, z3_r=18,
    h_s=18, h_r=36, b1_s=18, b1_r=36, b2_s=18, b2_r=36, out_s=18, out_r=36, hx_r=18,
)


def kernel(
    counts, tokens, cotan, w_in, w_down, gain, bias, pos,
    o_a1, o_a3, o_gt, o_gw, o_gv, o_gg, o_pos, o_pass, *scratch,
):
    R, S = Refs(), Refs()
    for name, ref in zip(SCRATCH, scratch):
        setattr(R, name, ref)
    free = scratch[-1]
    for name, ref in zip(SEMS, scratch[len(SCRATCH) :]):
        setattr(S, name, ref)

    group = lax.axis_index("dp")
    dp = lax.rem(group, 8)
    sec = lax.axis_index("section")
    z, y = lax.div(dp, 2), lax.rem(dp, 2)
    xx, c = lax.div(sec, 2), lax.rem(sec, 2)

    def at(px, pc):
        return {"section": px * 2 + pc}

    def at_dp(pz, py):
        return {"dp": group - dp + pz * 2 + py}

    core_peer, x_peer, diag = at(xx, 1 - c), at(1 - xx, c), at(1 - xx, 1 - c)
    y_peer = at_dp(z, 1 - y)
    z_near, z_over = at_dp(z ^ 1, y), at_dp(z ^ 3, y)
    middle = (z == 1) | (z == 2)
    dp_peers = [{"dp": group - dp + (dp ^ d)} for d in range(1, 8)]

    def rcopy(src, dst, ss, rs, dev):
        return pltpu.make_async_remote_copy(
            src_ref=src, dst_ref=dst, send_sem=ss, recv_sem=rs, device_id=dev, device_id_type=MESH
        )

    def lcopy(src, dst, sem):
        return pltpu.make_async_copy(src, dst, sem)

    def count_of(i):
        return counts[lax.rem(lax.div(i, 2), 2), 2 * (c + 2 * lax.div(i, 4)) + lax.rem(i, 2)]

    R.count_of = count_of
    is0, is1 = xx == 0, xx == 1
    c0, c1 = c == 0, c == 1

    barrier = pltpu.get_barrier_semaphore()
    partners = [core_peer, x_peer, diag] + dp_peers
    for dev in partners:
        pl.semaphore_signal(barrier, inc=1, device_id=dev, device_id_type=MESH)

    own_w = lcopy(w_in, R.wall.at[jnp.where(is0, c, 1 - c)], S.load.at[0])
    own_v = lcopy(w_down, R.v0.at[cut(c * 1536, 1536)], S.load.at[1])
    own_x = lcopy(tokens, R.x.at[0:512], S.load.at[2])
    own_ct = lcopy(cotan, R.cot.at[0:512], S.load.at[3])
    heads = [lcopy(cotan.at[pl.ds(k * 128, 16)], R.ctmp.at[k], S.ctmp.at[k]) for k in range(4)]

    @pl.when(is0)
    def _():
        own_x.start()

    own_w.start()

    @pl.when(is0 | c1)
    def _():
        own_v.start()

    for cp in heads:
        cp.start()
    R.gsum[...] = jnp.zeros_like(R.gsum)
    gslot = jnp.where(is0, c, 0)
    R.gains[gslot, 0:1, :] = gain[...].astype(f32)
    R.gains[gslot, 1:2, :] = bias[...].astype(f32)
    R.posf[...] = pos[...].astype(f32)
    for cp in heads:
        cp.wait()
    first_rows = []
    for k in range(4):
        n = counts[k // 2, 2 * sec + k % 2]
        r = R.ctmp[k].astype(f32)[0:1, :]
        first_rows.append(jnp.where(n > 0, r, 0.0))
    R.cfs[...] = jnp.concatenate(first_rows + first_rows, axis=0)

    pl.semaphore_wait(barrier, len(partners))

    send_w = rcopy(w_in, R.wall.at[c], S.ws.at[0], S.wr.at[0], core_peer)
    send_v = rcopy(w_down, R.v0.at[cut(c * 1536, 1536)], S.vs.at[0], S.vr.at[0], core_peer)
    send_g = rcopy(R.gains.at[c], R.gains.at[c], S.gns.at[0], S.gnr.at[0], core_peer)
    send_x = [
        rcopy(
            tokens.at[256 * k : 256 * k + 256],
            R.x.at[512 + 256 * k : 768 + 256 * k],
            S.tks.at[2 * k],
            S.tkr.at[2 * k],
            x_peer,
        )
        for k in range(2)
    ]
    send_ct = rcopy(cotan, R.cot.at[512:1024], S.tks.at[1], S.tkr.at[1], x_peer)
    other_w = rcopy(w_in, R.wall.at[1 - c], S.ws.at[0], S.wr.at[0], core_peer)
    other_v = rcopy(w_down, R.v0.at[cut((1 - c) * 1536, 1536)], S.vs.at[0], S.vr.at[0], core_peer)
    other_g = rcopy(R.gains.at[1 - c], R.gains.at[1 - c], S.gns.at[0], S.gnr.at[0], core_peer)

    def pos_copy(dev):
        return rcopy(R.posf, R.posr.at[sec], S.pos_s.at[0], S.pos_r.at[sec], dev)

    def cf_copy(dev):
        return rcopy(R.cfs, R.cfr.at[sec], S.cfs_s.at[0], S.cfr_r.at[sec], dev)

    def each_to(make, target):
        by = {2: (x_peer, diag, core_peer), 3: (diag, x_peer, core_peer)}[target]
        for s, dev in zip((0, 1, 5 - target), by):

            @pl.when(sec == s)
            def _(dev=dev):
                make(dev).start()

    def each_sent(make, target):
        @pl.when(sec != target)
        def _():
            make(core_peer).wait_send()

    @pl.when(is0)
    def _():
        send_w.start()
        send_g.start()
        send_v.start()

    @pl.when(is1)
    def _():
        send_x[0].start()
        send_x[1].start()

    each_to(pos_copy, 2)
    each_to(cf_copy, 3)

    def block_of(own, q):
        return 2 * (q % 6) + (own if q < EARLY else 1 - own)

    def slot(own, q, index):
        if q < 6:
            return R.m.at[0:768, pl.ds(pl.multiple_of(own * 1536 + q * CH, CH), CH)]
        return R.wall.at[index, :, pl.ds(pl.multiple_of(block_of(own, q) * CH, CH), CH)]

    def part_of(own, q):
        return slot(own, q, jnp.where(is0, 1 if q < EARLY else 0, c))

    def holder(k, q):
        return k if q < 6 else (1 if q < EARLY else 0)

    def add_rows(dst, r0, terms, n, step):
        def body(k):
            rs = pl.ds(pl.multiple_of(r0 + k * step, 32), step)
            total = dst[rs, :].astype(f32)
            for ref in terms:
                total = total + ref[pl.ds(pl.multiple_of(k * step, 32), step), :].astype(f32)
            dst[rs, :] = total.astype(bf16)

        loop(n // step, body)

    def s1_copy(q):
        return rcopy(
            part_of(1 - c, q), R.rx.at[q % 6], S.s1_s.at[q], S.s1_r.at[q], core_peer
        )

    def s1_send(q):
        if q >= 6:
            pl.semaphore_wait(free, 1)
        s1_copy(q).start()

    def xf_copy(q):
        return rcopy(part_of(c, q), slot(c, q, c), S.xf_s.at[q], S.xf_r.at[q], x_peer)

    def spot(k, q):
        return PLANE[k][:q].count(PLANE[k][q])

    def y_copy(k, q):
        half = part_of(c, q).at[pl.ds(pl.multiple_of((1 - y) * 384, 384), 384), :]
        return rcopy(half, R.yb.at[spot(k, q)], S.y_s.at[q], S.y_r.at[q], y_peer)

    def half_of(ref, h):
        return ref.at[pl.ds(pl.multiple_of(h * 384, 384), 384), :]

    def z1_copy(k, q):
        zone = R.zb.at[spot(k, q), 0]
        return rcopy(half_of(part_of(c, q), y), zone, S.z1_s.at[q], S.z1_r.at[q], z_near)

    def z2_copy(k, q):
        zone = R.zb.at[spot(k, q), 1]
        return rcopy(half_of(part_of(c, q), y), zone, S.z2_s.at[q], S.z2_r.at[q], z_over)

    def z3_copy(k, q):
        zone = R.zb.at[spot(k, q), 0]
        return rcopy(zone, zone, S.z3_s.at[q], S.z3_r.at[q], z_near)

    def final(k, q):
        if q < 6:
            return o_gv.at[:, pl.ds(q * CH, CH)]
        return o_gw.at[:, pl.ds(block_of(k, q) * CH, CH)]

    def passing(q):
        return o_pass.at[:, pl.ds(q * CH, CH)]

    def h_copy(k, q):
        zone = R.zb.at[spot(k, q), 0]
        if PLANE[k][q] == 1:
            return rcopy(zone, half_of(passing(q), y), S.h_s.at[q], S.hx_r.at[q], y_peer)
        there = {**y_peer, **at(xx, holder(k, q))}
        return rcopy(zone, half_of(final(k, q), y), S.h_s.at[q], S.h_r.at[SLOTS * k + q], there)

    def out_copy(k, q):
        zone, there = R.zb.at[spot(k, q), 0], half_of(final(k, q), y)
        if holder(k, q) == k:
            return lcopy(zone, there, S.out_s.at[q])
        return rcopy(zone, there, S.out_s.at[q], S.out_r.at[SLOTS * k + q], core_peer)

    def b1_copy(k, q):
        zone = R.zb.at[spot(k, q), 0]
        there = at(1 - xx, holder(k, q))
        return rcopy(zone, half_of(final(k, q), y), S.b1_s.at[q], S.b1_r.at[SLOTS * k + q], there)

    def b2_copy(k, q):
        src, there = half_of(passing(q), 1 - y), at(1 - xx, holder(k, q))
        return rcopy(src, half_of(final(k, q), 1 - y), S.b2_s.at[q], S.b2_r.at[SLOTS * k + q], there)

    def on(k, *steps):
        @pl.when(c == k)
        def _():
            for step, q in steps:
                step(k, q)

    def chip_sum(k, q):
        s1_copy(q).wait_recv()
        add_rows(part_of(c, q), 0, [R.rx.at[q % 6]], 768, 192)
        if q < SLOTS - 6:
            pl.semaphore_signal(free, inc=1, device_id=core_peer, device_id_type=MESH)
        if PLANE[k][q] == 0:
            y_copy(k, q).start()
        else:
            xf_copy(q).start()

    def step_a(k, q):
        xf_copy(q).wait_recv()
        y_copy(k, q).start()

    def step_b(k, q):
        y_copy(k, q).wait()
        add_rows(part_of(c, q), y * 384, [R.yb.at[spot(k, q)]], 384, 192)

        @pl.when(jnp.logical_not(middle))
        def _():
            z1_copy(k, q).start()

    def step_c(k, q):
        @pl.when(middle)
        def _():
            z1_copy(k, q).wait_recv()
            add_rows(part_of(c, q), y * 384, [R.zb.at[spot(k, q), 0]], 384, 192)
            z2_copy(k, q).start()

    def step_d(k, q):
        n = spot(k, q)

        @pl.when(middle)
        def _():
            z2_copy(k, q).wait()
            mine = half_of(part_of(c, q), y)

            def body(r):
                rs = cut(r * 192, 192)
                total = mine[rs, :].astype(f32) + R.zb[n, 1, rs, :].astype(f32)
                R.zb[n, 0, rs, :] = total.astype(bf16)

            loop(2, body)
            z3_copy(k, q).start()

        @pl.when(jnp.logical_not(middle))
        def _():
            z1_copy(k, q).wait_send()
            z3_copy(k, q).wait_recv()

        h_copy(k, q).start()
        if PLANE[k][q] == 0:
            out_copy(k, q).start()
        else:
            b1_copy(k, q).start()

    def step_e(k, q):
        h_copy(k, q).wait_recv()
        b2_copy(k, q).start()

    def step_end(k, q):
        @pl.when(middle)
        def _():
            z3_copy(k, q).wait_send()

        h_copy(k, q).wait_send()
        if PLANE[k][q] == 1:
            b1_copy(k, q).wait_send()
            b2_copy(k, q).wait_send()
        elif holder(k, q) == k:
            out_copy(k, q).wait()
        else:
            out_copy(k, q).wait_send()

    def arrived(k, q):
        if PLANE[k][q] == 1:
            b1_copy(k, q).wait_recv()
            b2_copy(k, q).wait_recv()
            return
        h_copy(k, q).wait_recv()
        if holder(k, q) != k:
            out_copy(k, q).wait_recv()

    def ticks(qs, steps):
        made = []
        for t in range(len(qs) + len(steps) - 1):
            made.append([(f, qs[t - n]) for n, f in enumerate(steps) if 0 <= t - n < len(qs)])
        return made

    early = [[q for q in range(EARLY) if PLANE[k][q] == 0] for k in range(2)]
    late = [[q for q in range(EARLY, SLOTS) if PLANE[k][q] == 0] for k in range(2)]
    planned = [ticks(early[k], [step_b, step_c, step_d]) for k in range(2)]

    def serve(first, last):
        for k in range(2):
            for tick in planned[k][first:last]:
                on(k, *tick)

    closing = [ticks(late[k], [step_b, step_c, step_d]) for k in range(2)]

    def serve_late(first, last):
        for k in range(2):
            for tick in closing[k][first:last]:
                on(k, *tick)

    def cx_copy(dev):
        return rcopy(R.cx, R.cxr.at[c], S.cx_s.at[0], S.cx_r.at[c], dev)

    def own_rows(r0, n):
        return R.da0.at[pl.ds(pl.multiple_of(128 + dp * 16 + r0, 8), n), :]

    def dc_copy(k, dev):
        return rcopy(own_rows(k * 8, 8), R.dcr, S.dc_s.at[k], S.dc_r.at[0], dev)

    def a3_copy(k, dev):
        return rcopy(own_rows(0, 16), o_a3, S.a3_s.at[k], S.a3_r.at[0], dev)

    def gp_copy(s, dev):
        return rcopy(R.gps.at[s], o_pos, S.gp_s.at[s], S.gp_r.at[0], dev)

    a1_copy = rcopy(R.a1.at[512:1024], o_a1, S.a1_s.at[0], S.a1_r.at[0], x_peer)
    gt_copy = rcopy(R.cot.at[512:1024], o_gt, S.gt_s.at[0], S.gt_r.at[0], x_peer)
    a1_own = lcopy(R.a1.at[0:512], o_a1, S.a1_l.at[0])
    gt_own = lcopy(R.cot.at[0:512], o_gt, S.gt_l.at[0])
    gg_own = lcopy(R.gtot, o_gg, S.og.at[0])

    @pl.when(is0)
    def _():
        own_x.wait()
        own_ct.start()

        @pl.when(c0)
        def _():
            own_w.wait()

        @pl.when(c1)
        def _():
            other_w.wait_recv()

        other_g.wait_recv()
        qkv_rows(R, 0, 512)
        attn_rows(R, 0, 512)
        send_x[0].wait_recv()
        qkv_rows(R, 512, 256)
        attn_rows(R, 512, 256)

        @pl.when(c1)
        def _():
            own_w.wait()

        @pl.when(c0)
        def _():
            other_w.wait_recv()

        ffn_up(R, 0)
        send_x[1].wait_recv()
        qkv_rows(R, 768, 256)
        attn_rows(R, 768, 256)
        own_v.wait()
        other_v.wait_recv()
        R.cx[...] = first_ffn(R)

        @pl.when(c0)
        def _():
            cx_copy(x_peer).start()

        @pl.when(c1)
        def _():
            cx_copy(diag).start()

        ffn_down(R, 0)
        ffn_up(R, 1)
        ffn_down(R, 1)
        a1_copy.start()
        a1_own.start()
        own_ct.wait()
        send_ct.wait_recv()
        ln1_back(R)
        row_pass(R)
        dc_copy(0, core_peer).wait_recv()
        first_back(R, R.dcr[...])
        transposes1(R)

        def chip_sums(q):
            on(0, (chip_sum, q))
            on(1, (chip_sum, q))

        for q in range(EARLY):
            if q in (0, 2, 4):
                dvt_block(R, q // 2)
                dvt_block(R, 3 + q // 2)
            elif q >= 6:
                if q == 6:
                    first_back_rest(R)
                dw1_block(R, q - 6)
            s1_send(q)
            if q > 0:
                chip_sums(q - 1)
        serve(0, 1)
        a1_copy.wait_send()
        a1_own.wait()
        ln0_back(R)
        chip_sums(EARLY - 1)
        serve(1, 2)
        chip_g = rcopy(R.gsum, R.gsr.at[0], S.gs_s.at[0], S.gs_r.at[0], core_peer)
        chip_g.start()
        dctx_pass(R)
        chip_g.wait_recv()
        R.gtot[...] = R.gsum[...] + R.gsr[0]
        gsends = [
            rcopy(R.gtot, R.gsr.at[d], S.gs_s.at[d], S.gs_r.at[d], dp_peers[d - 1])
            for d in range(1, 8)
        ]
        for cp in gsends:
            cp.start()
        transposes2(R)
        serve(2, 3)

        def seg(i):
            attn_block_back(R, i)
            for n, place in enumerate((1, 3, 5, 7)):

                @pl.when(i == place)
                def _(n=n):
                    serve(3 + n, 4 + n)

        loop(8, seg)
        dx_pass(R)
        serve(7, 99)
        gt_own.start()
        for q in range(EARLY, SLOTS):
            dw0_block(R, q - EARLY)
            s1_send(q)
            if q > EARLY:
                chip_sums(q - 1)
            if 0 <= q - EARLY - 4 < 3:
                serve_late(q - EARLY - 4, q - EARLY - 3)
        chip_sums(SLOTS - 1)
        gt_copy.start()
        serve_late(2, 99)

        for cp in gsends:
            cp.wait()
        total = R.gsum[...] + R.gsr[0]
        for d in range(1, 8):
            total = total + R.gsr[d]
        pair = jnp.where(c0, total[0:2], total[2:4])
        R.gtot[...] = jnp.concatenate([pair] * 4, axis=0)
        gg_own.start()
        send_w.wait_send()
        send_g.wait_send()
        send_v.wait_send()
        each_sent(pos_copy, 2)
        each_sent(cf_copy, 3)
        cx_copy(diag).wait_send()
        chip_g.wait_send()
        gt_copy.wait_send()
        gt_own.wait()
        for q in range(SLOTS):
            s1_copy(q).wait_send()
            for k in range(2):

                @pl.when(c == k)
                def _(q=q, k=k):
                    if PLANE[k][q] == 1:
                        xf_copy(q).wait_send()
                    else:
                        step_end(k, q)

                @pl.when(c == holder(k, q))
                def _(q=q, k=k):
                    arrived(k, q)

        a3_copy(0, diag).wait_recv()
        gp_copy(0, diag).wait_recv()
        gg_own.wait()

    def to_groups(part, first):
        def one(g, d):
            return rcopy(part(g), part(g), S.gat_s.at[first + d], S.gat_r.at[first + d], dp_peers[d - 1])

        return [one(dp, d) for d in range(1, 8)], [one(dp ^ d, d) for d in range(1, 8)]

    def rows_of(g):
        return R.da0.at[pl.ds(pl.multiple_of(256 + g * 16, 16), 16), :]

    def flags_of(g):
        return R.flags.at[pl.ds(pl.multiple_of(g * 16, 16), 16), :]

    def share(block):
        rows_of(dp)[...] = block
        sent, awaited = to_groups(rows_of, 0)
        for cp in sent:
            cp.start()
        for cp in awaited:
            cp.wait_recv()
        return sent

    @pl.when(is1)
    def _():
        send_x[0].wait_send()
        send_x[1].wait_send()
        send_ct.start()

    @pl.when(is1 & c0)
    def _():
        it = lax.broadcasted_iota(jnp.int32, (16, 128), 0)
        flags = jnp.zeros((16, 128), f32)
        for r in range(16):
            j = 2 * (r // 8 + 2 * ((r // 4) % 2)) + r % 2
            flags = jnp.where((it == r) & (counts[(r // 2) % 2, j] > 0), 1.0, flags)
        flags_of(dp)[...] = flags
        flags_sent, flags_awaited = to_groups(flags_of, 8)
        for cp in flags_sent:
            cp.start()
        rcopy(w_down, R.v0.at[0:1536], S.vs.at[0], S.vr.at[0], core_peer).start()
        for s in (0, 1, 3):
            rcopy(R.posf, R.posr.at[s], S.pos_s.at[0], S.pos_r.at[s], core_peer).wait_recv()
        R.posr[2] = R.posf[...]
        table = jnp.concatenate([R.posr[s] for s in range(4)], axis=1)
        picks = []
        for r in range(16):
            j = 2 * (r // 8 + 2 * ((r // 4) % 2)) + r % 2
            picks.append(table[j : j + 1, :])
        pos_rows = jnp.concatenate(picks, axis=0)
        own_w.wait()
        for k in range(2):
            rcopy(R.cx, R.cxr.at[k], S.cx_s.at[0], S.cx_r.at[k], x_peer).wait_recv()
        for cp in flags_awaited:
            cp.wait_recv()
        made = flags_sent + share(jnp.concatenate([R.cxr[0], R.cxr[1]], axis=0))
        cross_attn(R, pos_rows)
        a2 = rcopy(R.a0.at[0:128], R.a0.at[0:128], S.a2_s.at[0], S.a2_r.at[0], core_peer)
        a2.start()
        da2 = rcopy(R.a1.at[0:128], R.cot.at[0:128], S.da2_s.at[0], S.da2_r.at[0], core_peer)
        da2.wait_recv()
        cross_attn_back(R)
        dc_copy(0, x_peer).start()
        dc_copy(1, diag).start()
        rr = lax.broadcasted_iota(jnp.int32, (8, 128), 1)
        jj = lax.broadcasted_iota(jnp.int32, (8, 128), 0)
        seg_of = 2 * (((rr >> 3) & 1) + 2 * ((rr >> 2) & 1)) + (rr & 1)
        pick = jnp.where(seg_of == jj, 1.0, 0.0).astype(bf16)
        dpos = nn(pick, R.da0[128:256, :].astype(bf16))
        for s in range(4):
            R.gps[s] = dpos[:, 192 * s : 192 * s + 192]
        gp_copy(0, x_peer).start()
        gp_copy(1, diag).start()
        gp_copy(3, core_peer).start()
        gp_own = lcopy(R.gps.at[2], o_pos, S.gp_s.at[2])
        gp_own.start()
        R.gtot[...] = R.gsum[...]
        gg_own.start()
        cross_attn_weights(R)
        w_out = lcopy(R.wall.at[1], o_gw, S.ow.at[0])
        w_out.start()
        rcopy(w_down, R.v0.at[0:1536], S.vs.at[0], S.vr.at[0], core_peer).wait_send()
        each_sent(cf_copy, 3)
        for cp in made:
            cp.wait_send()
        a2.wait_send()
        dc_copy(0, x_peer).wait_send()
        dc_copy(1, diag).wait_send()
        gp_copy(0, x_peer).wait_send()
        gp_copy(1, diag).wait_send()
        gp_copy(3, core_peer).wait_send()
        gp_own.wait()
        gg_own.wait()
        w_out.wait()
        a3_copy(0, core_peer).wait_recv()

    @pl.when(is1 & c1)
    def _():
        for s in (0, 1, 2):
            rcopy(R.cfs, R.cfr.at[s], S.cfs_s.at[0], S.cfr_r.at[s], core_peer).wait_recv()
        R.cfr[3] = R.cfs[...]
        block = jnp.concatenate([R.cfr[k, 0:4] for k in (0, 2, 1, 3)], axis=0)
        made = share(block)
        own_w.wait()
        own_v.wait()
        rcopy(w_down, R.v0.at[0:1536], S.vs.at[0], S.vr.at[0], core_peer).wait_recv()
        rcopy(R.a0.at[0:128], R.a0.at[0:128], S.a2_s.at[0], S.a2_r.at[0], core_peer).wait_recv()
        cross_ffn(R)
        a3_copy(0, diag).start()
        a3_copy(1, x_peer).start()
        a3_copy(2, core_peer).start()
        a3_own = lcopy(own_rows(0, 16), o_a3, S.a3_s.at[3])
        a3_own.start()
        cross_ffn_back(R)
        da2 = rcopy(R.a1.at[0:128], R.cot.at[0:128], S.da2_s.at[0], S.da2_r.at[0], core_peer)
        da2.start()
        R.gtot[...] = R.gsum[...]
        gg_own.start()
        cross_ffn_weights(R)
        dv = rcopy(
            R.gp.at[128:896, 0:1536], o_gv, S.dv_s.at[0], S.dv_r.at[0], core_peer
        )
        dv.start()
        w_out = lcopy(R.wall.at[0], o_gw, S.ow.at[0])
        v_out = lcopy(R.gp.at[128:896, 1536:3072], o_gv, S.ow.at[1])
        w_out.start()
        v_out.start()
        each_sent(pos_copy, 2)
        for cp in made:
            cp.wait_send()
        a3_copy(0, diag).wait_send()
        a3_copy(1, x_peer).wait_send()
        a3_copy(2, core_peer).wait_send()
        a3_own.wait()
        da2.wait_send()
        gg_own.wait()
        dv.wait_send()
        w_out.wait()
        v_out.wait()
        gp_copy(0, core_peer).wait_recv()

    @pl.when(is1)
    def _():
        send_ct.wait_send()
        for k in range(2):

            @pl.when(c == k)
            def _(k=k):
                mine = [q for q in range(SLOTS) if PLANE[k][q] == 1]
                steps = [step_a, step_b, step_c, step_d, step_e]
                for qs in ([q for q in mine if q < EARLY], [q for q in mine if q >= EARLY]):
                    for tick in ticks(qs, steps):
                        for step, q in tick:
                            step(k, q)
                for q in mine:
                    step_end(k, q)

        a1_copy.wait_recv()
        gt_copy.wait_recv()

        @pl.when(c0)
        def _():
            dv = rcopy(
                R.gp.at[128:896, 0:1536], o_gv, S.dv_s.at[0], S.dv_r.at[0], core_peer
            )
            dv.wait_recv()


def fused(counts, tokens, cotan, w_in, w_down, gain, bias, pos):
    hbm = pl.BlockSpec(memory_space=pl.ANY)
    vmem = pl.BlockSpec(memory_space=pltpu.VMEM)
    out = jax.ShapeDtypeStruct
    return pl.pallas_call(
        kernel,
        in_specs=[pl.BlockSpec(memory_space=pltpu.SMEM), hbm, hbm, hbm, hbm, vmem, vmem, vmem],
        out_specs=[hbm] * 8,
        out_shape=[
            out((512, D), bf16),
            out((16, D), f32),
            out((512, D), bf16),
            out((D, FF), bf16),
            out((D, 1536), bf16),
            out((8, D), f32),
            out((8, 192), f32),
            out((D, 4608), bf16),
        ],
        scratch_shapes=[pltpu.VMEM(s, d) for s, d in SCRATCH.values()]
        + [pltpu.SemaphoreType.DMA((n,)) for n in SEMS.values()]
        + [pltpu.SemaphoreType.REGULAR],
        compiler_params=pltpu.CompilerParams(
            collective_id=0, has_side_effects=True, vmem_limit_bytes=64 * 2**20 - 2**17
        ),
        name="layers",
    )(counts, tokens, cotan, w_in, w_down, gain, bias, pos)


def finish(counts, a1, a3, gt, gw, gv, gg, gpos):
    def body(cnt, a1_ref, a3_ref, gt_ref, w_ref, v_ref, gg_ref, gpos_ref, *outs):
        o_mixed, o_gt, o_w, o_v, o_gain, o_bias, o_pos = outs
        sec = lax.axis_index("section")
        k = pl.program_id(0)
        n = cnt[lax.div(k, 2), 2 * sec + lax.rem(k, 2)]
        row = lax.broadcasted_iota(jnp.int32, (128, 1), 0)
        pick = lax.rem(sec, 2) * 8 + lax.div(sec, 2) * 4 + k
        it = lax.broadcasted_iota(jnp.int32, (16, 1), 0)
        top = jnp.sum(jnp.where(it == pick, a3_ref[...], 0.0), axis=0, keepdims=True)
        both = jnp.where(row == 0, top, a1_ref[...].astype(f32))
        o_mixed[...] = jnp.where(row < n, both, 0.0).astype(bf16)
        o_gt[...] = gt_ref[...].astype(f32)
        o_w[...] = w_ref[...].astype(f32)
        o_v[...] = v_ref[...].T.astype(f32)
        o_gain[...] = gg_ref[0:1, :]
        o_bias[...] = gg_ref[1:2, :]
        o_pos[...] = gpos_ref[...]

    out = jax.ShapeDtypeStruct
    rows = pl.BlockSpec((128, D), lambda i: (i, 0))

    def whole(*shape):
        return pl.BlockSpec(shape, lambda i: (0, 0))

    return pl.pallas_call(
        body,
        grid=(4,),
        in_specs=[
            pl.BlockSpec(memory_space=pltpu.SMEM),
            rows,
            whole(16, D),
            rows,
            pl.BlockSpec((192, FF), lambda i: (i, 0)),
            pl.BlockSpec((D, 384), lambda i: (0, i)),
            whole(8, D),
            whole(8, 192),
        ],
        out_specs=[
            rows,
            rows,
            pl.BlockSpec((192, FF), lambda i: (i, 0)),
            pl.BlockSpec((384, D), lambda i: (i, 0)),
            whole(1, D),
            whole(1, D),
            whole(8, 192),
        ],
        out_shape=[
            out((512, D), bf16),
            out((512, D), f32),
            out((D, FF), f32),
            out((1536, D), f32),
            out((1, D), f32),
            out((1, D), f32),
            out((8, 192), f32),
        ],
        compiler_params=pltpu.CompilerParams(vmem_limit_bytes=60 * 2**20),
        name="finish",
    )(counts, a1, a3, gt, gw, gv, gg, gpos)


def shards(tokens, seg_counts, w_in, w_down, ln_gain, ln_bias, pos_table, cotangent):
    a1, a3, gt, gw, gv, gg, gpos, _ = fused(
        seg_counts,
        tokens.reshape(512, D),
        cotangent.reshape(512, D),
        w_in[0],
        w_down,
        ln_gain,
        ln_bias,
        pos_table,
    )
    size = lax.axis_size("dp")
    if size > 8:
        rings = [[i + 8 * k for k in range(size // 8)] for i in range(8)]
        gw, gv, gg, gpos = lax.psum((gw, gv, gg, gpos), "dp", axis_index_groups=rings)
    made = finish(seg_counts, a1, a3, gt, gw, gv, gg, gpos)
    mixed, gtok, gw, gv, gain, bias, gpos = made
    return (
        mixed.reshape(2, 256, D),
        gtok.reshape(2, 256, D),
        gw[None],
        gv,
        gain,
        bias,
        gpos,
    )


def solution(mesh):
    return jax.shard_map(
        shards,
        mesh=mesh,
        in_specs=(
            P("dp", "section", None),
            P("dp", None),
            P("section", None, None),
            P("section", None),
            P("section", None),
            P("section", None),
            P(None, "section"),
            P("dp", "section", None),
        ),
        out_specs=(
            P("dp", "section", None),
            P("dp", "section", None),
            P("section", None, None),
            P("section", None),
            P("section", None),
            P("section", None),
            P(None, "section"),
        ),
        check_vma=False,
    )
```
